32 devices in a mesh: dp: 4 (over z), seq: 8 (over y, x, core).
Axes of the slice: x: 2, y: 2, z: 4, core: 2. Of those that a mesh axis runs over, the one named last changes fastest.
Arguments:
- source_tokens: bfloat16 [2048, 8, 1024], P('seq', 'dp'), may hold values from -6 to 6
- target_tokens: bfloat16 [128, 8, 1024], P('seq', 'dp'), may hold values from -6 to 6
- source_lengths: int32 [8], P('dp'), may hold values from 512 to 2048, as said below
- target_lengths: int32 [8], P('dp'), may hold values from 32 to 128, as said below
- encoder_query: bfloat16 [1024, 1024], replicated, may hold values from -0.25 to 0.25
- encoder_key: bfloat16 [1024, 1024], replicated, may hold values from -0.1875 to 0.1875
- encoder_value: bfloat16 [1024, 1024], replicated, may hold values from -0.1875 to 0.1875
- encoder_mix: bfloat16 [1024, 1024], replicated, may hold values from -3 to 3
- attend_gain: float32 [1024], replicated, may hold values from 0.5 to 1.5
- attend_shift: float32 [1024], replicated, may hold values from -1.75 to 1.75
- encoder_expand: bfloat16 [1024, 4096], P(None, 'seq'), may hold values from -0.1875 to 0.1875
- encoder_contract: bfloat16 [4096, 1024], P('seq'), may hold values from -0.09375 to 0.09375
- encoder_gain: float32 [1024], replicated, may hold values from 0.5 to 1.5
- encoder_shift: float32 [1024], replicated, may hold values from -1.75 to 1.75
- decoder_query: bfloat16 [1024, 1024], replicated, may hold values from -0.25 to 0.25
- decoder_key: bfloat16 [1024, 1024], replicated, may hold values from -0.1875 to 0.1875
- decoder_value: bfloat16 [1024, 1024], replicated, may hold values from -0.1875 to 0.1875
- decoder_mix: bfloat16 [1024, 1024], replicated, may hold values from -0.5 to 0.5
- self_gain: float32 [1024], replicated, may hold values from 0.5 to 1.5
- self_shift: float32 [1024], replicated, may hold values from -1.75 to 1.75
- cross_query: bfloat16 [1024, 1024], replicated, may hold values from -0.25 to 0.25
- cross_key: bfloat16 [1024, 1024], replicated, may hold values from -0.1875 to 0.1875
- cross_value: bfloat16 [1024, 1024], replicated, may hold values from -0.1875 to 0.1875
- cross_mix: bfloat16 [1024, 1024], replicated, may hold values from -3 to 3
- cross_gain: float32 [1024], replicated, may hold values from 0.5 to 1.5
- cross_shift: float32 [1024], replicated, may hold values from -1.75 to 1.75
- decoder_expand: bfloat16 [1024, 4096], P(None, 'seq'), may hold values from -0.1875 to 0.1875
- decoder_contract: bfloat16 [4096, 1024], P('seq'), may hold values from -0.09375 to 0.09375
- decoder_gain: float32 [1024], replicated, may hold values from 0.5 to 1.5
- decoder_shift: float32 [1024], replicated, may hold values from -1.75 to 1.75
- source_cotangent: bfloat16 [2048, 8, 1024], P('seq', 'dp'), may hold values from -6 to 6
- target_cotangent: bfloat16 [128, 8, 1024], P('seq', 'dp'), may hold values from -6 to 6
Outputs:
- encoded: bfloat16 [2048, 8, 1024], P('seq', 'dp')
- decoded: bfloat16 [128, 8, 1024], P('seq', 'dp')
- grad_source: float32 [2048, 8, 1024], P('seq', 'dp')
- grad_target: float32 [128, 8, 1024], P('seq', 'dp')
- grad_encoder_query: float32 [1024, 1024], P('seq')
- grad_encoder_key: float32 [1024, 1024], P('seq')
- grad_encoder_value: float32 [1024, 1024], P('seq')
- grad_encoder_mix: float32 [1024, 1024], P('seq')
- grad_attend_gain: float32 [1024], P('seq')
- grad_attend_shift: float32 [1024], P('seq')
- grad_encoder_expand: float32 [1024, 4096], P(None, 'seq')
- grad_encoder_contract: float32 [4096, 1024], P('seq')
- grad_encoder_gain: float32 [1024], P('seq')
- grad_encoder_shift: float32 [1024], P('seq')
- grad_decoder_query: float32 [1024, 1024], P('seq')
- grad_decoder_key: float32 [1024, 1024], P('seq')
- grad_decoder_value: float32 [1024, 1024], P('seq')
- grad_decoder_mix: float32 [1024, 1024], P('seq')
- grad_self_gain: float32 [1024], P('seq')
- grad_self_shift: float32 [1024], P('seq')
- grad_cross_query: float32 [1024, 1024], P('seq')
- grad_cross_key: float32 [1024, 1024], P('seq')
- grad_cross_value: float32 [1024, 1024], P('seq')
- grad_cross_mix: float32 [1024, 1024], P('seq')
- grad_cross_gain: float32 [1024], P('seq')
- grad_cross_shift: float32 [1024], P('seq')
- grad_decoder_expand: float32 [1024, 4096], P(None, 'seq')
- grad_decoder_contract: float32 [4096, 1024], P('seq')
- grad_decoder_gain: float32 [1024], P('seq')
- grad_decoder_shift: float32 [1024], P('seq')
The draws below stay inside these ranges and needn't reach their ends.
Inputs may be any that keep to these rules, and one draw needn't show every extreme that they name: `source_lengths`: in each aligned group of 2 tables (one index of dp) one table, drawn from the seed, has exactly 2048 used slots. `target_lengths`: in each aligned group of 2 tables one table, drawn from the seed, has exactly 128 used slots.
All inputs are finite; a program needn't handle non-finite values.
Results may differ from the reference program's by a relative error of at most 0.034.
Values may be sent and summed in bfloat16 or wider, within the bound.
A program may use at most 320 MiB of HBM per device.

```python
import math
import jax
import jax.numpy as jnp
from jax import lax

D = 1024
HEADS = 16
FF = 4096
SEQS = 2
L_ENC = 2048
DEC_LEN = 128
TABLES = 8


def spread_lengths(key, longest):
    groups = TABLES // SEQS
    first_key, second_key = jax.random.split(key)
    drawn = jax.random.randint(first_key, (groups, SEQS), longest // 4, longest + 1)
    chosen = jax.random.randint(second_key, (groups, 1), 0, SEQS)
    whole = jnp.arange(SEQS)[None, :] == chosen
    return jnp.where(whole, longest, drawn).reshape(TABLES).astype(jnp.int32)


def draw_source_lengths(key, part):
    key = jax.random.fold_in(key, 11)
    return spread_lengths(key, L_ENC)


def draw_target_lengths(key, part):
    key = jax.random.fold_in(key, 23)
    return spread_lengths(key, DEC_LEN)


def steps_of(rng, shape, shards, smallest, largest):
    def one(dim, parts):
        heights = jax.random.uniform(jax.random.fold_in(jax.random.fold_in(rng, 6), dim), (parts,), jnp.float32, smallest / len(shards), largest / len(shards))
        return jnp.repeat(jnp.exp(heights), shape[dim] // parts).reshape((-1,) + (1,) * (len(shape) - dim - 1))

    level = one(*shards[0])
    for cut in shards[1:]:
        level = level * one(*cut)
    return level


def bell_draw(stream_key, extent, deviation, limit, pieces=(), held_as=jnp.bfloat16):
    values = deviation * jax.random.normal(stream_key, extent, jnp.float32)
    if pieces:
        values = values * steps_of(stream_key, extent, pieces, -0.22, 0.18)
    return jnp.clip(values, -limit, limit).astype(held_as)


def setup_inputs(seed: int = 0) -> dict:
    key_list = jax.random.split(jax.random.key(seed), 33)
    source_tokens = bell_draw(key_list[0], (L_ENC, TABLES, D), 1.0, 6.0, ((0, 8), (1, 4)))
    target_tokens = bell_draw(key_list[1], (DEC_LEN, TABLES, D), 1.0, 6.0, ((0, 8), (1, 4)))
    source_lengths = draw_source_lengths(jax.random.fold_in(key_list[32], 71), 0)
    target_lengths = draw_target_lengths(jax.random.fold_in(key_list[32], 71), 0)
    encoder_query = bell_draw(key_list[4], (D, D), (D // 2) ** -0.5, 0.25)
    encoder_key = bell_draw(key_list[5], (D, D), D ** -0.5, 0.1875)
    encoder_value = bell_draw(key_list[6], (D, D), D ** -0.5, 0.1875)
    encoder_mix = bell_draw(key_list[7], (D, D), 4 ** -0.5, 3.0)
    attend_gain = jnp.clip(1.0 + 0.1 * jax.random.normal(key_list[8], (D,), jnp.float32), 0.5, 1.5)
    attend_shift = bell_draw(key_list[9], (D,), 0.3, 1.75, (), jnp.float32)
    encoder_expand = bell_draw(key_list[10], (D, FF), D ** -0.5, 0.1875, ((1, 8),))
    encoder_contract = bell_draw(key_list[11], (FF, D), FF ** -0.5, 0.09375, ((0, 8),))
    encoder_gain = jnp.clip(1.0 + 0.1 * jax.random.normal(key_list[12], (D,), jnp.float32), 0.5, 1.5)
    encoder_shift = bell_draw(key_list[13], (D,), 0.3, 1.75, (), jnp.float32)
    decoder_query = bell_draw(key_list[14], (D, D), (D // 2) ** -0.5, 0.25)
    decoder_key = bell_draw(key_list[15], (D, D), D ** -0.5, 0.1875)
    decoder_value = bell_draw(key_list[16], (D, D), D ** -0.5, 0.1875)
    decoder_mix = bell_draw(key_list[17], (D, D), (D // 8) ** -0.5, 0.5)
    self_gain = jnp.clip(1.0 + 0.1 * jax.random.normal(key_list[18], (D,), jnp.float32), 0.5, 1.5)
    self_shift = bell_draw(key_list[19], (D,), 0.3, 1.75, (), jnp.float32)
    cross_query = bell_draw(key_list[20], (D, D), (D // 2) ** -0.5, 0.25)
    cross_key = bell_draw(key_list[21], (D, D), D ** -0.5, 0.1875)
    cross_value = bell_draw(key_list[22], (D, D), D ** -0.5, 0.1875)
    cross_mix = bell_draw(key_list[23], (D, D), 4 ** -0.5, 3.0)
    cross_gain = jnp.clip(1.0 + 0.1 * jax.random.normal(key_list[24], (D,), jnp.float32), 0.5, 1.5)
    cross_shift = bell_draw(key_list[25], (D,), 0.3, 1.75, (), jnp.float32)
    decoder_expand = bell_draw(key_list[26], (D, FF), D ** -0.5, 0.1875, ((1, 8),))
    decoder_contract = bell_draw(key_list[27], (FF, D), FF ** -0.5, 0.09375, ((0, 8),))
    decoder_gain = jnp.clip(1.0 + 0.1 * jax.random.normal(key_list[28], (D,), jnp.float32), 0.5, 1.5)
    decoder_shift = bell_draw(key_list[29], (D,), 0.3, 1.75, (), jnp.float32)
    source_cotangent = bell_draw(key_list[30], (L_ENC, TABLES, D), 1.0, 6.0, ((0, 8), (1, 4)))
    target_cotangent = bell_draw(key_list[31], (DEC_LEN, TABLES, D), 1.0, 6.0, ((0, 8), (1, 4)))
    return dict(source_tokens=source_tokens, target_tokens=target_tokens, source_lengths=source_lengths, target_lengths=target_lengths, encoder_query=encoder_query, encoder_key=encoder_key, encoder_value=encoder_value, encoder_mix=encoder_mix, attend_gain=attend_gain, attend_shift=attend_shift, encoder_expand=encoder_expand, encoder_contract=encoder_contract, encoder_gain=encoder_gain, encoder_shift=encoder_shift, decoder_query=decoder_query, decoder_key=decoder_key, decoder_value=decoder_value, decoder_mix=decoder_mix, self_gain=self_gain, self_shift=self_shift, cross_query=cross_query, cross_key=cross_key, cross_value=cross_value, cross_mix=cross_mix, cross_gain=cross_gain, cross_shift=cross_shift, decoder_expand=decoder_expand, decoder_contract=decoder_contract, decoder_gain=decoder_gain, decoder_shift=decoder_shift, source_cotangent=source_cotangent, target_cotangent=target_cotangent)


@jax.custom_vjp
def low(v):
    return lax.optimization_barrier(v.astype(jnp.bfloat16)).astype(jnp.float32)

@jax.custom_vjp
def low_back(v):
    return v

def low_keep(v):
    return (low(v), None)

def low_pass(kept, grad):
    return (grad,)

def back_keep(v):
    return (v, None)

def back_low(kept, grad):
    return (low(grad),)
low.defvjp(low_keep, low_pass)
low_back.defvjp(back_keep, back_low)
highest = lax.Precision.HIGHEST
masked_fill = -1e+30
norm_epsilon = 1e-05

def round_both(values):
    return low_back(low(values))

def matmul(left, right):
    return jnp.dot(left, right, precision=highest)

def layer_norm(rows, gain, shift):
    centre = lax.optimization_barrier(jnp.mean(rows, -1, keepdims=True))
    centred = rows - centre
    spread = lax.optimization_barrier(jnp.mean(centred * centred, -1, keepdims=True))
    return centred * lax.rsqrt(spread + norm_epsilon) * gain + shift

def attention(from_rows, to_rows, w_query, w_key, w_value, w_mix, length, causal):
    width = from_rows.shape[-1]
    size = width // HEADS
    scale = size ** (-0.5)
    queries = round_both(matmul(from_rows, w_query)).reshape(-1, HEADS, size)
    keys = round_both(matmul(to_rows, w_key)).reshape(-1, HEADS, size)
    values = round_both(matmul(to_rows, w_value)).reshape(-1, HEADS, size)
    qlen = queries.shape[0]
    klen = keys.shape[0]
    block = math.gcd(qlen, 512)
    key_rows = jnp.arange(klen)

    def one_block(inputs):
        rows, first_row = inputs
        scores = low_back(jnp.einsum('qhd,khd->hqk', rows, keys, precision=highest) * scale)
        query_rows = first_row + jnp.arange(block)
        allowed = key_rows[None, :] < length
        if causal:
            allowed = allowed & (key_rows[None, :] <= query_rows[:, None])
        scores = jnp.where(allowed[None], scores, masked_fill)
        top = lax.optimization_barrier(jnp.max(scores, -1, keepdims=True))
        weights = jnp.exp(scores - top)
        probs = low(weights / lax.optimization_barrier(jnp.sum(weights, -1, keepdims=True)))
        return jnp.einsum('hqk,khd->qhd', probs, values, precision=highest)
    blocks = queries.reshape(qlen // block, block, HEADS, size)
    starts = jnp.arange(qlen // block) * block
    context = lax.map(jax.checkpoint(one_block), (blocks, starts))
    context = round_both(context.reshape(qlen, width))
    return low_back(matmul(context, w_mix))

def feed(rows, w_expand, w_contract):
    hidden = low_back(matmul(low(rows), w_expand))
    acts = low(jax.nn.gelu(hidden, approximate=False))
    return low_back(matmul(acts, w_contract))

def table_forward(weights, source, target, source_length, target_length):
    encoder_query, encoder_key, encoder_value, encoder_mix, attend_gain, attend_shift, encoder_expand, encoder_contract, encoder_gain, encoder_shift, decoder_query, decoder_key, decoder_value, decoder_mix, self_gain, self_shift, cross_query, cross_key, cross_value, cross_mix, cross_gain, cross_shift, decoder_expand, decoder_contract, decoder_gain, decoder_shift = weights
    attended = attention(source, source, encoder_query, encoder_key, encoder_value, encoder_mix, source_length, False)
    first = layer_norm(source + attended, attend_gain, attend_shift)
    second = layer_norm(first + feed(first, encoder_expand, encoder_contract), encoder_gain, encoder_shift)
    encoded = low(second)
    selfed = attention(target, target, decoder_query, decoder_key, decoder_value, decoder_mix, target_length, True)
    third = layer_norm(target + selfed, self_gain, self_shift)
    crossed = attention(low(third), encoded, cross_query, cross_key, cross_value, cross_mix, source_length, False)
    fourth = layer_norm(third + crossed, cross_gain, cross_shift)
    fifth = layer_norm(fourth + feed(fourth, decoder_expand, decoder_contract), decoder_gain, decoder_shift)
    return (encoded, low(fifth))

def reference(source_tokens, target_tokens, source_lengths, target_lengths, encoder_query, encoder_key, encoder_value, encoder_mix, attend_gain, attend_shift, encoder_expand, encoder_contract, encoder_gain, encoder_shift, decoder_query, decoder_key, decoder_value, decoder_mix, self_gain, self_shift, cross_query, cross_key, cross_value, cross_mix, cross_gain, cross_shift, decoder_expand, decoder_contract, decoder_gain, decoder_shift, source_cotangent, target_cotangent):
    params = tuple((weight.astype(jnp.float32) for weight in (encoder_query, encoder_key, encoder_value, encoder_mix, attend_gain, attend_shift, encoder_expand, encoder_contract, encoder_gain, encoder_shift, decoder_query, decoder_key, decoder_value, decoder_mix, self_gain, self_shift, cross_query, cross_key, cross_value, cross_mix, cross_gain, cross_shift, decoder_expand, decoder_contract, decoder_gain, decoder_shift)))

    def per_table(totals, inputs):
        source, target, source_length, target_length, source_grad, target_grad = inputs

        def forward(weights, source_rows, target_rows):
            return table_forward(weights, source_rows, target_rows, source_length, target_length)
        outputs, pullback = jax.vjp(forward, params, source, target)
        grads, d_source, d_target = pullback((source_grad, target_grad))
        totals = jax.tree.map(jnp.add, totals, grads)
        return (totals, (outputs[0].astype(jnp.bfloat16), outputs[1].astype(jnp.bfloat16), d_source, d_target))
    inputs = (jnp.moveaxis(source_tokens.astype(jnp.float32), 1, 0), jnp.moveaxis(target_tokens.astype(jnp.float32), 1, 0), source_lengths, target_lengths, jnp.moveaxis(source_cotangent.astype(jnp.float32), 1, 0), jnp.moveaxis(target_cotangent.astype(jnp.float32), 1, 0))
    zeros = tuple((jnp.zeros_like(weight) for weight in params))
    totals, stacked = lax.scan(per_table, zeros, inputs)
    encoded = jnp.moveaxis(stacked[0], 0, 1)
    decoded = jnp.moveaxis(stacked[1], 0, 1)
    grad_source = jnp.moveaxis(stacked[2], 0, 1)
    grad_target = jnp.moveaxis(stacked[3], 0, 1)
    return (encoded, decoded, grad_source, grad_target, totals[0], totals[1], totals[2], totals[3], totals[4], totals[5], totals[6], totals[7], totals[8], totals[9], totals[10], totals[11], totals[12], totals[13], totals[14], totals[15], totals[16], totals[17], totals[18], totals[19], totals[20], totals[21], totals[22], totals[23], totals[24], totals[25])
```

```python
import functools

import jax
import jax.numpy as jnp
from jax import lax
from jax.experimental import pallas as pl
from jax.experimental.pallas import tpu as pltpu
from jax.sharding import PartitionSpec as P

HEADS = 16


masked_fill = -1e30
norm_epsilon = 1e-05


def layer_norm(rows, gain, shift):
    centre = jnp.mean(rows, -1, keepdims=True)
    centred = rows - centre
    spread = jnp.mean(centred * centred, -1, keepdims=True)
    return centred * lax.rsqrt(spread + norm_epsilon) * gain + shift


def gelu_exact(values):
    return jax.nn.gelu(values, approximate=False)


def project(rows, weight):
    return jnp.dot(rows, weight, preferred_element_type=jnp.float32)


def project_back(grads, weight):
    return jnp.einsum("re,de->rd", grads, weight, preferred_element_type=jnp.float32)


def outer_sum(rows, grads):
    return jnp.einsum("rd,re->de", rows, grads, preferred_element_type=jnp.float32)


def by_heads(array):
    return array.reshape(array.shape[0], HEADS, -1)


def head_scale(width):
    return (width // HEADS) ** (-0.5)


def score_block(queries, keys):
    scores = jnp.einsum(
        "qhd,khd->hqk", by_heads(queries), by_heads(keys), preferred_element_type=jnp.float32
    )
    return scores * head_scale(queries.shape[-1])


def allowed_keys(query_rows, key_rows, length, causal):
    allowed = key_rows[None, :] < length
    if causal:
        allowed = allowed & (key_rows[None, :] <= query_rows[:, None])
    return allowed


def table_of(array, table):
    return lax.dynamic_index_in_dim(array, table, 1, keepdims=False)


def gather_pair(keys, values):
    return (
        lax.all_gather(keys, "seq", axis=0, tiled=True),
        lax.all_gather(values, "seq", axis=0, tiled=True),
    )


def gather_rows(rows):
    return lax.all_gather(rows, "seq", axis=0, tiled=True)


def sum_rows(terms, count):
    return lax.psum_scatter(
        terms(jnp.int32(0), count * lax.axis_size("seq")).astype(jnp.bfloat16),
        "seq",
        scatter_dimension=0,
        tiled=True,
    ).astype(jnp.float32)


def projections(from_rows, to_rows, w_query, w_key, w_value):
    qlen, tables, width = from_rows.shape
    klen = to_rows.shape[0]
    to_flat = to_rows.reshape(-1, width)
    queries = (
        project(from_rows.reshape(-1, width), w_query)
        .astype(jnp.bfloat16)
        .reshape(qlen, tables, width)
    )
    keys = project(to_flat, w_key).astype(jnp.bfloat16).reshape(klen, tables, width)
    values = project(to_flat, w_value).astype(jnp.bfloat16).reshape(klen, tables, width)
    return (queries, keys, values)


def finish_grads(from_rows, to_rows, w_query, w_key, w_value, d_queries, d_keys, d_values):
    width = from_rows.shape[-1]
    from_flat = from_rows.reshape(-1, width)
    to_flat = to_rows.reshape(-1, width)
    query_low = d_queries.astype(jnp.bfloat16).reshape(-1, width)
    key_low = d_keys.astype(jnp.bfloat16).reshape(-1, width)
    value_low = d_values.astype(jnp.bfloat16).reshape(-1, width)
    grad_query = outer_sum(from_flat, query_low)
    grad_key = outer_sum(to_flat, key_low)
    grad_value = outer_sum(to_flat, value_low)
    d_from = project_back(query_low, w_query)
    d_to = project_back(key_low, w_key) + project_back(value_low, w_value)
    return (d_from, d_to, grad_query, grad_key, grad_value)


def attend_forward(from_rows, to_rows, w_query, w_key, w_value, lengths, causal):
    qlen, tables, width = from_rows.shape
    queries, keys, values = projections(from_rows, to_rows, w_query, w_key, w_value)
    gathered = gather_pair(keys, values)
    all_keys, all_values = gathered
    query_rows = lax.axis_index("seq") * qlen + jnp.arange(qlen)
    key_rows = jnp.arange(all_keys.shape[0])

    def one_table(table):
        scores = score_block(table_of(queries, table), table_of(all_keys, table))
        allowed = allowed_keys(query_rows, key_rows, lengths[table], causal)
        scores = jnp.where(allowed[None], scores, masked_fill)
        top = jnp.max(scores, -1)
        weights = jnp.exp(scores - top[..., None])
        total = jnp.sum(weights, -1)
        probs = (weights / total[..., None]).astype(jnp.bfloat16)
        context = jnp.einsum(
            "hqk,khd->qhd",
            probs,
            by_heads(table_of(all_values, table)),
            preferred_element_type=jnp.float32,
        )
        return (context.reshape(qlen, width), top + jnp.log(total))

    context, logsum = lax.map(one_table, jnp.arange(tables))
    return (queries, keys, values, gathered, jnp.swapaxes(context, 0, 1), logsum)


def key_value_terms(
    query_part,
    grads_part,
    logsum_part,
    delta_part,
    key_part,
    value_part,
    query_rows,
    part_rows,
    length,
    causal,
    scale,
):
    scores = score_block(query_part, key_part)
    allowed = allowed_keys(query_rows, part_rows, length, causal)
    probs = jnp.where(allowed[None], jnp.exp(scores - logsum_part[..., None]), 0.0)
    grads_here = by_heads(grads_part)
    d_values = jnp.einsum(
        "hqk,qhd->khd", probs.astype(jnp.bfloat16), grads_here, preferred_element_type=jnp.float32
    )
    d_probs = jnp.einsum(
        "qhd,khd->hqk", grads_here, by_heads(value_part), preferred_element_type=jnp.float32
    )
    d_scores = (probs * (d_probs - delta_part.T[..., None])).astype(jnp.bfloat16)
    d_keys = (
        jnp.einsum(
            "hqk,qhd->khd", d_scores, by_heads(query_part), preferred_element_type=jnp.float32
        )
        * scale
    )
    count = key_part.shape[0]
    width = key_part.shape[-1]
    return jnp.concatenate([d_keys.reshape(count, width), d_values.reshape(count, width)], -1)


def attend_backward(state, from_rows, to_rows, w_query, w_key, w_value, lengths, causal, d_context):
    queries, keys, values, gathered, context, logsum = state
    qlen, tables, width = queries.shape
    klen = keys.shape[0]
    all_keys, all_values = gather_pair(keys, values)
    scale = head_scale(width)
    d_low = d_context.reshape(qlen, tables, width).astype(jnp.bfloat16)
    delta = jnp.sum((d_low.astype(jnp.float32) * context).reshape(qlen, tables, HEADS, -1), -1)
    query_rows = lax.axis_index("seq") * qlen + jnp.arange(qlen)
    key_rows = jnp.arange(all_keys.shape[0])

    def query_table(table):
        scores = score_block(table_of(queries, table), table_of(all_keys, table))
        allowed = allowed_keys(query_rows, key_rows, lengths[table], causal)
        probs = jnp.where(allowed[None], jnp.exp(scores - logsum[table][..., None]), 0.0)
        d_probs = jnp.einsum(
            "qhd,khd->hqk",
            by_heads(table_of(d_low, table)),
            by_heads(table_of(all_values, table)),
            preferred_element_type=jnp.float32,
        )
        d_scores = (probs * (d_probs - delta[:, table].T[..., None])).astype(jnp.bfloat16)
        d_query = jnp.einsum(
            "hqk,khd->qhd",
            d_scores,
            by_heads(table_of(all_keys, table)),
            preferred_element_type=jnp.float32,
        )
        return (d_query * scale).reshape(qlen, width)

    d_queries = jnp.swapaxes(lax.map(query_table, jnp.arange(tables)), 0, 1)
    part_rows = jnp.arange(klen * lax.axis_size("seq"))

    def key_table(table, terms):
        piece = key_value_terms(
            table_of(queries, table),
            table_of(d_low, table),
            logsum[table],
            delta[:, table],
            table_of(all_keys, table),
            table_of(all_values, table),
            query_rows,
            part_rows,
            lengths[table],
            causal,
            scale,
        )
        return lax.dynamic_update_index_in_dim(terms, piece, table, 1)

    summed = lax.psum_scatter(
        lax.fori_loop(
            0,
            tables,
            key_table,
            jnp.zeros((klen * lax.axis_size("seq"), tables, 2 * width), jnp.float32),
        ).astype(jnp.bfloat16),
        "seq",
        scatter_dimension=0,
        tiled=True,
    ).astype(jnp.float32)
    return finish_grads(
        from_rows,
        to_rows,
        w_query,
        w_key,
        w_value,
        d_queries,
        summed[..., :width],
        summed[..., width:],
    )


def token_forward(rows, w_expand, w_contract):
    all_rows = gather_rows(rows)
    acts = gelu_exact(project(all_rows, w_expand)).astype(jnp.bfloat16)

    def contract_terms(start, count):
        return project(acts, w_contract)

    return (sum_rows(contract_terms, rows.shape[0]), all_rows)


def token_backward(all_rows, d_out, w_expand, w_contract):
    all_grads = gather_rows(d_out.astype(jnp.bfloat16))
    acts, gelu_back = jax.vjp(gelu_exact, project(all_rows, w_expand))
    d_hidden = gelu_back(project_back(all_grads, w_contract))[0].astype(jnp.bfloat16)
    grad_expand = outer_sum(all_rows, d_hidden)
    grad_contract = outer_sum(acts.astype(jnp.bfloat16), all_grads)

    def expand_terms(start, count):
        return project_back(d_hidden, w_expand)

    return (sum_rows(expand_terms, d_out.shape[0]), grad_expand, grad_contract)


def general_body(
    source_tokens,
    target_tokens,
    source_lengths,
    target_lengths,
    encoder_query,
    encoder_key,
    encoder_value,
    encoder_mix,
    attend_gain,
    attend_shift,
    encoder_expand,
    encoder_contract,
    encoder_gain,
    encoder_shift,
    decoder_query,
    decoder_key,
    decoder_value,
    decoder_mix,
    self_gain,
    self_shift,
    cross_query,
    cross_key,
    cross_value,
    cross_mix,
    cross_gain,
    cross_shift,
    decoder_expand,
    decoder_contract,
    decoder_gain,
    decoder_shift,
    source_cotangent,
    target_cotangent,
):
    slots, tables, width = source_tokens.shape
    places = target_tokens.shape[0]
    source_flat = source_tokens.reshape(-1, width)
    target_flat = target_tokens.reshape(-1, width)
    encoder_state = attend_forward(
        source_tokens,
        source_tokens,
        encoder_query,
        encoder_key,
        encoder_value,
        source_lengths,
        False,
    )
    encoder_context = encoder_state[4].reshape(-1, width).astype(jnp.bfloat16)
    first, first_back = jax.vjp(
        layer_norm,
        source_flat.astype(jnp.float32) + project(encoder_context, encoder_mix),
        attend_gain,
        attend_shift,
    )
    first_low = first.astype(jnp.bfloat16)
    widened, encoder_kept = token_forward(first_low, encoder_expand, encoder_contract)
    second, second_back = jax.vjp(layer_norm, first + widened, encoder_gain, encoder_shift)
    encoded = second.astype(jnp.bfloat16).reshape(slots, tables, width)
    decoder_state = attend_forward(
        target_tokens,
        target_tokens,
        decoder_query,
        decoder_key,
        decoder_value,
        target_lengths,
        True,
    )
    decoder_context = decoder_state[4].reshape(-1, width).astype(jnp.bfloat16)
    third, third_back = jax.vjp(
        layer_norm,
        target_flat.astype(jnp.float32) + project(decoder_context, decoder_mix),
        self_gain,
        self_shift,
    )
    third_blocks = third.astype(jnp.bfloat16).reshape(places, tables, width)
    cross_state = attend_forward(
        third_blocks, encoded, cross_query, cross_key, cross_value, source_lengths, False
    )
    cross_context = cross_state[4].reshape(-1, width).astype(jnp.bfloat16)
    fourth, fourth_back = jax.vjp(
        layer_norm, third + project(cross_context, cross_mix), cross_gain, cross_shift
    )
    fourth_low = fourth.astype(jnp.bfloat16)
    narrowed, decoder_kept = token_forward(fourth_low, decoder_expand, decoder_contract)
    fifth, fifth_back = jax.vjp(layer_norm, fourth + narrowed, decoder_gain, decoder_shift)
    decoded = fifth.astype(jnp.bfloat16).reshape(places, tables, width)
    d_fifth, grad_decoder_gain, grad_decoder_shift = fifth_back(
        target_cotangent.reshape(-1, width).astype(jnp.float32)
    )
    d_rows, grad_decoder_expand, grad_decoder_contract = token_backward(
        decoder_kept, d_fifth, decoder_expand, decoder_contract
    )
    d_fourth, grad_cross_gain, grad_cross_shift = fourth_back(d_fifth + d_rows)
    cross_low = d_fourth.astype(jnp.bfloat16)
    grad_cross_mix = outer_sum(cross_context, cross_low)
    d_cross_context = project_back(cross_low, cross_mix)
    d_third_cross, d_encoded, grad_cross_query, grad_cross_key, grad_cross_value = attend_backward(
        cross_state,
        third_blocks,
        encoded,
        cross_query,
        cross_key,
        cross_value,
        source_lengths,
        False,
        d_cross_context,
    )
    d_third, grad_self_gain, grad_self_shift = third_back(d_fourth + d_third_cross)
    self_low = d_third.astype(jnp.bfloat16)
    grad_decoder_mix = outer_sum(decoder_context, self_low)
    d_from, d_to, grad_decoder_query, grad_decoder_key, grad_decoder_value = attend_backward(
        decoder_state,
        target_tokens,
        target_tokens,
        decoder_query,
        decoder_key,
        decoder_value,
        target_lengths,
        True,
        project_back(self_low, decoder_mix),
    )
    grad_target = (d_third + d_from + d_to).reshape(places, tables, width)
    d_second, grad_encoder_gain, grad_encoder_shift = second_back(
        source_cotangent.reshape(-1, width).astype(jnp.float32) + d_encoded
    )
    d_rows, grad_encoder_expand, grad_encoder_contract = token_backward(
        encoder_kept, d_second, encoder_expand, encoder_contract
    )
    d_first, grad_attend_gain, grad_attend_shift = first_back(d_second + d_rows)
    encoder_low = d_first.astype(jnp.bfloat16)
    grad_encoder_mix = outer_sum(encoder_context, encoder_low)
    d_from, d_to, grad_encoder_query, grad_encoder_key, grad_encoder_value = attend_backward(
        encoder_state,
        source_tokens,
        source_tokens,
        encoder_query,
        encoder_key,
        encoder_value,
        source_lengths,
        False,
        project_back(encoder_low, encoder_mix),
    )
    grad_source = (d_first + d_from + d_to).reshape(slots, tables, width)
    shards = (
        lax.psum_scatter(
            grad_encoder_query.astype(jnp.bfloat16), "seq", scatter_dimension=0, tiled=True
        ).astype(jnp.float32),
        lax.psum_scatter(
            grad_encoder_key.astype(jnp.bfloat16), "seq", scatter_dimension=0, tiled=True
        ).astype(jnp.float32),
        lax.psum_scatter(
            grad_encoder_value.astype(jnp.bfloat16), "seq", scatter_dimension=0, tiled=True
        ).astype(jnp.float32),
        lax.psum_scatter(
            grad_encoder_mix.astype(jnp.bfloat16), "seq", scatter_dimension=0, tiled=True
        ).astype(jnp.float32),
        lax.psum_scatter(
            grad_decoder_query.astype(jnp.bfloat16), "seq", scatter_dimension=0, tiled=True
        ).astype(jnp.float32),
        lax.psum_scatter(
            grad_decoder_key.astype(jnp.bfloat16), "seq", scatter_dimension=0, tiled=True
        ).astype(jnp.float32),
        lax.psum_scatter(
            grad_decoder_value.astype(jnp.bfloat16), "seq", scatter_dimension=0, tiled=True
        ).astype(jnp.float32),
        lax.psum_scatter(
            grad_decoder_mix.astype(jnp.bfloat16), "seq", scatter_dimension=0, tiled=True
        ).astype(jnp.float32),
        lax.psum_scatter(
            grad_cross_query.astype(jnp.bfloat16), "seq", scatter_dimension=0, tiled=True
        ).astype(jnp.float32),
        lax.psum_scatter(
            grad_cross_key.astype(jnp.bfloat16), "seq", scatter_dimension=0, tiled=True
        ).astype(jnp.float32),
        lax.psum_scatter(
            grad_cross_value.astype(jnp.bfloat16), "seq", scatter_dimension=0, tiled=True
        ).astype(jnp.float32),
        lax.psum_scatter(
            grad_cross_mix.astype(jnp.bfloat16), "seq", scatter_dimension=0, tiled=True
        ).astype(jnp.float32),
        lax.psum_scatter(
            grad_attend_gain.astype(jnp.bfloat16), "seq", scatter_dimension=0, tiled=True
        ).astype(jnp.float32),
        lax.psum_scatter(
            grad_attend_shift.astype(jnp.bfloat16), "seq", scatter_dimension=0, tiled=True
        ).astype(jnp.float32),
        lax.psum_scatter(
            grad_encoder_gain.astype(jnp.bfloat16), "seq", scatter_dimension=0, tiled=True
        ).astype(jnp.float32),
        lax.psum_scatter(
            grad_encoder_shift.astype(jnp.bfloat16), "seq", scatter_dimension=0, tiled=True
        ).astype(jnp.float32),
        lax.psum_scatter(
            grad_self_gain.astype(jnp.bfloat16), "seq", scatter_dimension=0, tiled=True
        ).astype(jnp.float32),
        lax.psum_scatter(
            grad_self_shift.astype(jnp.bfloat16), "seq", scatter_dimension=0, tiled=True
        ).astype(jnp.float32),
        lax.psum_scatter(
            grad_cross_gain.astype(jnp.bfloat16), "seq", scatter_dimension=0, tiled=True
        ).astype(jnp.float32),
        lax.psum_scatter(
            grad_cross_shift.astype(jnp.bfloat16), "seq", scatter_dimension=0, tiled=True
        ).astype(jnp.float32),
        lax.psum_scatter(
            grad_decoder_gain.astype(jnp.bfloat16), "seq", scatter_dimension=0, tiled=True
        ).astype(jnp.float32),
        lax.psum_scatter(
            grad_decoder_shift.astype(jnp.bfloat16), "seq", scatter_dimension=0, tiled=True
        ).astype(jnp.float32),
    )
    totals = (
        lax.psum(shards[0].astype(jnp.bfloat16), "dp").astype(jnp.float32),
        lax.psum(shards[1].astype(jnp.bfloat16), "dp").astype(jnp.float32),
        lax.psum(shards[2].astype(jnp.bfloat16), "dp").astype(jnp.float32),
        lax.psum(shards[3].astype(jnp.bfloat16), "dp").astype(jnp.float32),
        lax.psum(shards[4].astype(jnp.bfloat16), "dp").astype(jnp.float32),
        lax.psum(shards[5].astype(jnp.bfloat16), "dp").astype(jnp.float32),
        lax.psum(shards[6].astype(jnp.bfloat16), "dp").astype(jnp.float32),
        lax.psum(shards[7].astype(jnp.bfloat16), "dp").astype(jnp.float32),
        lax.psum(shards[8].astype(jnp.bfloat16), "dp").astype(jnp.float32),
        lax.psum(shards[9].astype(jnp.bfloat16), "dp").astype(jnp.float32),
        lax.psum(shards[10].astype(jnp.bfloat16), "dp").astype(jnp.float32),
        lax.psum(shards[11].astype(jnp.bfloat16), "dp").astype(jnp.float32),
        lax.psum(shards[12].astype(jnp.bfloat16), "dp").astype(jnp.float32),
        lax.psum(shards[13].astype(jnp.bfloat16), "dp").astype(jnp.float32),
        lax.psum(shards[14].astype(jnp.bfloat16), "dp").astype(jnp.float32),
        lax.psum(shards[15].astype(jnp.bfloat16), "dp").astype(jnp.float32),
        lax.psum(shards[16].astype(jnp.bfloat16), "dp").astype(jnp.float32),
        lax.psum(shards[17].astype(jnp.bfloat16), "dp").astype(jnp.float32),
        lax.psum(shards[18].astype(jnp.bfloat16), "dp").astype(jnp.float32),
        lax.psum(shards[19].astype(jnp.bfloat16), "dp").astype(jnp.float32),
        lax.psum(shards[20].astype(jnp.bfloat16), "dp").astype(jnp.float32),
        lax.psum(shards[21].astype(jnp.bfloat16), "dp").astype(jnp.float32),
        lax.psum(grad_encoder_expand.astype(jnp.bfloat16), "dp").astype(jnp.float32),
        lax.psum(grad_encoder_contract.astype(jnp.bfloat16), "dp").astype(jnp.float32),
        lax.psum(grad_decoder_expand.astype(jnp.bfloat16), "dp").astype(jnp.float32),
        lax.psum(grad_decoder_contract.astype(jnp.bfloat16), "dp").astype(jnp.float32),
    )
    return (
        encoded,
        decoded,
        grad_source,
        grad_target,
        totals[0],
        totals[1],
        totals[2],
        totals[3],
        totals[12],
        totals[13],
        totals[22],
        totals[23],
        totals[14],
        totals[15],
        totals[4],
        totals[5],
        totals[6],
        totals[7],
        totals[16],
        totals[17],
        totals[8],
        totals[9],
        totals[10],
        totals[11],
        totals[18],
        totals[19],
        totals[24],
        totals[25],
        totals[20],
        totals[21],
    )


MESH = pl.DeviceIdType.MESH
PEERS = (6, 7, 2, 3, 4, 5, 1)
low = jnp.bfloat16
wide = jnp.float32
VMEM_BYTES = 60 * 2**20


def fits_plane(mesh):
    return mesh.shape["seq"] == 8


def nt(left, right):
    return lax.dot_general(left, right, (((1,), (1,)), ((), ())), preferred_element_type=wide)


def nn(left, right):
    return lax.dot_general(left, right, (((1,), (0,)), ((), ())), preferred_element_type=wide)


def tn(left, right):
    return lax.dot_general(left, right, (((0,), (0,)), ((), ())), preferred_element_type=wide)


def lane_head(shape, size):
    return lax.broadcasted_iota(jnp.int32, shape, len(shape) - 1) // size


def vmem_spec():
    return pl.BlockSpec(memory_space=pltpu.VMEM)


def any_spec():
    return pl.BlockSpec(memory_space=pl.ANY)


def greet(masks):
    me = lax.axis_index("seq")
    barrier = pltpu.get_barrier_semaphore()
    for mask in masks:
        pl.semaphore_signal(barrier, inc=1, device_id={"seq": me ^ mask}, device_id_type=MESH)
    pl.semaphore_wait(barrier, len(masks))


def remote(src, dst, send, recv, to):
    return pltpu.make_async_remote_copy(
        src_ref=src, dst_ref=dst, send_sem=send, recv_sem=recv, device_id={"seq": to}, device_id_type=MESH
    )


def params(collective_id):
    return pltpu.CompilerParams(
        collective_id=collective_id, has_side_effects=True, vmem_limit_bytes=VMEM_BYTES
    )


def gather_table_kernel(rows, out, send, recv, keep):
    me = lax.axis_index("seq")
    mine = me // 4
    greet((1, 2, 4, 6))
    local = pltpu.make_async_copy(rows.at[mine], out.at[me], keep)
    local.start()
    started = []
    for slot, mask, table in ((0, 6, 1 - mine), (1, 2, mine), (2, 4, 1 - mine), (3, 1, mine)):
        copy = remote(rows.at[table], out.at[me], send.at[slot], recv.at[slot], me ^ mask)
        copy.start()
        started.append(copy)
    for slot, mask in ((1, 2), (2, 4), (0, 6)):
        owner = me ^ mask
        remote(rows.at[0], out.at[owner], send.at[slot], recv.at[slot], me ^ 1).wait_recv()
        copy = remote(out.at[owner], out.at[owner], send.at[4 + slot], recv.at[4 + slot], me ^ 1)
        copy.start()
        started.append(copy)
    remote(rows.at[0], out.at[me ^ 1], send.at[3], recv.at[3], me ^ 1).wait_recv()
    for slot, mask in ((1, 2), (2, 4), (0, 6)):
        remote(rows.at[0], out.at[me ^ mask ^ 1], send.at[4 + slot], recv.at[4 + slot], me ^ 1).wait_recv()
    for copy in started:
        copy.wait_send()
    local.wait()


def gather_table(rows):
    return pl.pallas_call(
        gather_table_kernel,
        out_shape=jax.ShapeDtypeStruct((8,) + rows.shape[1:], rows.dtype),
        in_specs=[any_spec()],
        out_specs=any_spec(),
        scratch_shapes=[
            pltpu.SemaphoreType.DMA((7,)),
            pltpu.SemaphoreType.DMA((7,)),
            pltpu.SemaphoreType.DMA,
        ],
        compiler_params=params(1),
    )(rows)


def heads_to_rows_kernel(blocks, out, send, recv, keep):
    me = lax.axis_index("seq")
    width = blocks.shape[2]
    greet(PEERS)

    def place(owner):
        return out.at[owner // 4, :, pl.ds(pl.multiple_of((owner % 4) * width, width), width)]

    local = pltpu.make_async_copy(blocks.at[me], place(me), keep)
    local.start()
    started = []
    for mask in PEERS:
        copy = remote(blocks.at[me ^ mask], place(me), send.at[mask], recv.at[mask], me ^ mask)
        copy.start()
        started.append(copy)
    for mask in PEERS:
        remote(blocks.at[0], place(me ^ mask), send.at[mask], recv.at[mask], me ^ mask).wait_recv()
    for copy in started:
        copy.wait_send()
    local.wait()


def heads_to_rows(blocks):
    _, rows, width = blocks.shape
    return pl.pallas_call(
        heads_to_rows_kernel,
        out_shape=jax.ShapeDtypeStruct((2, rows, 4 * width), blocks.dtype),
        in_specs=[any_spec()],
        out_specs=any_spec(),
        scratch_shapes=[
            pltpu.SemaphoreType.DMA((8,)),
            pltpu.SemaphoreType.DMA((8,)),
            pltpu.SemaphoreType.DMA,
        ],
        compiler_params=params(2),
    )(blocks)


def rows_to_heads_kernel(rows, out, send, recv, keep):
    me = lax.axis_index("seq")
    width = out.shape[2]
    greet(PEERS)

    def part(owner):
        return rows.at[owner // 4, :, pl.ds(pl.multiple_of((owner % 4) * width, width), width)]

    local = pltpu.make_async_copy(part(me), out.at[me], keep)
    local.start()
    started = []
    for mask in PEERS:
        copy = remote(part(me ^ mask), out.at[me], send.at[mask], recv.at[mask], me ^ mask)
        copy.start()
        started.append(copy)
    for mask in PEERS:
        remote(part(me), out.at[me ^ mask], send.at[mask], recv.at[mask], me ^ mask).wait_recv()
    for copy in started:
        copy.wait_send()
    local.wait()


def rows_to_heads(rows):
    _, count, width = rows.shape
    return pl.pallas_call(
        rows_to_heads_kernel,
        out_shape=jax.ShapeDtypeStruct((8, count, width // 4), rows.dtype),
        in_specs=[any_spec()],
        out_specs=any_spec(),
        scratch_shapes=[
            pltpu.SemaphoreType.DMA((8,)),
            pltpu.SemaphoreType.DMA((8,)),
            pltpu.SemaphoreType.DMA,
        ],
        compiler_params=params(3),
    )(rows)


def sum_small_kernel(terms, out, mine, came, send, recv, send_back, recv_back):
    me = lax.axis_index("seq")
    greet(PEERS)
    mine[...] = terms[...].astype(low)
    started = []
    for mask in PEERS:
        copy = remote(mine.at[me ^ mask], came.at[mask], send.at[mask], recv.at[mask], me ^ mask)
        copy.start()
        started.append(copy)
    total = terms[me].astype(wide)
    for mask in PEERS:
        remote(mine.at[0], came.at[mask], send.at[mask], recv.at[mask], me ^ mask).wait_recv()
        total = total + came[mask].astype(wide)
    out[me] = total.astype(low)
    for mask in PEERS:
        copy = remote(out.at[me], out.at[me], send_back.at[mask], recv_back.at[mask], me ^ mask)
        copy.start()
        started.append(copy)
    for mask in PEERS:
        remote(mine.at[0], out.at[me ^ mask], send_back.at[mask], recv_back.at[mask], me ^ mask).wait_recv()
    for copy in started:
        copy.wait_send()


def sum_small(terms):
    count, width = terms.shape
    blocks = (8, count // 8, width)
    return pl.pallas_call(
        sum_small_kernel,
        out_shape=jax.ShapeDtypeStruct(blocks, low),
        in_specs=[vmem_spec()],
        out_specs=vmem_spec(),
        scratch_shapes=[pltpu.VMEM(blocks, low), pltpu.VMEM(blocks, low)]
        + [pltpu.SemaphoreType.DMA((8,))] * 4,
        compiler_params=params(4),
    )(terms.reshape(blocks)).reshape(count, width)


def merge_parts_kernel(terms, stats, out, logsum, came, came_stats, send, recv, send_st, recv_st, back, recv_back, back_st, recv_back_st):
    me = lax.axis_index("seq")
    width = out.shape[2]
    greet(PEERS)
    started = []
    for mask in PEERS:
        for src, dst, s, r in ((stats, came_stats, send_st, recv_st), (terms, came, send, recv)):
            copy = remote(src.at[me ^ mask], dst.at[mask], s.at[mask], r.at[mask], me ^ mask)
            copy.start()
            started.append(copy)
    for mask in PEERS:
        remote(stats.at[0], came_stats.at[mask], send_st.at[mask], recv_st.at[mask], me ^ mask).wait_recv()
    tops = [stats[me, 0]] + [came_stats[mask, 0] for mask in PEERS]
    sums = [stats[me, 1]] + [came_stats[mask, 1] for mask in PEERS]
    top = functools.reduce(jnp.maximum, tops)
    weights = [s * jnp.exp(t - top) for t, s in zip(tops, sums)]
    total = functools.reduce(jnp.add, weights)
    logsum[me] = top + jnp.log(total)
    size = width // HEADS
    spread = (
        lax.broadcasted_iota(jnp.int32, (128, width), 1) // size
        == lax.broadcasted_iota(jnp.int32, (128, width), 0)
    ).astype(wide)
    scaled = jnp.concatenate([w / total for w in weights], 0)
    scaled = lax.dot_general(
        scaled, spread, (((1,), (0,)), ((), ())), precision=lax.Precision.HIGHEST, preferred_element_type=wide
    )
    rows = tops[0].shape[0]
    result = scaled[:rows] * terms[me].astype(wide)
    for place, mask in enumerate(PEERS):
        remote(terms.at[0], came.at[mask], send.at[mask], recv.at[mask], me ^ mask).wait_recv()
        result = result + scaled[(place + 1) * rows : (place + 2) * rows] * came[mask].astype(wide)
    out[me] = result.astype(low)
    for mask in PEERS:
        for ref, s, r in ((out, back, recv_back), (logsum, back_st, recv_back_st)):
            copy = remote(ref.at[me], ref.at[me], s.at[mask], r.at[mask], me ^ mask)
            copy.start()
            started.append(copy)
    for mask in PEERS:
        for ref, s, r in ((out, back, recv_back), (logsum, back_st, recv_back_st)):
            remote(ref.at[me], ref.at[me ^ mask], s.at[mask], r.at[mask], me ^ mask).wait_recv()
    for copy in started:
        copy.wait_send()


def merge_parts(terms, tops, sums):
    count, width = terms.shape
    rows = count // 8
    stats = jnp.stack([tops.reshape(8, rows, 128), sums.reshape(8, rows, 128)], 1)
    out, logsum = pl.pallas_call(
        merge_parts_kernel,
        out_shape=(
            jax.ShapeDtypeStruct((8, rows, width), low),
            jax.ShapeDtypeStruct((8, rows, 128), wide),
        ),
        in_specs=[vmem_spec()] * 2,
        out_specs=(vmem_spec(), vmem_spec()),
        scratch_shapes=[pltpu.VMEM((8, rows, width), low), pltpu.VMEM((8, 2, rows, 128), wide)]
        + [pltpu.SemaphoreType.DMA((8,))] * 8,
        compiler_params=params(5),
    )(terms.reshape(8, rows, width), stats)
    return out.reshape(count, width), logsum.reshape(count, 128)


def scatter_rows_kernel(terms, grads, out, out_grads, sib, pair, came, send, recv, send_pair, recv_pair, send_grad, recv_grad, keep):
    me = lax.axis_index("seq")
    mine = me // 4
    core = me % 2
    greet(PEERS)
    local = pltpu.make_async_copy(grads.at[me], out_grads.at[me], keep)
    local.start()
    started = []
    chips = (6, 2, 4, 0)
    for slot, mask in enumerate(chips):
        copy = remote(terms.at[me ^ 1 ^ mask], sib.at[slot], send.at[slot], recv.at[slot], me ^ 1)
        copy.start()
        started.append(copy)
    for slot, mask in enumerate(chips):
        remote(terms.at[0], sib.at[slot], send.at[slot], recv.at[slot], me ^ 1).wait_recv()
        if mask:
            pair[slot] = (terms[me ^ mask].astype(wide) + sib[slot].astype(wide)).astype(low)
            copy = remote(pair.at[slot], came.at[slot], send_pair.at[slot], recv_pair.at[slot], me ^ mask)
            copy.start()
            started.append(copy)
    for mask in PEERS:
        copy = remote(grads.at[me ^ mask], out_grads.at[me], send_grad.at[mask], recv_grad.at[mask], me ^ mask)
        copy.start()
        started.append(copy)
    for slot, mask in enumerate(chips[:3]):
        remote(pair.at[0], came.at[slot], send_pair.at[slot], recv_pair.at[slot], me ^ mask).wait_recv()
    out[mine] = terms[me].astype(wide) + sib[3].astype(wide) + came[1].astype(wide)
    out[1 - mine] = came[2].astype(wide) + came[0].astype(wide)
    for mask in PEERS:
        remote(grads.at[0], out_grads.at[me ^ mask], send_grad.at[mask], recv_grad.at[mask], me ^ mask).wait_recv()
    for copy in started:
        copy.wait_send()
    local.wait()


def scatter_rows(terms, grads):
    _, rows, width = terms.shape
    return pl.pallas_call(
        scatter_rows_kernel,
        out_shape=(
            jax.ShapeDtypeStruct((2, rows, width), wide),
            jax.ShapeDtypeStruct(grads.shape, low),
        ),
        in_specs=[vmem_spec(), any_spec()],
        out_specs=(vmem_spec(), any_spec()),
        scratch_shapes=[
            pltpu.VMEM((4, rows, width), low),
            pltpu.VMEM((3, rows, width), low),
            pltpu.VMEM((3, rows, width), low),
            pltpu.SemaphoreType.DMA((4,)),
            pltpu.SemaphoreType.DMA((4,)),
            pltpu.SemaphoreType.DMA((3,)),
            pltpu.SemaphoreType.DMA((3,)),
            pltpu.SemaphoreType.DMA((8,)),
            pltpu.SemaphoreType.DMA((8,)),
            pltpu.SemaphoreType.DMA,
        ],
        compiler_params=params(6),
    )(terms, grads)


def plain(**more):
    return pltpu.CompilerParams(vmem_limit_bytes=VMEM_BYTES, **more)


def flash_forward_kernel(length, queries, keys, values, context, logsum):
    rows, width = queries.shape
    count = keys.shape[0]
    heads = width // 64
    of_head = lane_head((1, width), 64)
    q = queries[...] * jnp.asarray(0.125, low)
    k = keys[...]
    v = values[...]
    total = jnp.zeros((rows, width), wide)
    logs = jnp.zeros((rows, 128), wide)
    lanes = lax.broadcasted_iota(jnp.int32, (1, 128), 1)
    fill = jnp.where(lax.broadcasted_iota(jnp.int32, (1, count), 1) < length[0], 0.0, masked_fill)
    for head in range(heads):
        scores = nt(jnp.where(of_head == head, q, jnp.zeros_like(q)), k) + fill
        top = jnp.max(scores, -1, keepdims=True)
        weights = jnp.exp(scores - top)
        summed = jnp.sum(weights, -1, keepdims=True)
        probs = (weights * (1.0 / summed)).astype(low)
        part = nn(probs, v)
        total = jnp.where(of_head == head, part, total)
        logs = jnp.where(lanes == head, top + jnp.log(summed), logs)
    context[...] = total.astype(low)
    logsum[...] = logs


def flash_forward(length, queries, keys, values, block):
    count, width = queries.shape
    return pl.pallas_call(
        flash_forward_kernel,
        out_shape=(
            jax.ShapeDtypeStruct((count, width), low),
            jax.ShapeDtypeStruct((count, 128), wide),
        ),
        grid_spec=pltpu.PrefetchScalarGridSpec(
            num_scalar_prefetch=1,
            grid=(count // block,),
            in_specs=[
                pl.BlockSpec((block, width), lambda i, n: (i, 0)),
                pl.BlockSpec((count, width), lambda i, n: (0, 0)),
                pl.BlockSpec((count, width), lambda i, n: (0, 0)),
            ],
            out_specs=[
                pl.BlockSpec((block, width), lambda i, n: (i, 0)),
                pl.BlockSpec((block, 128), lambda i, n: (i, 0)),
            ],
        ),
        compiler_params=plain(),
        cost_estimate=pl.CostEstimate(
            flops=16 * count * count * width, bytes_accessed=8 * count * width, transcendentals=0
        ),
    )(length, queries, keys, values)


def flash_backward_kernel(chunk, length, queries, grads, logsum, delta, keys, keys_t, values, dq_t, dk, dv, q_stack, g_stack, p_stack, s_stack, k_sum, v_sum):
    step = pl.program_id(0)
    rows, width = queries.shape
    count = keys.shape[0]
    heads = width // 64
    of_head = lane_head((1, width), 64)

    @pl.when(step == 0)
    def _():
        k_sum[...] = jnp.zeros_like(k_sum)
        v_sum[...] = jnp.zeros_like(v_sum)

    q = queries[...] * jnp.asarray(0.125, low)
    g = grads[...]
    for head in range(heads):
        place = pl.ds(head * rows, rows)
        q_stack[place] = jnp.where(of_head == head, q, jnp.zeros_like(q))
        g_stack[place] = jnp.where(of_head == head, g, jnp.zeros_like(g))
    dq_sums = [jnp.zeros((64, rows), wide)] * heads
    for start in range(0, count, chunk):
        part = pl.ds(start, chunk)
        k = keys[part]
        v = values[part]
        allowed = start + lax.broadcasted_iota(jnp.int32, (chunk, 1), 0) < length[0]
        fill = jnp.where(allowed, 0.0, masked_fill)
        for head in range(heads):
            place = pl.ds(head * rows, rows)
            scores = nt(k, q_stack[place])
            probs = jnp.exp(scores - logsum[head : head + 1, :] + fill)
            p_stack[:, place] = probs.astype(low)
            d_probs = nt(v, g_stack[place])
            d_scores = (probs * (d_probs - delta[head : head + 1, :])).astype(low)
            s_stack[:, place] = d_scores
            dq_sums[head] = dq_sums[head] + nn(keys_t[head * 64 : head * 64 + 64, part], d_scores)
        v_sum[part] += nn(p_stack[...], g_stack[...])
        k_sum[part] += nn(s_stack[...], q_stack[...])
    for head in range(heads):
        dq_t[head * 64 : head * 64 + 64, :] = (dq_sums[head] * 0.125).astype(low)

    @pl.when(step == pl.num_programs(0) - 1)
    def _():
        dk[...] = k_sum[...].astype(low)
        dv[...] = v_sum[...].astype(low)


def flash_backward(length, queries, grads, logsum, delta, keys, values, block, chunk):
    count, width = queries.shape
    heads = width // 64
    return pl.pallas_call(
        functools.partial(flash_backward_kernel, chunk),
        out_shape=(
            jax.ShapeDtypeStruct((width, count), low),
            jax.ShapeDtypeStruct((count, width), low),
            jax.ShapeDtypeStruct((count, width), low),
        ),
        grid_spec=pltpu.PrefetchScalarGridSpec(
            num_scalar_prefetch=1,
            grid=(count // block,),
            in_specs=[
                pl.BlockSpec((block, width), lambda i, n: (i, 0)),
                pl.BlockSpec((block, width), lambda i, n: (i, 0)),
                pl.BlockSpec((heads, block), lambda i, n: (0, i)),
                pl.BlockSpec((heads, block), lambda i, n: (0, i)),
                pl.BlockSpec((count, width), lambda i, n: (0, 0)),
                pl.BlockSpec((width, count), lambda i, n: (0, 0)),
                pl.BlockSpec((count, width), lambda i, n: (0, 0)),
            ],
            out_specs=[
                pl.BlockSpec((width, block), lambda i, n: (0, i)),
                pl.BlockSpec((count, width), lambda i, n: (0, 0)),
                pl.BlockSpec((count, width), lambda i, n: (0, 0)),
            ],
            scratch_shapes=[
                pltpu.VMEM((heads * block, width), low),
                pltpu.VMEM((heads * block, width), low),
                pltpu.VMEM((chunk, heads * block), low),
                pltpu.VMEM((chunk, heads * block), low),
                pltpu.VMEM((count, width), wide),
                pltpu.VMEM((count, width), wide),
            ],
        ),
        compiler_params=plain(),
        cost_estimate=pl.CostEstimate(
            flops=40 * count * count * width, bytes_accessed=14 * count * width, transcendentals=0
        ),
    )(length, queries, grads, logsum, delta, keys, keys.T, values)


def small_forward_kernel(causal, length, queries, keys, values, context, tops, sums):
    table = pl.program_id(0)
    rows, width = queries.shape
    count = keys.shape[0]
    half = lane_head((1, 128), 64)
    lanes = lax.broadcasted_iota(jnp.int32, (1, 128), 1)
    allowed = lax.broadcasted_iota(jnp.int32, (rows, count), 1) < length[table]
    if causal:
        allowed = allowed & (
            lax.broadcasted_iota(jnp.int32, (rows, count), 1)
            <= lax.broadcasted_iota(jnp.int32, (rows, count), 0)
        )
    top_all = jnp.zeros((rows, 128), wide)
    sum_all = jnp.ones((rows, 128), wide)
    for two in range(width // 128):
        place = pl.ds(two * 128, 128)
        q = queries[:, place] * jnp.asarray(0.125, low)
        k = keys[:, place]
        v = values[:, place]
        total = jnp.zeros((rows, 128), wide)
        for side in range(2):
            scores = nt(jnp.where(half == side, q, jnp.zeros_like(q)), k)
            scores = jnp.where(allowed, scores, masked_fill)
            top = jnp.max(scores, -1, keepdims=True)
            weights = jnp.exp(scores - top)
            summed = jnp.sum(weights, -1, keepdims=True)
            probs = (weights * (1.0 / summed)).astype(low)
            total = jnp.where(half == side, nn(probs, v), total)
            top_all = jnp.where(lanes == 2 * two + side, top, top_all)
            sum_all = jnp.where(lanes == 2 * two + side, summed, sum_all)
        context[:, place] = total.astype(low)
    tops[...] = top_all
    sums[...] = sum_all


def small_forward(length, queries, keys, values, causal):
    tables = length.shape[0]
    rows, width = queries.shape[0] // tables, queries.shape[1]
    count = keys.shape[0] // tables

    def block(size, last):
        return pl.BlockSpec((size, last), lambda t, n: (t, 0))

    return pl.pallas_call(
        functools.partial(small_forward_kernel, causal),
        out_shape=(
            jax.ShapeDtypeStruct(queries.shape, low),
            jax.ShapeDtypeStruct((queries.shape[0], 128), wide),
            jax.ShapeDtypeStruct((queries.shape[0], 128), wide),
        ),
        grid_spec=pltpu.PrefetchScalarGridSpec(
            num_scalar_prefetch=1,
            grid=(tables,),
            in_specs=[block(rows, width), block(count, width), block(count, width)],
            out_specs=[block(rows, width), block(rows, 128), block(rows, 128)],
        ),
        compiler_params=plain(),
        cost_estimate=pl.CostEstimate(
            flops=16 * tables * rows * count * width, bytes_accessed=6 * tables * count * width, transcendentals=0
        ),
    )(length, queries, keys, values)


def small_backward_kernel(causal, length, queries, keys, values, grads, context, logsum, dq, dk, dv):
    table = pl.program_id(0)
    rows, width = queries.shape
    count = keys.shape[0]
    half = lane_head((1, 128), 64)
    allowed = lax.broadcasted_iota(jnp.int32, (rows, count), 1) < length[table]
    if causal:
        allowed = allowed & (
            lax.broadcasted_iota(jnp.int32, (rows, count), 1)
            <= lax.broadcasted_iota(jnp.int32, (rows, count), 0)
        )
    logs = logsum[...]
    for two in range(width // 128):
        place = pl.ds(two * 128, 128)
        q = queries[:, place] * jnp.asarray(0.125, low)
        k = keys[:, place]
        v = values[:, place]
        g = grads[:, place]
        both = g.astype(wide) * context[:, place].astype(wide)
        dq_here = jnp.zeros((rows, 128), wide)
        dk_here = jnp.zeros((count, 128), wide)
        dv_here = jnp.zeros((count, 128), wide)
        for side in range(2):
            head = 2 * two + side
            q_one = jnp.where(half == side, q, jnp.zeros_like(q))
            g_one = jnp.where(half == side, g, jnp.zeros_like(g))
            delta = jnp.sum(jnp.where(half == side, both, 0.0), -1, keepdims=True)
            scores = nt(q_one, k)
            probs = jnp.where(allowed, jnp.exp(scores - logs[:, head : head + 1]), 0.0)
            d_probs = nt(g_one, v)
            d_scores = (probs * (d_probs - delta)).astype(low)
            dq_here = jnp.where(half == side, nn(d_scores, k), dq_here)
            dk_here = dk_here + tn(d_scores, q_one)
            dv_here = dv_here + tn(probs.astype(low), g_one)
        dq[:, place] = dq_here * 0.125
        dk[:, place] = dk_here.astype(low)
        dv[:, place] = dv_here.astype(low)


def small_backward(length, queries, keys, values, grads, context, logsum, causal):
    tables = length.shape[0]
    rows, width = queries.shape[0] // tables, queries.shape[1]
    count = keys.shape[0] // tables

    def block(size, last):
        return pl.BlockSpec((size, last), lambda t, n: (t, 0))

    return pl.pallas_call(
        functools.partial(small_backward_kernel, causal),
        out_shape=(
            jax.ShapeDtypeStruct(queries.shape, wide),
            jax.ShapeDtypeStruct(keys.shape, low),
            jax.ShapeDtypeStruct(keys.shape, low),
        ),
        grid_spec=pltpu.PrefetchScalarGridSpec(
            num_scalar_prefetch=1,
            grid=(tables,),
            in_specs=[
                block(rows, width),
                block(count, width),
                block(count, width),
                block(rows, width),
                block(rows, width),
                block(rows, 128),
            ],
            out_specs=[block(rows, width), block(count, width), block(count, width)],
        ),
        compiler_params=plain(),
        cost_estimate=pl.CostEstimate(
            flops=40 * tables * rows * count * width, bytes_accessed=10 * tables * count * width, transcendentals=0
        ),
    )(length, queries, keys, values, grads, context, logsum)


def gelu_parts(values):
    bell = 0.5 * (1.0 + lax.erf(values * 0.7071067811865476))
    slope = bell + values * (0.3989422804014327 * jnp.exp(-0.5 * values * values))
    return values * bell, slope


def feed_forward_kernel(rows, expand, contract, out, acts, slopes):
    act, slope = gelu_parts(nn(rows[...], expand[0]))
    act = act.astype(low)
    acts[0] = act
    slopes[0] = slope.astype(low)
    term = nn(act, contract[0])

    @pl.when(pl.program_id(0) == 0)
    def _():
        out[...] = term

    @pl.when(pl.program_id(0) > 0)
    def _():
        out[...] += term


def feed_forward(rows, expand, contract):
    count, width = rows.shape
    parts, _, hidden = expand.shape
    return pl.pallas_call(
        feed_forward_kernel,
        out_shape=(
            jax.ShapeDtypeStruct((count, width), wide),
            jax.ShapeDtypeStruct((parts, count, hidden), low),
            jax.ShapeDtypeStruct((parts, count, hidden), low),
        ),
        grid=(parts,),
        in_specs=[
            pl.BlockSpec((count, width), lambda j: (0, 0)),
            pl.BlockSpec((1, width, hidden), lambda j: (j, 0, 0)),
            pl.BlockSpec((1, hidden, width), lambda j: (j, 0, 0)),
        ],
        out_specs=[
            pl.BlockSpec((count, width), lambda j: (0, 0)),
            pl.BlockSpec((1, count, hidden), lambda j: (j, 0, 0)),
            pl.BlockSpec((1, count, hidden), lambda j: (j, 0, 0)),
        ],
        compiler_params=plain(),
        cost_estimate=pl.CostEstimate(
            flops=4 * count * width * hidden * parts, bytes_accessed=4 * width * hidden * parts, transcendentals=0
        ),
    )(rows, expand, contract)


def feed_backward_kernel(rows_t, grads, acts, slopes, expand, contract, out, d_expand, d_contract):
    g = grads[...]
    act = acts[0]
    d_hidden = (nt(g, contract[0]) * slopes[0].astype(wide)).astype(low)
    d_contract[0] = tn(act, g).astype(low)
    d_expand[0] = nn(rows_t[...], d_hidden).astype(low)
    term = nt(d_hidden, expand[0])

    @pl.when(pl.program_id(0) == 0)
    def _():
        out[...] = term

    @pl.when(pl.program_id(0) > 0)
    def _():
        out[...] += term


def feed_backward(rows, grads, acts, slopes, expand, contract):
    count, width = rows.shape
    parts, _, hidden = expand.shape
    return pl.pallas_call(
        feed_backward_kernel,
        out_shape=(
            jax.ShapeDtypeStruct((count, width), wide),
            jax.ShapeDtypeStruct((parts, width, hidden), low),
            jax.ShapeDtypeStruct((parts, hidden, width), low),
        ),
        grid=(parts,),
        in_specs=[
            pl.BlockSpec((width, count), lambda j: (0, 0)),
            pl.BlockSpec((count, width), lambda j: (0, 0)),
            pl.BlockSpec((1, count, hidden), lambda j: (j, 0, 0)),
            pl.BlockSpec((1, count, hidden), lambda j: (j, 0, 0)),
            pl.BlockSpec((1, width, hidden), lambda j: (j, 0, 0)),
            pl.BlockSpec((1, hidden, width), lambda j: (j, 0, 0)),
        ],
        out_specs=[
            pl.BlockSpec((count, width), lambda j: (0, 0)),
            pl.BlockSpec((1, width, hidden), lambda j: (j, 0, 0)),
            pl.BlockSpec((1, hidden, width), lambda j: (j, 0, 0)),
        ],
        compiler_params=plain(),
        cost_estimate=pl.CostEstimate(
            flops=8 * count * width * hidden * parts, bytes_accessed=10 * width * hidden * parts, transcendentals=0
        ),
    )(rows.T, grads, acts, slopes, expand, contract)


def plane_body(
    source_tokens,
    target_tokens,
    source_lengths,
    target_lengths,
    encoder_query,
    encoder_key,
    encoder_value,
    encoder_mix,
    attend_gain,
    attend_shift,
    encoder_expand,
    encoder_contract,
    encoder_gain,
    encoder_shift,
    decoder_query,
    decoder_key,
    decoder_value,
    decoder_mix,
    self_gain,
    self_shift,
    cross_query,
    cross_key,
    cross_value,
    cross_mix,
    cross_gain,
    cross_shift,
    decoder_expand,
    decoder_contract,
    decoder_gain,
    decoder_shift,
    source_cotangent,
    target_cotangent,
):
    slots, tables, width = source_tokens.shape
    places = target_tokens.shape[0]
    me = lax.axis_index("seq")
    quarter = width // 4
    slice_rows = width // 8

    def flat(array):
        return jnp.swapaxes(array, 0, 1).reshape(-1, width)

    def unflat(array):
        return jnp.swapaxes(array.reshape(tables, -1, width), 0, 1)

    def columns(weight):
        return lax.dynamic_slice_in_dim(weight, (me % 4) * quarter, quarter, 1)

    def own(rows):
        return lax.dynamic_slice_in_dim(rows, me * slice_rows, slice_rows, 1)

    def own_places(rows):
        return lax.dynamic_slice_in_dim(rows.reshape(tables, 8 * places, width), me * places, places, 1)

    def own_vector(vector):
        return lax.dynamic_slice_in_dim(vector, me * slice_rows, slice_rows, 0)

    source_flat = flat(source_tokens)
    target_all = lax.all_gather(
        jnp.stack([jnp.swapaxes(target_tokens, 0, 1), jnp.swapaxes(target_cotangent, 0, 1)], 0), "seq", axis=2, tiled=True
    )
    target_flat = target_all[0].reshape(-1, width)
    target_grad = target_all[1].reshape(-1, width)
    all_expand = lax.all_gather(encoder_expand, "seq", axis=0)
    all_contract = lax.all_gather(encoder_contract, "seq", axis=0)

    rows = gather_table(source_flat.reshape(tables, slots, width))
    rows = rows.reshape(-1, width)
    w_query, w_key, w_value = columns(encoder_query), columns(encoder_key), columns(encoder_value)
    length = lax.dynamic_slice_in_dim(source_lengths, me // 4, 1, 0)
    queries = project(rows, w_query).astype(low)
    keys = project(rows, w_key).astype(low)
    values = project(rows, w_value).astype(low)
    context, logsum = flash_forward(length, queries, keys, values, 256)
    encoder_context = heads_to_rows(context.reshape(8, slots, quarter)).reshape(-1, width)
    first, first_back = jax.vjp(
        layer_norm, source_flat.astype(wide) + project(encoder_context, encoder_mix), attend_gain, attend_shift
    )
    first_low = first.astype(low)
    widened, acts, slopes = feed_forward(first_low, all_expand, all_contract)
    second, second_back = jax.vjp(layer_norm, first + widened, encoder_gain, encoder_shift)
    encoded = second.astype(low)

    self_queries = project(target_flat, decoder_query).astype(low)
    self_keys = project(target_flat, decoder_key).astype(low)
    self_values = project(target_flat, decoder_value).astype(low)
    decoder_context, self_tops, self_sums = small_forward(
        target_lengths, self_queries, self_keys, self_values, True
    )
    self_logs = self_tops + jnp.log(self_sums)
    third, third_back = jax.vjp(
        layer_norm, target_flat.astype(wide) + project(decoder_context, decoder_mix), self_gain, self_shift
    )
    third_low = third.astype(low)
    cross_queries = project(third_low, cross_query).astype(low)

    cross_keys = project(encoded, cross_key).astype(low)
    cross_values = project(encoded, cross_value).astype(low)
    here = source_lengths - me * slots
    part, part_tops, part_sums = small_forward(here, cross_queries, cross_keys, cross_values, False)
    cross_context, cross_logs = merge_parts(part, part_tops, part_sums)
    fourth, fourth_back = jax.vjp(
        layer_norm, third + project(cross_context, cross_mix), cross_gain, cross_shift
    )
    fourth_low = fourth.astype(low)
    hidden = project(fourth_low, decoder_expand)
    decoder_acts, gelu_back = jax.vjp(gelu_exact, hidden)
    decoder_acts = decoder_acts.astype(low)
    narrowed = sum_small(project(decoder_acts, decoder_contract)).astype(wide)
    fifth, fifth_back = jax.vjp(layer_norm, fourth + narrowed, decoder_gain, decoder_shift)
    decoded = jnp.swapaxes(own_places(fifth.astype(low)), 0, 1)

    d_fifth, grad_decoder_gain, grad_decoder_shift = fifth_back(target_grad.astype(wide))
    fifth_low = d_fifth.astype(low)
    d_hidden = gelu_back(project_back(fifth_low, decoder_contract))[0].astype(low)
    grad_decoder_expand = outer_sum(fourth_low, d_hidden)
    grad_decoder_contract = outer_sum(decoder_acts, fifth_low)
    d_rows = sum_small(project_back(d_hidden, decoder_expand)).astype(wide)
    d_fourth, grad_cross_gain, grad_cross_shift = fourth_back(d_fifth + d_rows)
    cross_low = d_fourth.astype(low)
    grad_cross_mix = outer_sum(own(cross_context), cross_low)
    d_cross = project_back(cross_low, cross_mix).astype(low)
    dq_part, dk_cross, dv_cross = small_backward(
        here, cross_queries, cross_keys, cross_values, d_cross, cross_context, cross_logs, False
    )
    d_encoded = project_back(dk_cross, cross_key) + project_back(dv_cross, cross_value)
    cross_pair = outer_sum(encoded, jnp.concatenate([dk_cross, dv_cross], 1)).astype(low)
    cross_pair = lax.psum_scatter(cross_pair, "seq", scatter_dimension=0, tiled=True)

    d_second, grad_encoder_gain, grad_encoder_shift = second_back(flat(source_cotangent).astype(wide) + d_encoded)
    d_rows, d_expand, d_contract = feed_backward(
        first_low, d_second.astype(low), acts, slopes, all_expand, all_contract
    )
    d_expand = lax.psum_scatter(d_expand, "seq", scatter_dimension=0, tiled=False)
    d_contract = lax.psum_scatter(d_contract, "seq", scatter_dimension=0, tiled=False)
    d_first, grad_attend_gain, grad_attend_shift = first_back(d_second + d_rows)
    encoder_low = d_first.astype(low)
    encoder_mix_part = outer_sum(encoder_context, encoder_low).astype(low)
    encoder_mix_part = lax.psum_scatter(encoder_mix_part, "seq", scatter_dimension=0, tiled=True)
    d_context = rows_to_heads(project_back(encoder_low, encoder_mix).astype(low).reshape(tables, slots, width))
    d_context = d_context.reshape(-1, quarter)
    delta = jnp.sum(
        (d_context.astype(wide) * context.astype(wide)).reshape(-1, quarter // 64, 64), -1
    )
    dq_t, dk, dv = flash_backward(
        length, queries, d_context, logsum[:, : quarter // 64].T, delta.T, keys, values, 256, 512
    )
    term = (
        lax.dot_general(dq_t, w_query, (((0,), (1,)), ((), ())), preferred_element_type=wide)
        + project_back(dk, w_key)
        + project_back(dv, w_value)
    ).astype(low)
    weight_terms = jnp.concatenate(
        [
            lax.dot_general(rows, dq_t, (((0,), (1,)), ((), ())), preferred_element_type=wide).astype(low),
            outer_sum(rows, dk).astype(low),
            outer_sum(rows, dv).astype(low),
        ],
        1,
    )
    vectors = jnp.stack(
        [grad_attend_gain, grad_attend_shift, grad_encoder_gain, grad_encoder_shift], 0
    ).astype(low)
    vectors = jnp.swapaxes(vectors.reshape(4, 8, slice_rows), 0, 1)
    vectors = jnp.pad(vectors, ((0, 0), (0, 12), (0, 3 * quarter - slice_rows)))
    grads = jnp.concatenate([weight_terms.reshape(8, slice_rows, 3 * quarter), vectors], 1)
    d_source, came = scatter_rows(term.reshape(8, slots, width), grads)
    came = jnp.sum(came.reshape(2, 4, slice_rows + 16, 3 * quarter).astype(wide), 0)
    grad_source = unflat(d_first + d_source.reshape(-1, width))
    encoder_three = jnp.moveaxis(came[:, :slice_rows].reshape(4, slice_rows, 3, quarter), (2, 1), (0, 1))
    encoder_three = encoder_three.reshape(3, slice_rows, width)
    encoder_vectors = jnp.sum(came[:, slice_rows : slice_rows + 4, :slice_rows], 0)

    dq_cross = sum_small(dq_part)
    grad_cross_query = outer_sum(own(third_low), dq_cross)
    d_third, grad_self_gain, grad_self_shift = third_back(d_fourth + project_back(dq_cross, cross_query))
    self_low = d_third.astype(low)
    grad_decoder_mix = outer_sum(own(decoder_context), self_low)
    dq_self, dk_self, dv_self = small_backward(
        target_lengths,
        self_queries,
        self_keys,
        self_values,
        project_back(self_low, decoder_mix).astype(low),
        decoder_context,
        self_logs,
        True,
    )
    dq_self = dq_self.astype(low)
    target_own = own(target_flat)
    grad_decoder_query = outer_sum(target_own, dq_self)
    grad_decoder_key = outer_sum(target_own, dk_self)
    grad_decoder_value = outer_sum(target_own, dv_self)
    grad_target = own_places(
        d_third
        + project_back(dq_self, decoder_query)
        + project_back(dk_self, decoder_key)
        + project_back(dv_self, decoder_value)
    )
    grad_target = jnp.swapaxes(grad_target, 0, 1)

    def over_tables(*arrays):
        return [a.astype(wide) for a in lax.psum([a.astype(low) for a in arrays], "dp")]

    decoder_vectors = jnp.stack(
        [
            own_vector(v)
            for v in (
                grad_self_gain,
                grad_self_shift,
                grad_cross_gain,
                grad_cross_shift,
                grad_decoder_gain,
                grad_decoder_shift,
            )
        ],
        0,
    )
    (
        grad_decoder_query,
        grad_decoder_key,
        grad_decoder_value,
        grad_decoder_mix,
        grad_cross_query,
        grad_cross_mix,
        grad_decoder_expand,
        grad_decoder_contract,
        decoder_vectors,
    ) = over_tables(
        grad_decoder_query,
        grad_decoder_key,
        grad_decoder_value,
        grad_decoder_mix,
        grad_cross_query,
        grad_cross_mix,
        grad_decoder_expand,
        grad_decoder_contract,
        decoder_vectors,
    )
    cross_pair, d_expand, d_contract, encoder_mix_part, decoder_vectors = lax.optimization_barrier(
        (cross_pair, d_expand, d_contract, encoder_mix_part, decoder_vectors)
    )
    cross_pair, d_expand, d_contract, encoder_mix_part = over_tables(
        cross_pair, d_expand, d_contract, encoder_mix_part
    )
    encoder_three, encoder_vectors, encoder_mix_part = lax.optimization_barrier(
        (encoder_three, encoder_vectors, encoder_mix_part)
    )
    encoder_three, encoder_vectors = over_tables(encoder_three, encoder_vectors)
    return (
        unflat(encoded),
        decoded,
        grad_source,
        grad_target,
        encoder_three[0],
        encoder_three[1],
        encoder_three[2],
        encoder_mix_part,
        encoder_vectors[0],
        encoder_vectors[1],
        d_expand,
        d_contract,
        encoder_vectors[2],
        encoder_vectors[3],
        grad_decoder_query,
        grad_decoder_key,
        grad_decoder_value,
        grad_decoder_mix,
        decoder_vectors[0],
        decoder_vectors[1],
        grad_cross_query,
        cross_pair[:, :width],
        cross_pair[:, width:],
        grad_cross_mix,
        decoder_vectors[2],
        decoder_vectors[3],
        grad_decoder_expand,
        grad_decoder_contract,
        decoder_vectors[4],
        decoder_vectors[5],
    )


def solution(mesh):
    body = plane_body if fits_plane(mesh) else general_body
    in_specs = (
        P("seq", "dp", None),
        P("seq", "dp", None),
        P("dp"),
        P("dp"),
        P(),
        P(),
        P(),
        P(),
        P(),
        P(),
        P(None, "seq"),
        P("seq", None),
        P(),
        P(),
        P(),
        P(),
        P(),
        P(),
        P(),
        P(),
        P(),
        P(),
        P(),
        P(),
        P(),
        P(),
        P(None, "seq"),
        P("seq", None),
        P(),
        P(),
        P("seq", "dp", None),
        P("seq", "dp", None),
    )
    out_specs = (
        P("seq", "dp", None),
        P("seq", "dp", None),
        P("seq", "dp", None),
        P("seq", "dp", None),
        P("seq", None),
        P("seq", None),
        P("seq", None),
        P("seq", None),
        P("seq"),
        P("seq"),
        P(None, "seq"),
        P("seq", None),
        P("seq"),
        P("seq"),
        P("seq", None),
        P("seq", None),
        P("seq", None),
        P("seq", None),
        P("seq"),
        P("seq"),
        P("seq", None),
        P("seq", None),
        P("seq", None),
        P("seq", None),
        P("seq"),
        P("seq"),
        P(None, "seq"),
        P("seq", None),
        P("seq"),
        P("seq"),
    )
    return jax.shard_map(body, mesh=mesh, in_specs=in_specs, out_specs=out_specs, check_vma=False)
```

```python
import functools

import jax
import jax.numpy as jnp
from jax import lax
from jax.experimental import pallas as pl
from jax.experimental.pallas import tpu as pltpu
from jax.sharding import PartitionSpec as P

HEADS = 16


masked_fill = -1e30
norm_epsilon = 1e-05


def layer_norm(rows, gain, shift):
    centre = jnp.mean(rows, -1, keepdims=True)
    centred = rows - centre
    spread = jnp.mean(centred * centred, -1, keepdims=True)
    return centred * lax.rsqrt(spread + norm_epsilon) * gain + shift


def gelu_exact(values):
    return jax.nn.gelu(values, approximate=False)


def project(rows, weight):
    return jnp.dot(rows, weight, preferred_element_type=jnp.float32)


def project_back(grads, weight):
    return jnp.einsum("re,de->rd", grads, weight, preferred_element_type=jnp.float32)


def outer_sum(rows, grads):
    return jnp.einsum("rd,re->de", rows, grads, preferred_element_type=jnp.float32)


def by_heads(array):
    return array.reshape(array.shape[0], HEADS, -1)


def head_scale(width):
    return (width // HEADS) ** (-0.5)


def score_block(queries, keys):
    scores = jnp.einsum(
        "qhd,khd->hqk", by_heads(queries), by_heads(keys), preferred_element_type=jnp.float32
    )
    return scores * head_scale(queries.shape[-1])


def allowed_keys(query_rows, key_rows, length, causal):
    allowed = key_rows[None, :] < length
    if causal:
        allowed = allowed & (key_rows[None, :] <= query_rows[:, None])
    return allowed


def table_of(array, table):
    return lax.dynamic_index_in_dim(array, table, 1, keepdims=False)


def gather_pair(keys, values):
    return (
        lax.all_gather(keys, "seq", axis=0, tiled=True),
        lax.all_gather(values, "seq", axis=0, tiled=True),
    )


def gather_rows(rows):
    return lax.all_gather(rows, "seq", axis=0, tiled=True)


def sum_rows(terms, count):
    return lax.psum_scatter(
        terms(jnp.int32(0), count * lax.axis_size("seq")).astype(jnp.bfloat16),
        "seq",
        scatter_dimension=0,
        tiled=True,
    ).astype(jnp.float32)


def projections(from_rows, to_rows, w_query, w_key, w_value):
    qlen, tables, width = from_rows.shape
    klen = to_rows.shape[0]
    to_flat = to_rows.reshape(-1, width)
    queries = (
        project(from_rows.reshape(-1, width), w_query)
        .astype(jnp.bfloat16)
        .reshape(qlen, tables, width)
    )
    keys = project(to_flat, w_key).astype(jnp.bfloat16).reshape(klen, tables, width)
    values = project(to_flat, w_value).astype(jnp.bfloat16).reshape(klen, tables, width)
    return (queries, keys, values)


def finish_grads(from_rows, to_rows, w_query, w_key, w_value, d_queries, d_keys, d_values):
    width = from_rows.shape[-1]
    from_flat = from_rows.reshape(-1, width)
    to_flat = to_rows.reshape(-1, width)
    query_low = d_queries.astype(jnp.bfloat16).reshape(-1, width)
    key_low = d_keys.astype(jnp.bfloat16).reshape(-1, width)
    value_low = d_values.astype(jnp.bfloat16).reshape(-1, width)
    grad_query = outer_sum(from_flat, query_low)
    grad_key = outer_sum(to_flat, key_low)
    grad_value = outer_sum(to_flat, value_low)
    d_from = project_back(query_low, w_query)
    d_to = project_back(key_low, w_key) + project_back(value_low, w_value)
    return (d_from, d_to, grad_query, grad_key, grad_value)


def attend_forward(from_rows, to_rows, w_query, w_key, w_value, lengths, causal):
    qlen, tables, width = from_rows.shape
    queries, keys, values = projections(from_rows, to_rows, w_query, w_key, w_value)
    gathered = gather_pair(keys, values)
    all_keys, all_values = gathered
    query_rows = lax.axis_index("seq") * qlen + jnp.arange(qlen)
    key_rows = jnp.arange(all_keys.shape[0])

    def one_table(table):
        scores = score_block(table_of(queries, table), table_of(all_keys, table))
        allowed = allowed_keys(query_rows, key_rows, lengths[table], causal)
        scores = jnp.where(allowed[None], scores, masked_fill)
        top = jnp.max(scores, -1)
        weights = jnp.exp(scores - top[..., None])
        total = jnp.sum(weights, -1)
        probs = (weights / total[..., None]).astype(jnp.bfloat16)
        context = jnp.einsum(
            "hqk,khd->qhd",
            probs,
            by_heads(table_of(all_values, table)),
            preferred_element_type=jnp.float32,
        )
        return (context.reshape(qlen, width), top + jnp.log(total))

    context, logsum = lax.map(one_table, jnp.arange(tables))
    return (queries, keys, values, gathered, jnp.swapaxes(context, 0, 1), logsum)


def key_value_terms(
    query_part,
    grads_part,
    logsum_part,
    delta_part,
    key_part,
    value_part,
    query_rows,
    part_rows,
    length,
    causal,
    scale,
):
    scores = score_block(query_part, key_part)
    allowed = allowed_keys(query_rows, part_rows, length, causal)
    probs = jnp.where(allowed[None], jnp.exp(scores - logsum_part[..., None]), 0.0)
    grads_here = by_heads(grads_part)
    d_values = jnp.einsum(
        "hqk,qhd->khd", probs.astype(jnp.bfloat16), grads_here, preferred_element_type=jnp.float32
    )
    d_probs = jnp.einsum(
        "qhd,khd->hqk", grads_here, by_heads(value_part), preferred_element_type=jnp.float32
    )
    d_scores = (probs * (d_probs - delta_part.T[..., None])).astype(jnp.bfloat16)
    d_keys = (
        jnp.einsum(
            "hqk,qhd->khd", d_scores, by_heads(query_part), preferred_element_type=jnp.float32
        )
        * scale
    )
    count = key_part.shape[0]
    width = key_part.shape[-1]
    return jnp.concatenate([d_keys.reshape(count, width), d_values.reshape(count, width)], -1)


def attend_backward(state, from_rows, to_rows, w_query, w_key, w_value, lengths, causal, d_context):
    queries, keys, values, gathered, context, logsum = state
    qlen, tables, width = queries.shape
    klen = keys.shape[0]
    all_keys, all_values = gather_pair(keys, values)
    scale = head_scale(width)
    d_low = d_context.reshape(qlen, tables, width).astype(jnp.bfloat16)
    delta = jnp.sum((d_low.astype(jnp.float32) * context).reshape(qlen, tables, HEADS, -1), -1)
    query_rows = lax.axis_index("seq") * qlen + jnp.arange(qlen)
    key_rows = jnp.arange(all_keys.shape[0])

    def query_table(table):
        scores = score_block(table_of(queries, table), table_of(all_keys, table))
        allowed = allowed_keys(query_rows, key_rows, lengths[table], causal)
        probs = jnp.where(allowed[None], jnp.exp(scores - logsum[table][..., None]), 0.0)
        d_probs = jnp.einsum(
            "qhd,khd->hqk",
            by_heads(table_of(d_low, table)),
            by_heads(table_of(all_values, table)),
            preferred_element_type=jnp.float32,
        )
        d_scores = (probs * (d_probs - delta[:, table].T[..., None])).astype(jnp.bfloat16)
        d_query = jnp.einsum(
            "hqk,khd->qhd",
            d_scores,
            by_heads(table_of(all_keys, table)),
            preferred_element_type=jnp.float32,
        )
        return (d_query * scale).reshape(qlen, width)

    d_queries = jnp.swapaxes(lax.map(query_table, jnp.arange(tables)), 0, 1)
    part_rows = jnp.arange(klen * lax.axis_size("seq"))

    def key_table(table, terms):
        piece = key_value_terms(
            table_of(queries, table),
            table_of(d_low, table),
            logsum[table],
            delta[:, table],
            table_of(all_keys, table),
            table_of(all_values, table),
            query_rows,
            part_rows,
            lengths[table],
            causal,
            scale,
        )
        return lax.dynamic_update_index_in_dim(terms, piece, table, 1)

    summed = lax.psum_scatter(
        lax.fori_loop(
            0,
            tables,
            key_table,
            jnp.zeros((klen * lax.axis_size("seq"), tables, 2 * width), jnp.float32),
        ).astype(jnp.bfloat16),
        "seq",
        scatter_dimension=0,
        tiled=True,
    ).astype(jnp.float32)
    return finish_grads(
        from_rows,
        to_rows,
        w_query,
        w_key,
        w_value,
        d_queries,
        summed[..., :width],
        summed[..., width:],
    )


def token_forward(rows, w_expand, w_contract):
    all_rows = gather_rows(rows)
    acts = gelu_exact(project(all_rows, w_expand)).astype(jnp.bfloat16)

    def contract_terms(start, count):
        return project(acts, w_contract)

    return (sum_rows(contract_terms, rows.shape[0]), all_rows)


def token_backward(all_rows, d_out, w_expand, w_contract):
    all_grads = gather_rows(d_out.astype(jnp.bfloat16))
    acts, gelu_back = jax.vjp(gelu_exact, project(all_rows, w_expand))
    d_hidden = gelu_back(project_back(all_grads, w_contract))[0].astype(jnp.bfloat16)
    grad_expand = outer_sum(all_rows, d_hidden)
    grad_contract = outer_sum(acts.astype(jnp.bfloat16), all_grads)

    def expand_terms(start, count):
        return project_back(d_hidden, w_expand)

    return (sum_rows(expand_terms, d_out.shape[0]), grad_expand, grad_contract)


def general_body(
    source_tokens,
    target_tokens,
    source_lengths,
    target_lengths,
    encoder_query,
    encoder_key,
    encoder_value,
    encoder_mix,
    attend_gain,
    attend_shift,
    encoder_expand,
    encoder_contract,
    encoder_gain,
    encoder_shift,
    decoder_query,
    decoder_key,
    decoder_value,
    decoder_mix,
    self_gain,
    self_shift,
    cross_query,
    cross_key,
    cross_value,
    cross_mix,
    cross_gain,
    cross_shift,
    decoder_expand,
    decoder_contract,
    decoder_gain,
    decoder_shift,
    source_cotangent,
    target_cotangent,
):
    slots, tables, width = source_tokens.shape
    places = target_tokens.shape[0]
    source_flat = source_tokens.reshape(-1, width)
    target_flat = target_tokens.reshape(-1, width)
    encoder_state = attend_forward(
        source_tokens,
        source_tokens,
        encoder_query,
        encoder_key,
        encoder_value,
        source_lengths,
        False,
    )
    encoder_context = encoder_state[4].reshape(-1, width).astype(jnp.bfloat16)
    first, first_back = jax.vjp(
        layer_norm,
        source_flat.astype(jnp.float32) + project(encoder_context, encoder_mix),
        attend_gain,
        attend_shift,
    )
    first_low = first.astype(jnp.bfloat16)
    widened, encoder_kept = token_forward(first_low, encoder_expand, encoder_contract)
    second, second_back = jax.vjp(layer_norm, first + widened, encoder_gain, encoder_shift)
    encoded = second.astype(jnp.bfloat16).reshape(slots, tables, width)
    decoder_state = attend_forward(
        target_tokens,
        target_tokens,
        decoder_query,
        decoder_key,
        decoder_value,
        target_lengths,
        True,
    )
    decoder_context = decoder_state[4].reshape(-1, width).astype(jnp.bfloat16)
    third, third_back = jax.vjp(
        layer_norm,
        target_flat.astype(jnp.float32) + project(decoder_context, decoder_mix),
        self_gain,
        self_shift,
    )
    third_blocks = third.astype(jnp.bfloat16).reshape(places, tables, width)
    cross_state = attend_forward(
        third_blocks, encoded, cross_query, cross_key, cross_value, source_lengths, False
    )
    cross_context = cross_state[4].reshape(-1, width).astype(jnp.bfloat16)
    fourth, fourth_back = jax.vjp(
        layer_norm, third + project(cross_context, cross_mix), cross_gain, cross_shift
    )
    fourth_low = fourth.astype(jnp.bfloat16)
    narrowed, decoder_kept = token_forward(fourth_low, decoder_expand, decoder_contract)
    fifth, fifth_back = jax.vjp(layer_norm, fourth + narrowed, decoder_gain, decoder_shift)
    decoded = fifth.astype(jnp.bfloat16).reshape(places, tables, width)
    d_fifth, grad_decoder_gain, grad_decoder_shift = fifth_back(
        target_cotangent.reshape(-1, width).astype(jnp.float32)
    )
    d_rows, grad_decoder_expand, grad_decoder_contract = token_backward(
        decoder_kept, d_fifth, decoder_expand, decoder_contract
    )
    d_fourth, grad_cross_gain, grad_cross_shift = fourth_back(d_fifth + d_rows)
    cross_low = d_fourth.astype(jnp.bfloat16)
    grad_cross_mix = outer_sum(cross_context, cross_low)
    d_cross_context = project_back(cross_low, cross_mix)
    d_third_cross, d_encoded, grad_cross_query, grad_cross_key, grad_cross_value = attend_backward(
        cross_state,
        third_blocks,
        encoded,
        cross_query,
        cross_key,
        cross_value,
        source_lengths,
        False,
        d_cross_context,
    )
    d_third, grad_self_gain, grad_self_shift = third_back(d_fourth + d_third_cross)
    self_low = d_third.astype(jnp.bfloat16)
    grad_decoder_mix = outer_sum(decoder_context, self_low)
    d_from, d_to, grad_decoder_query, grad_decoder_key, grad_decoder_value = attend_backward(
        decoder_state,
        target_tokens,
        target_tokens,
        decoder_query,
        decoder_key,
        decoder_value,
        target_lengths,
        True,
        project_back(self_low, decoder_mix),
    )
    grad_target = (d_third + d_from + d_to).reshape(places, tables, width)
    d_second, grad_encoder_gain, grad_encoder_shift = second_back(
        source_cotangent.reshape(-1, width).astype(jnp.float32) + d_encoded
    )
    d_rows, grad_encoder_expand, grad_encoder_contract = token_backward(
        encoder_kept, d_second, encoder_expand, encoder_contract
    )
    d_first, grad_attend_gain, grad_attend_shift = first_back(d_second + d_rows)
    encoder_low = d_first.astype(jnp.bfloat16)
    grad_encoder_mix = outer_sum(encoder_context, encoder_low)
    d_from, d_to, grad_encoder_query, grad_encoder_key, grad_encoder_value = attend_backward(
        encoder_state,
        source_tokens,
        source_tokens,
        encoder_query,
        encoder_key,
        encoder_value,
        source_lengths,
        False,
        project_back(encoder_low, encoder_mix),
    )
    grad_source = (d_first + d_from + d_to).reshape(slots, tables, width)
    shards = (
        lax.psum_scatter(
            grad_encoder_query.astype(jnp.bfloat16), "seq", scatter_dimension=0, tiled=True
        ).astype(jnp.float32),
        lax.psum_scatter(
            grad_encoder_key.astype(jnp.bfloat16), "seq", scatter_dimension=0, tiled=True
        ).astype(jnp.float32),
        lax.psum_scatter(
            grad_encoder_value.astype(jnp.bfloat16), "seq", scatter_dimension=0, tiled=True
        ).astype(jnp.float32),
        lax.psum_scatter(
            grad_encoder_mix.astype(jnp.bfloat16), "seq", scatter_dimension=0, tiled=True
        ).astype(jnp.float32),
        lax.psum_scatter(
            grad_decoder_query.astype(jnp.bfloat16), "seq", scatter_dimension=0, tiled=True
        ).astype(jnp.float32),
        lax.psum_scatter(
            grad_decoder_key.astype(jnp.bfloat16), "seq", scatter_dimension=0, tiled=True
        ).astype(jnp.float32),
        lax.psum_scatter(
            grad_decoder_value.astype(jnp.bfloat16), "seq", scatter_dimension=0, tiled=True
        ).astype(jnp.float32),
        lax.psum_scatter(
            grad_decoder_mix.astype(jnp.bfloat16), "seq", scatter_dimension=0, tiled=True
        ).astype(jnp.float32),
        lax.psum_scatter(
            grad_cross_query.astype(jnp.bfloat16), "seq", scatter_dimension=0, tiled=True
        ).astype(jnp.float32),
        lax.psum_scatter(
            grad_cross_key.astype(jnp.bfloat16), "seq", scatter_dimension=0, tiled=True
        ).astype(jnp.float32),
        lax.psum_scatter(
            grad_cross_value.astype(jnp.bfloat16), "seq", scatter_dimension=0, tiled=True
        ).astype(jnp.float32),
        lax.psum_scatter(
            grad_cross_mix.astype(jnp.bfloat16), "seq", scatter_dimension=0, tiled=True
        ).astype(jnp.float32),
        lax.psum_scatter(
            grad_attend_gain.astype(jnp.bfloat16), "seq", scatter_dimension=0, tiled=True
        ).astype(jnp.float32),
        lax.psum_scatter(
            grad_attend_shift.astype(jnp.bfloat16), "seq", scatter_dimension=0, tiled=True
        ).astype(jnp.float32),
        lax.psum_scatter(
            grad_encoder_gain.astype(jnp.bfloat16), "seq", scatter_dimension=0, tiled=True
        ).astype(jnp.float32),
        lax.psum_scatter(
            grad_encoder_shift.astype(jnp.bfloat16), "seq", scatter_dimension=0, tiled=True
        ).astype(jnp.float32),
        lax.psum_scatter(
            grad_self_gain.astype(jnp.bfloat16), "seq", scatter_dimension=0, tiled=True
        ).astype(jnp.float32),
        lax.psum_scatter(
            grad_self_shift.astype(jnp.bfloat16), "seq", scatter_dimension=0, tiled=True
        ).astype(jnp.float32),
        lax.psum_scatter(
            grad_cross_gain.astype(jnp.bfloat16), "seq", scatter_dimension=0, tiled=True
        ).astype(jnp.float32),
        lax.psum_scatter(
            grad_cross_shift.astype(jnp.bfloat16), "seq", scatter_dimension=0, tiled=True
        ).astype(jnp.float32),
        lax.psum_scatter(
            grad_decoder_gain.astype(jnp.bfloat16), "seq", scatter_dimension=0, tiled=True
        ).astype(jnp.float32),
        lax.psum_scatter(
            grad_decoder_shift.astype(jnp.bfloat16), "seq", scatter_dimension=0, tiled=True
        ).astype(jnp.float32),
    )
    totals = (
        lax.psum(shards[0].astype(jnp.bfloat16), "dp").astype(jnp.float32),
        lax.psum(shards[1].astype(jnp.bfloat16), "dp").astype(jnp.float32),
        lax.psum(shards[2].astype(jnp.bfloat16), "dp").astype(jnp.float32),
        lax.psum(shards[3].astype(jnp.bfloat16), "dp").astype(jnp.float32),
        lax.psum(shards[4].astype(jnp.bfloat16), "dp").astype(jnp.float32),
        lax.psum(shards[5].astype(jnp.bfloat16), "dp").astype(jnp.float32),
        lax.psum(shards[6].astype(jnp.bfloat16), "dp").astype(jnp.float32),
        lax.psum(shards[7].astype(jnp.bfloat16), "dp").astype(jnp.float32),
        lax.psum(shards[8].astype(jnp.bfloat16), "dp").astype(jnp.float32),
        lax.psum(shards[9].astype(jnp.bfloat16), "dp").astype(jnp.float32),
        lax.psum(shards[10].astype(jnp.bfloat16), "dp").astype(jnp.float32),
        lax.psum(shards[11].astype(jnp.bfloat16), "dp").astype(jnp.float32),
        lax.psum(shards[12].astype(jnp.bfloat16), "dp").astype(jnp.float32),
        lax.psum(shards[13].astype(jnp.bfloat16), "dp").astype(jnp.float32),
        lax.psum(shards[14].astype(jnp.bfloat16), "dp").astype(jnp.float32),
        lax.psum(shards[15].astype(jnp.bfloat16), "dp").astype(jnp.float32),
        lax.psum(shards[16].astype(jnp.bfloat16), "dp").astype(jnp.float32),
        lax.psum(shards[17].astype(jnp.bfloat16), "dp").astype(jnp.float32),
        lax.psum(shards[18].astype(jnp.bfloat16), "dp").astype(jnp.float32),
        lax.psum(shards[19].astype(jnp.bfloat16), "dp").astype(jnp.float32),
        lax.psum(shards[20].astype(jnp.bfloat16), "dp").astype(jnp.float32),
        lax.psum(shards[21].astype(jnp.bfloat16), "dp").astype(jnp.float32),
        lax.psum(grad_encoder_expand.astype(jnp.bfloat16), "dp").astype(jnp.float32),
        lax.psum(grad_encoder_contract.astype(jnp.bfloat16), "dp").astype(jnp.float32),
        lax.psum(grad_decoder_expand.astype(jnp.bfloat16), "dp").astype(jnp.float32),
        lax.psum(grad_decoder_contract.astype(jnp.bfloat16), "dp").astype(jnp.float32),
    )
    return (
        encoded,
        decoded,
        grad_source,
        grad_target,
        totals[0],
        totals[1],
        totals[2],
        totals[3],
        totals[12],
        totals[13],
        totals[22],
        totals[23],
        totals[14],
        totals[15],
        totals[4],
        totals[5],
        totals[6],
        totals[7],
        totals[16],
        totals[17],
        totals[8],
        totals[9],
        totals[10],
        totals[11],
        totals[18],
        totals[19],
        totals[24],
        totals[25],
        totals[20],
        totals[21],
    )


MESH = pl.DeviceIdType.MESH
PEERS = (6, 7, 2, 3, 4, 5, 1)
low = jnp.bfloat16
wide = jnp.float32
VMEM_BYTES = 60 * 2**20


def fits_plane(mesh):
    return mesh.shape["seq"] == 8


def add_low(left, right):
    return (left.astype(wide) + right.astype(wide)).astype(low)


def nt(left, right):
    return lax.dot_general(left, right, (((1,), (1,)), ((), ())), preferred_element_type=wide)


def nn(left, right):
    return lax.dot_general(left, right, (((1,), (0,)), ((), ())), preferred_element_type=wide)


def tn(left, right):
    return lax.dot_general(left, right, (((0,), (0,)), ((), ())), preferred_element_type=wide)


def lane_head(shape, size):
    return lax.broadcasted_iota(jnp.int32, shape, len(shape) - 1) // size


def vmem_spec():
    return pl.BlockSpec(memory_space=pltpu.VMEM)


def any_spec():
    return pl.BlockSpec(memory_space=pl.ANY)


def greet(masks, size=0):
    me = lax.axis_index("seq")
    barrier = pltpu.get_barrier_semaphore()
    for mask in masks:
        pl.semaphore_signal(barrier, inc=1, device_id={"seq": me ^ mask}, device_id_type=MESH)
    if not size:
        pl.semaphore_wait(barrier, len(masks))
        return
    place = lax.axis_index("dp")
    inner = (place > 0) & (place < size - 1)

    @pl.when(place > 0)
    def _():
        pl.semaphore_signal(barrier, inc=1, device_id={"dp": place - 1}, device_id_type=MESH)

    @pl.when(place < size - 1)
    def _():
        pl.semaphore_signal(barrier, inc=1, device_id={"dp": place + 1}, device_id_type=MESH)

    @pl.when(inner)
    def _():
        pl.semaphore_wait(barrier, len(masks) + 2)

    @pl.when(jnp.logical_not(inner))
    def _():
        pl.semaphore_wait(barrier, len(masks) + 1)


class Line:
    lag = 2

    def __init__(self, size, chunks, mine, came, sent, send, recv):
        place = lax.axis_index("dp")
        self.chunks, self.mine, self.came, self.sent, self.send, self.recv = chunks, mine, came, sent, send, recv
        self.count = mine.shape[0] // chunks
        self.has = (place > 0, place < size - 1)
        self.neighbour = (place - 1, place + 1)
        self.lower = place < size // 2
        self.steps = chunks + self.lag

    def copy(self, side, chunk, first=False):
        part = pl.ds(chunk * self.count, self.count)
        return pltpu.make_async_remote_copy(
            src_ref=self.mine.at[part] if first else self.sent.at[side, part],
            dst_ref=self.came.at[side, part],
            send_sem=self.send.at[side, chunk],
            recv_sem=self.recv.at[side, chunk],
            device_id={"dp": self.neighbour[1 - side]},
            device_id_type=MESH,
        )

    def begin(self):
        for side in range(2):

            @pl.when(jnp.logical_not(self.has[side]))
            def _(side=side):
                for chunk in range(self.chunks):
                    self.copy(side, chunk, True).start()
                self.came[side] = jnp.zeros(self.mine.shape, low)

    def forward(self, side, chunk):
        part = pl.ds(chunk * self.count, self.count)

        @pl.when(self.has[side])
        def _():
            self.copy(side, chunk).wait_recv()

            @pl.when(self.has[1 - side])
            def _():
                self.sent[side, part] = add_low(self.mine[part], self.came[side, part])
                self.copy(side, chunk).start()

    def step(self, number):
        if number >= self.steps:
            return
        for near in range(2):

            @pl.when(self.lower if near == 0 else jnp.logical_not(self.lower))
            def _(near=near):
                if number < self.chunks:
                    self.forward(near, number)
                if number >= self.lag:
                    self.forward(1 - near, number - self.lag)

    def rest(self, first):
        for number in range(first, self.steps):
            self.step(number)

    def total(self, part=slice(None)):
        return self.mine[part].astype(wide) + self.came[0, part].astype(wide) + self.came[1, part].astype(wide)

    def end(self):
        for side in range(2):

            @pl.when(self.has[1 - side])
            def _(side=side):
                for chunk in range(self.chunks):
                    self.copy(side, chunk).wait_send()


def line_scratch(shape, chunks):
    return [
        pltpu.VMEM((2,) + shape, low),
        pltpu.VMEM((2,) + shape, low),
        pltpu.SemaphoreType.DMA((2, chunks)),
        pltpu.SemaphoreType.DMA((2, chunks)),
    ]


def remote(src, dst, send, recv, to):
    return pltpu.make_async_remote_copy(
        src_ref=src, dst_ref=dst, send_sem=send, recv_sem=recv, device_id={"seq": to}, device_id_type=MESH
    )


def params(collective_id):
    return pltpu.CompilerParams(
        collective_id=collective_id, has_side_effects=True, vmem_limit_bytes=VMEM_BYTES
    )


def gather_table_kernel(rows, extra, out, out_extra, send, recv, keep):
    me = lax.axis_index("seq")
    mine = me // 4
    greet((1, 2, 4, 6))
    own = [
        pltpu.make_async_copy(rows.at[mine], out.at[me], keep.at[0]),
        pltpu.make_async_copy(extra, out_extra.at[me], keep.at[1]),
    ]
    for copy in own:
        copy.start()
    started = []
    both = ((0, lambda table: rows.at[table], out), (1, lambda table: extra, out_extra))
    for slot, mask, table in ((0, 6, 1 - mine), (1, 2, mine), (2, 4, 1 - mine), (3, 1, mine)):
        for kind, source, place in both:
            copy = remote(source(table), place.at[me], send.at[kind, slot], recv.at[kind, slot], me ^ mask)
            copy.start()
            started.append(copy)
    for slot, mask in ((1, 2), (2, 4), (0, 6)):
        owner = me ^ mask
        for kind, source, place in both:
            remote(source(0), place.at[owner], send.at[kind, slot], recv.at[kind, slot], me ^ 1).wait_recv()
            copy = remote(
                place.at[owner], place.at[owner], send.at[kind, 4 + slot], recv.at[kind, 4 + slot], me ^ 1
            )
            copy.start()
            started.append(copy)
    for kind, source, place in both:
        remote(source(0), place.at[me ^ 1], send.at[kind, 3], recv.at[kind, 3], me ^ 1).wait_recv()
        for slot, mask in ((1, 2), (2, 4), (0, 6)):
            remote(
                source(0), place.at[me ^ mask ^ 1], send.at[kind, 4 + slot], recv.at[kind, 4 + slot], me ^ 1
            ).wait_recv()
    for copy in started:
        copy.wait_send()
    for copy in own:
        copy.wait()


def gather_table(rows, extra):
    return pl.pallas_call(
        gather_table_kernel,
        out_shape=(
            jax.ShapeDtypeStruct((8,) + rows.shape[1:], rows.dtype),
            jax.ShapeDtypeStruct((8,) + extra.shape, extra.dtype),
        ),
        in_specs=[any_spec()] * 2,
        out_specs=(any_spec(), any_spec()),
        scratch_shapes=[
            pltpu.SemaphoreType.DMA((2, 7)),
            pltpu.SemaphoreType.DMA((2, 7)),
            pltpu.SemaphoreType.DMA((2,)),
        ],
        compiler_params=params(1),
    )(rows, extra)


def scatter_plane_kernel(terms, out, sib, pair, came, far, came_far, send, recv, send_pair, recv_pair, send_far, recv_far):
    me = lax.axis_index("seq")
    half = out.shape[0] // 2
    greet((1, 2, 4))
    halves = (pl.ds(0, half), pl.ds(half, half))
    started = []
    chips = (6, 2, 4, 0)
    for slot, mask in enumerate(chips):
        copy = remote(terms.at[me ^ 1 ^ mask], sib.at[slot], send.at[slot], recv.at[slot], me ^ 1)
        copy.start()
        started.append(copy)

    def pair_copy(slot):
        return remote(
            pair.at[slot], came.at[slot], send_pair.at[slot], recv_pair.at[slot], me ^ (2, 4, 2, 4)[slot]
        )

    def far_copy(slot):
        return remote(far.at[slot], came_far.at[slot], send_far.at[slot], recv_far.at[slot], me ^ (4, 2)[slot])

    def both(mask, slot, rows):
        return terms[me ^ mask, rows].astype(wide) + sib[slot, rows].astype(wide)

    for slot, mask in enumerate(chips):
        remote(terms.at[0], sib.at[slot], send.at[slot], recv.at[slot], me ^ 1).wait_recv()
        if mask == 6:
            for side in range(2):
                pair[side] = both(6, 0, halves[side]).astype(low)
                pair_copy(side).start()
        if mask == 2:
            pair[2] = both(2, 1, halves[0]).astype(low)
            pair_copy(2).start()
        if mask == 4:
            pair[3] = both(4, 2, halves[1]).astype(low)
            pair_copy(3).start()
    for side in range(2):
        pair_copy(side).wait_recv()
        mask, slot = ((4, 2), (2, 1))[side]
        far[side] = (both(mask, slot, halves[side]) + came[side].astype(wide)).astype(low)
        far_copy(side).start()
    for side in range(2):
        pair_copy(2 + side).wait_recv()
        out[halves[side]] = both(0, 3, halves[side]) + came[2 + side].astype(wide)
    for side in range(2):
        far_copy(side).wait_recv()
        out[halves[side]] += came_far[side].astype(wide)
    for copy in started:
        copy.wait_send()
    for slot in range(4):
        pair_copy(slot).wait_send()
    for side in range(2):
        far_copy(side).wait_send()


def scatter_plane(terms):
    _, rows, width = terms.shape
    return pl.pallas_call(
        scatter_plane_kernel,
        out_shape=jax.ShapeDtypeStruct((rows, width), wide),
        in_specs=[vmem_spec()],
        out_specs=vmem_spec(),
        scratch_shapes=[
            pltpu.VMEM((4, rows, width), low),
            pltpu.VMEM((4, rows // 2, width), low),
            pltpu.VMEM((4, rows // 2, width), low),
            pltpu.VMEM((2, rows // 2, width), low),
            pltpu.VMEM((2, rows // 2, width), low),
        ]
        + [pltpu.SemaphoreType.DMA((4,))] * 4
        + [pltpu.SemaphoreType.DMA((2,))] * 2,
        compiler_params=params(9),
    )(terms)


def heads_to_rows_kernel(blocks, out, send, recv, keep):
    me = lax.axis_index("seq")
    width = blocks.shape[2]
    greet(PEERS)

    def place(owner):
        return out.at[owner // 4, :, pl.ds(pl.multiple_of((owner % 4) * width, width), width)]

    local = pltpu.make_async_copy(blocks.at[me], place(me), keep)
    local.start()
    started = []
    for mask in PEERS:
        copy = remote(blocks.at[me ^ mask], place(me), send.at[mask], recv.at[mask], me ^ mask)
        copy.start()
        started.append(copy)
    for mask in PEERS:
        remote(blocks.at[0], place(me ^ mask), send.at[mask], recv.at[mask], me ^ mask).wait_recv()
    for copy in started:
        copy.wait_send()
    local.wait()


def heads_to_rows(blocks):
    _, rows, width = blocks.shape
    return pl.pallas_call(
        heads_to_rows_kernel,
        out_shape=jax.ShapeDtypeStruct((2, rows, 4 * width), blocks.dtype),
        in_specs=[any_spec()],
        out_specs=any_spec(),
        scratch_shapes=[
            pltpu.SemaphoreType.DMA((8,)),
            pltpu.SemaphoreType.DMA((8,)),
            pltpu.SemaphoreType.DMA,
        ],
        compiler_params=params(2),
    )(blocks)


def rows_to_heads_kernel(rows, out, send, recv, keep):
    me = lax.axis_index("seq")
    width = out.shape[2]
    greet(PEERS)

    def part(owner):
        return rows.at[owner // 4, :, pl.ds(pl.multiple_of((owner % 4) * width, width), width)]

    local = pltpu.make_async_copy(part(me), out.at[me], keep)
    local.start()
    started = []
    for mask in PEERS:
        copy = remote(part(me ^ mask), out.at[me], send.at[mask], recv.at[mask], me ^ mask)
        copy.start()
        started.append(copy)
    for mask in PEERS:
        remote(part(me), out.at[me ^ mask], send.at[mask], recv.at[mask], me ^ mask).wait_recv()
    for copy in started:
        copy.wait_send()
    local.wait()


def rows_to_heads(rows):
    _, count, width = rows.shape
    return pl.pallas_call(
        rows_to_heads_kernel,
        out_shape=jax.ShapeDtypeStruct((8, count, width // 4), rows.dtype),
        in_specs=[any_spec()],
        out_specs=any_spec(),
        scratch_shapes=[
            pltpu.SemaphoreType.DMA((8,)),
            pltpu.SemaphoreType.DMA((8,)),
            pltpu.SemaphoreType.DMA,
        ],
        compiler_params=params(3),
    )(rows)


def sum_small_kernel(terms, earlier, out, mine, came, send, recv, send_back, recv_back):
    me = lax.axis_index("seq")
    greet(PEERS)
    mine[...] = terms[...].astype(low)
    started = []
    for mask in PEERS:
        copy = remote(mine.at[me ^ mask], came.at[mask], send.at[mask], recv.at[mask], me ^ mask)
        copy.start()
        started.append(copy)
    total = terms[me].astype(wide)
    for mask in PEERS:
        remote(mine.at[0], came.at[mask], send.at[mask], recv.at[mask], me ^ mask).wait_recv()
        total = total + came[mask].astype(wide)
    out[me] = total.astype(low)
    for mask in PEERS:
        copy = remote(out.at[me], out.at[me], send_back.at[mask], recv_back.at[mask], me ^ mask)
        copy.start()
        started.append(copy)
    for mask in PEERS:
        remote(mine.at[0], out.at[me ^ mask], send_back.at[mask], recv_back.at[mask], me ^ mask).wait_recv()
    for copy in started:
        copy.wait_send()


def sum_small(terms, collective_id, earlier=None):
    count, width = terms.shape
    earlier = terms if earlier is None else earlier
    blocks = (8, count // 8, width)
    return pl.pallas_call(
        sum_small_kernel,
        out_shape=jax.ShapeDtypeStruct(blocks, low),
        in_specs=[vmem_spec(), any_spec()],
        out_specs=vmem_spec(),
        scratch_shapes=[pltpu.VMEM(blocks, low), pltpu.VMEM(blocks, low)]
        + [pltpu.SemaphoreType.DMA((8,))] * 4,
        compiler_params=params(collective_id),
    )(terms.reshape(blocks), earlier).reshape(count, width)


def merge_parts_kernel(terms, stats, out, logsum, came, came_stats, send, recv, send_st, recv_st, back, recv_back, back_st, recv_back_st):
    me = lax.axis_index("seq")
    width = out.shape[2]
    greet(PEERS)
    started = []
    for mask in PEERS:
        for src, dst, s, r in ((stats, came_stats, send_st, recv_st), (terms, came, send, recv)):
            copy = remote(src.at[me ^ mask], dst.at[mask], s.at[mask], r.at[mask], me ^ mask)
            copy.start()
            started.append(copy)
    for mask in PEERS:
        remote(stats.at[0], came_stats.at[mask], send_st.at[mask], recv_st.at[mask], me ^ mask).wait_recv()
    tops = [stats[me, 0]] + [came_stats[mask, 0] for mask in PEERS]
    sums = [stats[me, 1]] + [came_stats[mask, 1] for mask in PEERS]
    top = functools.reduce(jnp.maximum, tops)
    weights = [s * jnp.exp(t - top) for t, s in zip(tops, sums)]
    total = functools.reduce(jnp.add, weights)
    logsum[me] = top + jnp.log(total)
    size = width // HEADS
    spread = (
        lax.broadcasted_iota(jnp.int32, (128, width), 1) // size
        == lax.broadcasted_iota(jnp.int32, (128, width), 0)
    ).astype(wide)
    scaled = jnp.concatenate([w / total for w in weights], 0)
    scaled = lax.dot_general(
        scaled, spread, (((1,), (0,)), ((), ())), precision=lax.Precision.HIGHEST, preferred_element_type=wide
    )
    rows = tops[0].shape[0]
    result = scaled[:rows] * terms[me].astype(wide)
    for place, mask in enumerate(PEERS):
        remote(terms.at[0], came.at[mask], send.at[mask], recv.at[mask], me ^ mask).wait_recv()
        result = result + scaled[(place + 1) * rows : (place + 2) * rows] * came[mask].astype(wide)
    out[me] = result.astype(low)
    for mask in PEERS:
        for ref, s, r in ((out, back, recv_back), (logsum, back_st, recv_back_st)):
            copy = remote(ref.at[me], ref.at[me], s.at[mask], r.at[mask], me ^ mask)
            copy.start()
            started.append(copy)
    for mask in PEERS:
        for ref, s, r in ((out, back, recv_back), (logsum, back_st, recv_back_st)):
            remote(ref.at[me], ref.at[me ^ mask], s.at[mask], r.at[mask], me ^ mask).wait_recv()
    for copy in started:
        copy.wait_send()


def merge_parts(terms, tops, sums):
    count, width = terms.shape
    rows = count // 8
    stats = jnp.stack([tops.reshape(8, rows, 128), sums.reshape(8, rows, 128)], 1)
    out, logsum = pl.pallas_call(
        merge_parts_kernel,
        out_shape=(
            jax.ShapeDtypeStruct((8, rows, width), low),
            jax.ShapeDtypeStruct((8, rows, 128), wide),
        ),
        in_specs=[vmem_spec()] * 2,
        out_specs=(vmem_spec(), vmem_spec()),
        scratch_shapes=[pltpu.VMEM((8, rows, width), low), pltpu.VMEM((8, 2, rows, 128), wide)]
        + [pltpu.SemaphoreType.DMA((8,))] * 8,
        compiler_params=params(5),
    )(terms.reshape(8, rows, width), stats)
    return out.reshape(count, width), logsum.reshape(count, 128)


def finish_kernel(
    size, rows, grads, weights, vectors, joined, out, out_line, out_joined,
    terms, sib, pair, came, blocks, came_blocks, line,
    send, recv, send_pair, recv_pair, send_block, recv_block,
    line_came, line_sent, send_line, recv_line, join_came, join_sent, send_join, recv_join,
):
    me = lax.axis_index("seq")
    mine = me // 4
    count = out.shape[1]
    width = grads.shape[1]
    cut = blocks.shape[1] - 16
    quarter = width // 3
    greet(PEERS, size)
    other = Line(size, 4, joined, join_came, join_sent, send_join, recv_join)
    other.begin()
    own = Line(size, 7, line, line_came, line_sent, send_line, recv_line)

    d = grads[...]

    def block_copy(mask):
        return remote(
            blocks.at[me ^ mask], came_blocks.at[mask], send_block.at[mask], recv_block.at[mask], me ^ mask
        )

    for mask in PEERS + (0,):
        owner = me ^ mask
        columns = pl.ds(pl.multiple_of(owner * cut, cut), cut)
        blocks[owner, :cut] = tn(rows[:, columns], d).astype(low)
        blocks[owner, cut:] = vectors[owner]
        if mask:
            block_copy(mask).start()
    for number in range(3):
        other.step(number)
    chips = (6, 2, 4, 0)

    def term(owner):
        return nt(grads[pl.ds(pl.multiple_of(owner * count, count), count)], weights[...])

    def sib_copy(slot):
        return remote(terms.at[slot], sib.at[slot], send.at[slot], recv.at[slot], me ^ 1)

    def pair_copy(slot):
        return remote(pair.at[slot], came.at[slot], send_pair.at[slot], recv_pair.at[slot], me ^ chips[slot])

    for slot, mask in enumerate(chips):
        terms[slot] = term(me ^ 1 ^ mask).astype(low)
        sib_copy(slot).start()
    other.rest(3)
    for slot, mask in enumerate(chips):
        here = term(me ^ mask)
        sib_copy(slot).wait_recv()
        here = here + sib[slot].astype(wide)
        if mask:
            pair[slot] = here.astype(low)
            pair_copy(slot).start()
        else:
            out[mine] = here

    for mask in PEERS:
        block_copy(mask).wait_recv()
    came_blocks[0] = blocks[me]

    def came_from(owner, part):
        return came_blocks[owner ^ me, part].astype(wide)

    total = jnp.zeros((16, width), wide)
    for source in range(4):
        both = came_from(source, pl.ds(0, cut)) + came_from(source + 4, pl.ds(0, cut))
        for kind in range(3):
            line[kind * cut : (kind + 1) * cut, source * quarter : (source + 1) * quarter] = both[
                :, kind * quarter : (kind + 1) * quarter
            ].astype(low)
        total = total + came_from(source, pl.ds(cut, 16)) + came_from(source + 4, pl.ds(cut, 16))
    line[3 * cut :] = jnp.zeros_like(line[3 * cut :])
    line[3 * cut : 3 * cut + 16, :width] = total.astype(low)

    own.begin()
    own.rest(0)
    for slot in (1, 2, 0):
        pair_copy(slot).wait_recv()
    out[mine] += came[1].astype(wide)
    out[1 - mine] = came[2].astype(wide) + came[0].astype(wide)

    out_line[...] = own.total()
    out_joined[...] = other.total()
    for mask in PEERS:
        block_copy(mask).wait_send()
    for slot in range(4):
        sib_copy(slot).wait_send()
    for slot in range(3):
        pair_copy(slot).wait_send()
    own.end()
    other.end()


def finish(rows, grads, weights, vectors, joined):
    width = rows.shape[1]
    count = rows.shape[0] // 8
    cut = width // 8
    line = (3 * cut + 64, width)
    blocks = (8, cut + 16, grads.shape[1])
    four, three = pltpu.SemaphoreType.DMA((4,)), pltpu.SemaphoreType.DMA((3,))
    return pl.pallas_call(
        functools.partial(finish_kernel, lax.axis_size("dp")),
        out_shape=(
            jax.ShapeDtypeStruct((2, count, width), wide),
            jax.ShapeDtypeStruct(line, wide),
            jax.ShapeDtypeStruct(joined.shape, wide),
        ),
        in_specs=[vmem_spec()] * 5,
        out_specs=(vmem_spec(),) * 3,
        scratch_shapes=[
            pltpu.VMEM((4, count, width), low),
            pltpu.VMEM((4, count, width), low),
            pltpu.VMEM((3, count, width), low),
            pltpu.VMEM((3, count, width), low),
            pltpu.VMEM(blocks, low),
            pltpu.VMEM(blocks, low),
            pltpu.VMEM(line, low),
            four,
            four,
            three,
            three,
        ]
        + [pltpu.SemaphoreType.DMA((8,))] * 2
        + line_scratch(line, 7)
        + line_scratch(joined.shape, 4),
        compiler_params=params(6),
    )(rows, grads, weights, vectors, joined)


def plain(**more):
    return pltpu.CompilerParams(vmem_limit_bytes=VMEM_BYTES, **more)


def flash_forward_kernel(length, queries, keys, values, context, logsum):
    rows, width = queries.shape
    count = keys.shape[0]
    heads = width // 64
    of_head = lane_head((1, width), 64)
    q = queries[...] * jnp.asarray(0.125, low)
    k = keys[...]
    v = values[...]
    total = jnp.zeros((rows, width), wide)
    logs = jnp.zeros((rows, 128), wide)
    lanes = lax.broadcasted_iota(jnp.int32, (1, 128), 1)
    fill = jnp.where(lax.broadcasted_iota(jnp.int32, (1, count), 1) < length[0], 0.0, masked_fill)
    for head in range(heads):
        scores = nt(jnp.where(of_head == head, q, jnp.zeros_like(q)), k) + fill
        top = jnp.max(scores, -1, keepdims=True)
        weights = jnp.exp(scores - top)
        summed = jnp.sum(weights, -1, keepdims=True)
        probs = (weights * (1.0 / summed)).astype(low)
        part = nn(probs, v)
        total = jnp.where(of_head == head, part, total)
        logs = jnp.where(lanes == head, top + jnp.log(summed), logs)
    context[...] = total.astype(low)
    logsum[...] = logs


def flash_forward(length, three, block):
    count, width = three.shape[0], three.shape[1] // 3
    return pl.pallas_call(
        flash_forward_kernel,
        out_shape=(
            jax.ShapeDtypeStruct((count, width), low),
            jax.ShapeDtypeStruct((count, 128), wide),
        ),
        grid_spec=pltpu.PrefetchScalarGridSpec(
            num_scalar_prefetch=1,
            grid=(count // block,),
            in_specs=[
                pl.BlockSpec((block, width), lambda i, n: (i, 0)),
                pl.BlockSpec((count, width), lambda i, n: (0, 1)),
                pl.BlockSpec((count, width), lambda i, n: (0, 2)),
            ],
            out_specs=[
                pl.BlockSpec((block, width), lambda i, n: (i, 0)),
                pl.BlockSpec((block, 128), lambda i, n: (i, 0)),
            ],
        ),
        compiler_params=plain(),
    )(length, three, three, three)


def flash_backward_kernel(chunk, length, queries, grads, logsum, delta, keys, keys_t, values, out, q_stack, g_stack, p_stack, s_stack, k_sum, v_sum):
    step = pl.program_id(0)
    rows, width = queries.shape
    count = keys.shape[0]
    heads = width // 64
    of_head = lane_head((1, width), 64)

    @pl.when(step == 0)
    def _():
        k_sum[...] = jnp.zeros_like(k_sum)
        v_sum[...] = jnp.zeros_like(v_sum)

    q = queries[...] * jnp.asarray(0.125, low)
    g = grads[...]
    for head in range(heads):
        place = pl.ds(head * rows, rows)
        q_stack[place] = jnp.where(of_head == head, q, jnp.zeros_like(q))
        g_stack[place] = jnp.where(of_head == head, g, jnp.zeros_like(g))
    dq_sums = [jnp.zeros((64, rows), wide)] * heads
    for start in range(0, count, chunk):
        part = pl.ds(start, chunk)
        k = keys[part]
        v = values[part]
        allowed = start + lax.broadcasted_iota(jnp.int32, (chunk, 1), 0) < length[0]
        fill = jnp.where(allowed, 0.0, masked_fill)
        for head in range(heads):
            place = pl.ds(head * rows, rows)
            scores = nt(k, q_stack[place])
            probs = jnp.exp(scores - logsum[head : head + 1, :] + fill)
            p_stack[:, place] = probs.astype(low)
            d_probs = nt(v, g_stack[place])
            d_scores = (probs * (d_probs - delta[head : head + 1, :])).astype(low)
            s_stack[:, place] = d_scores
            dq_sums[head] = dq_sums[head] + nn(keys_t[head * 64 : head * 64 + 64, part], d_scores)
        v_sum[part] += nn(p_stack[...], g_stack[...])
        k_sum[part] += nn(s_stack[...], q_stack[...])
    dq = jnp.concatenate(dq_sums, 0) * 0.125
    out[pl.ds(pl.multiple_of(step * rows, rows), rows), 0:width] = dq.T.astype(low)

    @pl.when(step == pl.num_programs(0) - 1)
    def _():
        out[:, width : 2 * width] = k_sum[...].astype(low)
        out[:, 2 * width : 3 * width] = v_sum[...].astype(low)


def flash_backward(length, three, grads, logsum, delta, block, chunk):
    count, width = grads.shape
    heads = width // 64
    return pl.pallas_call(
        functools.partial(flash_backward_kernel, chunk),
        out_shape=jax.ShapeDtypeStruct((count, 3 * width), low),
        grid_spec=pltpu.PrefetchScalarGridSpec(
            num_scalar_prefetch=1,
            grid=(count // block,),
            in_specs=[
                pl.BlockSpec((block, width), lambda i, n: (i, 0)),
                pl.BlockSpec((block, width), lambda i, n: (i, 0)),
                pl.BlockSpec((heads, block), lambda i, n: (0, i)),
                pl.BlockSpec((heads, block), lambda i, n: (0, i)),
                pl.BlockSpec((count, width), lambda i, n: (0, 1)),
                pl.BlockSpec((width, count), lambda i, n: (0, 0)),
                pl.BlockSpec((count, width), lambda i, n: (0, 2)),
            ],
            out_specs=pl.BlockSpec((count, 3 * width), lambda i, n: (0, 0)),
            scratch_shapes=[
                pltpu.VMEM((heads * block, width), low),
                pltpu.VMEM((heads * block, width), low),
                pltpu.VMEM((chunk, heads * block), low),
                pltpu.VMEM((chunk, heads * block), low),
                pltpu.VMEM((count, width), wide),
                pltpu.VMEM((count, width), wide),
            ],
        ),
        compiler_params=plain(),
    )(length, three, grads, logsum, delta, three, three[:, width : 2 * width].T, three)


def small_forward_kernel(causal, length, queries, keys, values, context, tops, sums):
    table = pl.program_id(0)
    rows, width = queries.shape
    count = keys.shape[0]
    half = lane_head((1, 128), 64)
    lanes = lax.broadcasted_iota(jnp.int32, (1, 128), 1)
    allowed = lax.broadcasted_iota(jnp.int32, (rows, count), 1) < length[table]
    if causal:
        allowed = allowed & (
            lax.broadcasted_iota(jnp.int32, (rows, count), 1)
            <= lax.broadcasted_iota(jnp.int32, (rows, count), 0)
        )
    top_all = jnp.zeros((rows, 128), wide)
    sum_all = jnp.ones((rows, 128), wide)
    for two in range(width // 128):
        place = pl.ds(two * 128, 128)
        q = queries[:, place] * jnp.asarray(0.125, low)
        k = keys[:, place]
        v = values[:, place]
        total = jnp.zeros((rows, 128), wide)
        for side in range(2):
            scores = nt(jnp.where(half == side, q, jnp.zeros_like(q)), k)
            scores = jnp.where(allowed, scores, masked_fill)
            top = jnp.max(scores, -1, keepdims=True)
            weights = jnp.exp(scores - top)
            summed = jnp.sum(weights, -1, keepdims=True)
            probs = (weights * (1.0 / summed)).astype(low)
            total = jnp.where(half == side, nn(probs, v), total)
            top_all = jnp.where(lanes == 2 * two + side, top, top_all)
            sum_all = jnp.where(lanes == 2 * two + side, summed, sum_all)
        context[:, place] = total.astype(low)
    tops[...] = top_all
    sums[...] = sum_all


def small_forward(length, queries, keys, values, causal):
    tables = length.shape[0]
    rows, width = queries.shape[0] // tables, queries.shape[1]
    count = keys.shape[0] // tables

    def block(size, last):
        return pl.BlockSpec((size, last), lambda t, n: (t, 0))

    return pl.pallas_call(
        functools.partial(small_forward_kernel, causal),
        out_shape=(
            jax.ShapeDtypeStruct(queries.shape, low),
            jax.ShapeDtypeStruct((queries.shape[0], 128), wide),
            jax.ShapeDtypeStruct((queries.shape[0], 128), wide),
        ),
        grid_spec=pltpu.PrefetchScalarGridSpec(
            num_scalar_prefetch=1,
            grid=(tables,),
            in_specs=[block(rows, width), block(count, width), block(count, width)],
            out_specs=[block(rows, width), block(rows, 128), block(rows, 128)],
        ),
        compiler_params=plain(),
    )(length, queries, keys, values)


def small_backward_kernel(causal, length, queries, keys, values, grads, context, logsum, earlier, dq, dk, dv):
    table = pl.program_id(0)
    rows, width = queries.shape
    count = keys.shape[0]
    half = lane_head((1, 128), 64)
    allowed = lax.broadcasted_iota(jnp.int32, (rows, count), 1) < length[table]
    if causal:
        allowed = allowed & (
            lax.broadcasted_iota(jnp.int32, (rows, count), 1)
            <= lax.broadcasted_iota(jnp.int32, (rows, count), 0)
        )
    logs = logsum[...]
    for two in range(width // 128):
        place = pl.ds(two * 128, 128)
        q = queries[:, place] * jnp.asarray(0.125, low)
        k = keys[:, place]
        v = values[:, place]
        g = grads[:, place]
        both = g.astype(wide) * context[:, place].astype(wide)
        dq_here = jnp.zeros((rows, 128), wide)
        dk_here = jnp.zeros((count, 128), wide)
        dv_here = jnp.zeros((count, 128), wide)
        for side in range(2):
            head = 2 * two + side
            q_one = jnp.where(half == side, q, jnp.zeros_like(q))
            g_one = jnp.where(half == side, g, jnp.zeros_like(g))
            delta = jnp.sum(jnp.where(half == side, both, 0.0), -1, keepdims=True)
            scores = nt(q_one, k)
            probs = jnp.where(allowed, jnp.exp(scores - logs[:, head : head + 1]), 0.0)
            d_probs = nt(g_one, v)
            d_scores = (probs * (d_probs - delta)).astype(low)
            dq_here = jnp.where(half == side, nn(d_scores, k), dq_here)
            dk_here = dk_here + tn(d_scores, q_one)
            dv_here = dv_here + tn(probs.astype(low), g_one)
        dq[:, place] = dq_here * 0.125
        dk[:, place] = dk_here.astype(low)
        dv[:, place] = dv_here.astype(low)


def small_backward(length, queries, keys, values, grads, context, logsum, causal, earlier):
    tables = length.shape[0]
    rows, width = queries.shape[0] // tables, queries.shape[1]
    count = keys.shape[0] // tables

    def block(size, last):
        return pl.BlockSpec((size, last), lambda t, n: (t, 0))

    return pl.pallas_call(
        functools.partial(small_backward_kernel, causal),
        out_shape=(
            jax.ShapeDtypeStruct(queries.shape, wide),
            jax.ShapeDtypeStruct(keys.shape, low),
            jax.ShapeDtypeStruct(keys.shape, low),
        ),
        grid_spec=pltpu.PrefetchScalarGridSpec(
            num_scalar_prefetch=1,
            grid=(tables,),
            in_specs=[
                block(rows, width),
                block(count, width),
                block(count, width),
                block(rows, width),
                block(rows, width),
                block(rows, 128),
                any_spec(),
            ],
            out_specs=[block(rows, width), block(count, width), block(count, width)],
        ),
        compiler_params=plain(),
    )(length, queries, keys, values, grads, context, logsum, earlier)


def gelu_parts(values):
    bell = 0.5 * (1.0 + lax.erf(values * 0.7071067811865476))
    slope = bell + values * (0.3989422804014327 * jnp.exp(-0.5 * values * values))
    return values * bell, slope


def feed_forward_kernel(rows, expand, contract, out):
    hidden = nn(rows[...], expand[0])
    act = (hidden * (0.5 * (1.0 + lax.erf(hidden * 0.7071067811865476)))).astype(low)
    term = nn(act, contract[0])

    @pl.when(pl.program_id(0) == 0)
    def _():
        out[...] = term

    @pl.when(pl.program_id(0) > 0)
    def _():
        out[...] += term


def feed_forward(rows, expand, contract):
    count, width = rows.shape
    parts, _, hidden = expand.shape
    return pl.pallas_call(
        feed_forward_kernel,
        out_shape=jax.ShapeDtypeStruct((count, width), wide),
        grid=(parts,),
        in_specs=[
            pl.BlockSpec((count, width), lambda j: (0, 0)),
            pl.BlockSpec((1, width, hidden), lambda j: (j, 0, 0)),
            pl.BlockSpec((1, hidden, width), lambda j: (j, 0, 0)),
        ],
        out_specs=pl.BlockSpec((count, width), lambda j: (0, 0)),
        compiler_params=plain(),
    )(rows, expand, contract)


def outer_kernel(order, earlier, rows, *refs):
    *grads, away, kept = refs
    step = pl.program_id(0)
    half = pl.num_programs(0) // 2
    size = rows.shape[1]
    for place, grad in enumerate(grads):
        term = tn(rows[...], grad[...]).astype(low)

        @pl.when(step < half)
        def _(place=place, term=term):
            away[0, place * size : (place + 1) * size] = term

        @pl.when(step >= half)
        def _(place=place, term=term):
            kept[0, place * size : (place + 1) * size] = term


def outer_by_owner(order, earlier, rows, *grads):
    count, width = rows.shape
    parts = order.shape[0]
    half, size = parts // 2, width // parts
    shape = jax.ShapeDtypeStruct((half, len(grads) * size, width), low)
    return pl.pallas_call(
        outer_kernel,
        out_shape=(shape, shape),
        grid_spec=pltpu.PrefetchScalarGridSpec(
            num_scalar_prefetch=1,
            grid=(parts,),
            in_specs=[any_spec(), pl.BlockSpec((count, size), lambda j, o: (0, o[j]))]
            + [pl.BlockSpec((count, width), lambda j, o: (0, 0))] * len(grads),
            out_specs=[
                pl.BlockSpec((1,) + shape.shape[1:], lambda j, o: (jnp.minimum(j, half - 1), 0, 0)),
                pl.BlockSpec((1,) + shape.shape[1:], lambda j, o: (jnp.maximum(j - half, 0), 0, 0)),
            ],
        ),
        compiler_params=plain(),
    )(order, earlier, rows, *grads)


def widen_kernel(feed, later, earlier, *outs):
    half = outs[1].shape[0]
    outs[0][...] = feed[:half].astype(wide).T
    outs[1][...] = feed[half:].astype(wide)
    start = 0
    for out in outs[2:]:
        out[...] = later[start : start + out.shape[0]].astype(wide)
        start += out.shape[0]


def widen_after(feed, later, heights, earlier):
    width = feed.shape[1]
    half = feed.shape[0] // 2
    shapes = [jax.ShapeDtypeStruct((width, half), wide), jax.ShapeDtypeStruct((half, width), wide)]
    shapes += [jax.ShapeDtypeStruct((height, width), wide) for height in heights]
    return pl.pallas_call(
        widen_kernel,
        out_shape=tuple(shapes),
        in_specs=[vmem_spec()] * 2 + [any_spec()],
        out_specs=tuple(vmem_spec() for _ in shapes),
        compiler_params=plain(),
    )(feed, later, earlier)


def feed_backward_kernel(rows, grads, expand, contract, earlier, out, d_both, expand_sum, contract_sum):
    step = pl.program_id(0)
    x = rows[0]
    g = grads[0]
    act, slope = gelu_parts(nn(x, expand[...]))
    d_hidden = (nt(g, contract[...]) * slope).astype(low)
    out[0] = nt(d_hidden, expand[...]).astype(low)
    one = tn(d_hidden, x)
    two = tn(act.astype(low), g)

    @pl.when(step == 0)
    def _():
        expand_sum[...] = one
        contract_sum[...] = two

    @pl.when(step > 0)
    def _():
        expand_sum[...] += one
        contract_sum[...] += two

    @pl.when(step == pl.num_programs(0) - 1)
    def _():
        d_both[: expand_sum.shape[0]] = expand_sum[...].astype(low)
        d_both[expand_sum.shape[0] :] = contract_sum[...].astype(low)


def feed_backward(rows, grads, expand, contract, earlier):
    parts, count, width = rows.shape
    hidden = contract.shape[0]
    return pl.pallas_call(
        feed_backward_kernel,
        out_shape=(jax.ShapeDtypeStruct(rows.shape, low), jax.ShapeDtypeStruct((2 * hidden, width), low)),
        grid=(parts,),
        in_specs=[
            pl.BlockSpec((1, count, width), lambda j: (j, 0, 0)),
            pl.BlockSpec((1, count, width), lambda j: (j, 0, 0)),
            pl.BlockSpec((width, hidden), lambda j: (0, 0)),
            pl.BlockSpec((hidden, width), lambda j: (0, 0)),
            any_spec(),
        ],
        out_specs=[
            pl.BlockSpec((1, count, width), lambda j: (j, 0, 0)),
            pl.BlockSpec((2 * hidden, width), lambda j: (0, 0)),
        ],
        scratch_shapes=[pltpu.VMEM((hidden, width), wide)] * 2,
        compiler_params=plain(),
    )(rows, grads, expand, contract, earlier)


def feed_weights_kernel(rows, grads, expand, contract, earlier, d_expand, d_contract, expand_sum, contract_sum):
    step = pl.program_id(0)
    x = rows[...].reshape(-1, rows.shape[3])
    g = grads[...].reshape(-1, rows.shape[3])
    act, slope = gelu_parts(nn(x, expand[...]))
    d_hidden = (nt(g, contract[...]) * slope).astype(low)
    one = tn(d_hidden, x)
    two = tn(act.astype(low), g)

    @pl.when(step == 0)
    def _():
        expand_sum[...] = one
        contract_sum[...] = two

    @pl.when(step > 0)
    def _():
        expand_sum[...] += one
        contract_sum[...] += two

    @pl.when(step == pl.num_programs(0) - 1)
    def _():
        d_expand[...] = expand_sum[...].T
        d_contract[...] = contract_sum[...]


def feed_weights(both, expand, contract, earlier):
    parts, _, count, width = both.shape
    hidden = contract.shape[0]
    block = (parts // 2, 1, count, width)
    return pl.pallas_call(
        feed_weights_kernel,
        out_shape=(jax.ShapeDtypeStruct((width, hidden), wide), jax.ShapeDtypeStruct((hidden, width), wide)),
        grid=(2,),
        in_specs=[
            pl.BlockSpec(block, lambda j: (j, 0, 0, 0)),
            pl.BlockSpec(block, lambda j: (j, 1, 0, 0)),
            pl.BlockSpec((width, hidden), lambda j: (0, 0)),
            pl.BlockSpec((hidden, width), lambda j: (0, 0)),
            any_spec(),
        ],
        out_specs=[
            pl.BlockSpec((width, hidden), lambda j: (0, 0)),
            pl.BlockSpec((hidden, width), lambda j: (0, 0)),
        ],
        scratch_shapes=[pltpu.VMEM((hidden, width), wide)] * 2,
        compiler_params=plain(),
    )(both, both, expand, contract, earlier)


OWNERS = (3, 5, 7, 1, 2, 4, 6, 0)


def swap(array, mask):
    return lax.ppermute(array, "seq", [(i, i ^ mask) for i in range(8)])


def add_kernel(left, right, earlier, out):
    out[...] = add_low(left[...], right[...])


def add_after(left, right, earlier):
    return pl.pallas_call(
        add_kernel,
        out_shape=jax.ShapeDtypeStruct(left.shape, low),
        in_specs=[vmem_spec()] * 2 + [any_spec()],
        out_specs=vmem_spec(),
        compiler_params=plain(),
    )(left, right, earlier)


def scatter_cores(away, kept, earlier):
    return add_after(kept, swap(away, 1), earlier)


def scatter_first(both):
    half = both.shape[1] // 2
    one, two = both[:, :half], both[:, half:]
    one_came = swap(jnp.stack([one[0], one[2]]), 2)
    two_came = swap(jnp.stack([two[1], two[2]]), 4)
    return (
        add_low(one[3], one_came[0]),
        add_low(one[1], one_came[1]),
        add_low(two[3], two_came[0]),
        add_low(two[0], two_came[1]),
    )


def scatter_second(parts):
    one, one_far, two, two_far = parts
    return add_low(one, swap(one_far, 4)), add_low(two, swap(two_far, 2))


def plane_body(
    source_tokens,
    target_tokens,
    source_lengths,
    target_lengths,
    encoder_query,
    encoder_key,
    encoder_value,
    encoder_mix,
    attend_gain,
    attend_shift,
    encoder_expand,
    encoder_contract,
    encoder_gain,
    encoder_shift,
    decoder_query,
    decoder_key,
    decoder_value,
    decoder_mix,
    self_gain,
    self_shift,
    cross_query,
    cross_key,
    cross_value,
    cross_mix,
    cross_gain,
    cross_shift,
    decoder_expand,
    decoder_contract,
    decoder_gain,
    decoder_shift,
    source_cotangent,
    target_cotangent,
):
    slots, tables, width = source_tokens.shape
    places = target_tokens.shape[0]
    me = lax.axis_index("seq")
    quarter = width // 4
    slice_rows = width // 8

    def flat(array):
        return jnp.swapaxes(array, 0, 1).reshape(-1, width)

    def unflat(array):
        return jnp.swapaxes(array.reshape(tables, -1, width), 0, 1)

    def columns(weight):
        return lax.dynamic_slice_in_dim(weight, (me % 4) * quarter, quarter, 1)

    def own(rows):
        return lax.dynamic_slice_in_dim(rows, me * slice_rows, slice_rows, 1)

    def own_places(rows):
        return lax.dynamic_slice_in_dim(rows.reshape(tables, 8 * places, width), me * places, places, 1)

    def own_vector(vector):
        return lax.dynamic_slice_in_dim(vector, me * slice_rows, slice_rows, 0)

    source_flat = flat(source_tokens)
    all_expand = lax.all_gather(encoder_expand, "seq", axis=0)
    all_contract = lax.all_gather(encoder_contract, "seq", axis=0)
    target_pair = jnp.stack([jnp.swapaxes(target_tokens, 0, 1), jnp.swapaxes(target_cotangent, 0, 1)], 0)
    rows, target_all = gather_table(source_flat.reshape(tables, slots, width), target_pair.reshape(-1, width))
    rows = rows.reshape(-1, width)
    target_all = jnp.moveaxis(target_all.reshape(8, 2, tables, places, width), 0, 2).reshape(2, -1, width)
    target_flat, target_grad = target_all[0], target_all[1]
    w_three = jnp.concatenate([columns(encoder_query), columns(encoder_key), columns(encoder_value)], 1)
    length = lax.dynamic_slice_in_dim(source_lengths, me // 4, 1, 0)
    three = project(rows, w_three).astype(low)
    context, logsum = flash_forward(length, three, 256)
    encoder_context = heads_to_rows(context.reshape(8, slots, quarter)).reshape(-1, width)
    first, first_back = jax.vjp(
        layer_norm, source_flat.astype(wide) + project(encoder_context, encoder_mix), attend_gain, attend_shift
    )
    first_low = first.astype(low)
    widened = feed_forward(first_low, all_expand, all_contract)
    first_all = lax.all_gather(first_low, "seq", axis=0)
    second, second_back = jax.vjp(layer_norm, first + widened, encoder_gain, encoder_shift)
    encoded = second.astype(low)

    self_queries = project(target_flat, decoder_query).astype(low)
    self_keys = project(target_flat, decoder_key).astype(low)
    self_values = project(target_flat, decoder_value).astype(low)
    decoder_context, self_tops, self_sums = small_forward(
        target_lengths, self_queries, self_keys, self_values, True
    )
    self_logs = self_tops + jnp.log(self_sums)
    third, third_back = jax.vjp(
        layer_norm, target_flat.astype(wide) + project(decoder_context, decoder_mix), self_gain, self_shift
    )
    third_low = third.astype(low)
    cross_queries = project(third_low, cross_query).astype(low)

    cross_keys = project(encoded, cross_key).astype(low)
    cross_values = project(encoded, cross_value).astype(low)
    here = source_lengths - me * slots
    part, part_tops, part_sums = small_forward(here, cross_queries, cross_keys, cross_values, False)
    cross_context, cross_logs = merge_parts(part, part_tops, part_sums)
    fourth, fourth_back = jax.vjp(
        layer_norm, third + project(cross_context, cross_mix), cross_gain, cross_shift
    )
    fourth_low = fourth.astype(low)
    hidden = project(fourth_low, decoder_expand)
    decoder_acts, gelu_back = jax.vjp(gelu_exact, hidden)
    decoder_acts = decoder_acts.astype(low)
    narrowed = sum_small(project(decoder_acts, decoder_contract), 4, first_all).astype(wide)
    fifth, fifth_back = jax.vjp(layer_norm, fourth + narrowed, decoder_gain, decoder_shift)
    decoded = jnp.swapaxes(own_places(fifth.astype(low)), 0, 1)

    d_fifth, grad_decoder_gain, grad_decoder_shift = fifth_back(target_grad.astype(wide))
    fifth_low = d_fifth.astype(low)
    d_hidden = gelu_back(project_back(fifth_low, decoder_contract))[0].astype(low)
    eighth = fourth_low.shape[0] // 8
    decoder_pair = jnp.stack(
        [lax.dynamic_slice_in_dim(array, me * eighth, eighth, 0) for array in (fourth_low, fifth_low)], 0
    )
    decoder_pair = lax.all_gather(decoder_pair, ("dp", "seq"), axis=0)
    def over_tables(terms):
        part = lax.psum_scatter(terms, "dp", scatter_dimension=0, tiled=True)
        return lax.all_gather(part, "dp", axis=0, tiled=True)

    def join(arrays):
        return jnp.concatenate([a.astype(low) for a in arrays], 0)

    d_rows = sum_small(project_back(d_hidden, decoder_expand), 10).astype(wide)
    d_fourth, grad_cross_gain, grad_cross_shift = fourth_back(d_fifth + d_rows)
    cross_low = d_fourth.astype(low)
    grad_cross_mix = outer_sum(own(cross_context), cross_low)
    d_cross = project_back(cross_low, cross_mix).astype(low)
    dq_part, dk_cross, dv_cross = small_backward(
        here, cross_queries, cross_keys, cross_values, d_cross, cross_context, cross_logs, False, cross_logs
    )
    d_encoded = project_back(dk_cross, cross_key) + project_back(dv_cross, cross_value)
    order = me ^ jnp.array(OWNERS, jnp.int32)


    d_second, grad_encoder_gain, grad_encoder_shift = second_back(flat(source_cotangent).astype(wide) + d_encoded)
    d_second_low = d_second.astype(low)
    d_all = lax.all_gather(d_second_low, "seq", axis=0)
    dq_cross = sum_small(dq_part, 11, d_second_low)
    cross_away, cross_kept = outer_by_owner(order, decoder_pair, encoded, dk_cross, dv_cross)
    grad_cross_query = outer_sum(own(third_low), dq_cross)
    d_third, grad_self_gain, grad_self_shift = third_back(d_fourth + project_back(dq_cross, cross_query))
    self_low = d_third.astype(low)
    grad_decoder_mix = outer_sum(own(decoder_context), self_low)
    dq_self, dk_self, dv_self = small_backward(
        target_lengths,
        self_queries,
        self_keys,
        self_values,
        project_back(self_low, decoder_mix).astype(low),
        decoder_context,
        self_logs,
        True,
        cross_away,
    )
    dq_self = dq_self.astype(low)
    target_own = own(target_flat)
    grad_decoder_query = outer_sum(target_own, dq_self)
    grad_decoder_key = outer_sum(target_own, dk_self)
    grad_decoder_value = outer_sum(target_own, dv_self)
    grad_target = own_places(
        d_third
        + project_back(dq_self, decoder_query)
        + project_back(dk_self, decoder_key)
        + project_back(dv_self, decoder_value)
    )
    grad_target = jnp.swapaxes(grad_target, 0, 1)

    decoder_vectors = jnp.stack(
        [
            own_vector(v)
            for v in (
                grad_self_gain,
                grad_self_shift,
                grad_cross_gain,
                grad_cross_shift,
                grad_decoder_gain,
                grad_decoder_shift,
            )
        ],
        0,
    )
    decoder_vectors = jnp.pad(decoder_vectors.reshape(1, -1), ((0, 15), (0, width - 6 * slice_rows)))
    middle = [
        grad_decoder_query,
        grad_decoder_key,
        grad_decoder_value,
        grad_decoder_mix,
        grad_cross_query,
        grad_cross_mix,
        decoder_vectors,
    ]
    middle_join = join(middle + [jnp.zeros((48, width), low)])
    middle_sum = over_tables(middle_join)
    d_terms, feed_join = feed_backward(first_all, d_all, encoder_expand, encoder_contract, dq_self)
    feed_sum = over_tables(feed_join)
    cross_both = scatter_cores(cross_away, cross_kept, feed_join)
    d_rows = scatter_plane(d_terms)
    d_first, grad_attend_gain, grad_attend_shift = first_back(d_second + d_rows)
    encoder_low = d_first.astype(low)
    mix_away, mix_kept = outer_by_owner(order, encoder_low, encoder_context, encoder_low)
    d_context = rows_to_heads(project_back(encoder_low, encoder_mix).astype(low).reshape(tables, slots, width))
    mix_both = scatter_cores(mix_away, mix_kept, d_context)
    d_context = d_context.reshape(-1, quarter)
    delta = jnp.sum(
        (d_context.astype(wide) * context.astype(wide)).reshape(-1, quarter // 64, 64), -1
    )
    d_three = flash_backward(length, three, d_context, logsum[:, : quarter // 64].T, delta.T, 256, 512)
    vectors = jnp.stack(
        [grad_attend_gain, grad_attend_shift, grad_encoder_gain, grad_encoder_shift], 0
    ).astype(low)
    vectors = jnp.swapaxes(vectors.reshape(4, 8, slice_rows), 0, 1)
    vectors = jnp.pad(vectors, ((0, 0), (0, 12), (0, 3 * quarter - slice_rows)))
    parts = scatter_second(scatter_first(mix_both)) + scatter_second(scatter_first(cross_both))
    d_source, line, plane_sum = finish(rows, d_three, w_three, vectors, join(parts))
    grad_decoder_expand, grad_decoder_contract = feed_weights(
        decoder_pair, decoder_expand, decoder_contract, d_three
    )
    grad_source = unflat(d_first + d_source.reshape(-1, width))
    encoder_three = line[: 3 * slice_rows].reshape(3, slice_rows, width)
    encoder_vectors = line[3 * slice_rows : 3 * slice_rows + 4, :slice_rows]
    plane_three = plane_sum.reshape(3, slice_rows, width)
    sums = widen_after(feed_sum, middle_sum, [part.shape[0] for part in middle], line)
    grad_encoder_expand, grad_encoder_contract, *six, decoder_vectors = sums
    decoder_vectors = decoder_vectors[0, : 6 * slice_rows].reshape(6, slice_rows)
    return (
        unflat(encoded),
        decoded,
        grad_source,
        grad_target,
        encoder_three[0],
        encoder_three[1],
        encoder_three[2],
        plane_three[0],
        encoder_vectors[0],
        encoder_vectors[1],
        grad_encoder_expand,
        grad_encoder_contract,
        encoder_vectors[2],
        encoder_vectors[3],
        six[0],
        six[1],
        six[2],
        six[3],
        decoder_vectors[0],
        decoder_vectors[1],
        six[4],
        plane_three[1],
        plane_three[2],
        six[5],
        decoder_vectors[2],
        decoder_vectors[3],
        grad_decoder_expand,
        grad_decoder_contract,
        decoder_vectors[4],
        decoder_vectors[5],
    )


def solution(mesh):
    body = plane_body if fits_plane(mesh) else general_body
    in_specs = (
        P("seq", "dp", None),
        P("seq", "dp", None),
        P("dp"),
        P("dp"),
        P(),
        P(),
        P(),
        P(),
        P(),
        P(),
        P(None, "seq"),
        P("seq", None),
        P(),
        P(),
        P(),
        P(),
        P(),
        P(),
        P(),
        P(),
        P(),
        P(),
        P(),
        P(),
        P(),
        P(),
        P(None, "seq"),
        P("seq", None),
        P(),
        P(),
        P("seq", "dp", None),
        P("seq", "dp", None),
    )
    out_specs = (
        P("seq", "dp", None),
        P("seq", "dp", None),
        P("seq", "dp", None),
        P("seq", "dp", None),
        P("seq", None),
        P("seq", None),
        P("seq", None),
        P("seq", None),
        P("seq"),
        P("seq"),
        P(None, "seq"),
        P("seq", None),
        P("seq"),
        P("seq"),
        P("seq", None),
        P("seq", None),
        P("seq", None),
        P("seq", None),
        P("seq"),
        P("seq"),
        P("seq", None),
        P("seq", None),
        P("seq", None),
        P("seq", None),
        P("seq"),
        P("seq"),
        P(None, "seq"),
        P("seq", None),
        P("seq"),
        P("seq"),
    )
    return jax.shard_map(body, mesh=mesh, in_specs=in_specs, out_specs=out_specs, check_vma=False)
```

```python
import functools

import jax
import jax.numpy as jnp
from jax import lax
from jax.experimental import pallas as pl
from jax.experimental.pallas import tpu as pltpu
from jax.sharding import PartitionSpec as P

HEADS = 16


masked_fill = -1e30
norm_epsilon = 1e-05


def layer_norm(rows, gain, shift):
    centre = jnp.mean(rows, -1, keepdims=True)
    centred = rows - centre
    spread = jnp.mean(centred * centred, -1, keepdims=True)
    return centred * lax.rsqrt(spread + norm_epsilon) * gain + shift


def gelu_exact(values):
    return jax.nn.gelu(values, approximate=False)


def project(rows, weight):
    return jnp.dot(rows, weight, preferred_element_type=jnp.float32)


def project_back(grads, weight):
    return jnp.einsum("re,de->rd", grads, weight, preferred_element_type=jnp.float32)


def outer_sum(rows, grads):
    return jnp.einsum("rd,re->de", rows, grads, preferred_element_type=jnp.float32)


def by_heads(array):
    return array.reshape(array.shape[0], HEADS, -1)


def head_scale(width):
    return (width // HEADS) ** (-0.5)


def score_block(queries, keys):
    scores = jnp.einsum(
        "qhd,khd->hqk", by_heads(queries), by_heads(keys), preferred_element_type=jnp.float32
    )
    return scores * head_scale(queries.shape[-1])


def allowed_keys(query_rows, key_rows, length, causal):
    allowed = key_rows[None, :] < length
    if causal:
        allowed = allowed & (key_rows[None, :] <= query_rows[:, None])
    return allowed


def table_of(array, table):
    return lax.dynamic_index_in_dim(array, table, 1, keepdims=False)


def gather_pair(keys, values):
    return (
        lax.all_gather(keys, "seq", axis=0, tiled=True),
        lax.all_gather(values, "seq", axis=0, tiled=True),
    )


def gather_rows(rows):
    return lax.all_gather(rows, "seq", axis=0, tiled=True)


def sum_rows(terms, count):
    return lax.psum_scatter(
        terms(jnp.int32(0), count * lax.axis_size("seq")).astype(jnp.bfloat16),
        "seq",
        scatter_dimension=0,
        tiled=True,
    ).astype(jnp.float32)


def projections(from_rows, to_rows, w_query, w_key, w_value):
    qlen, tables, width = from_rows.shape
    klen = to_rows.shape[0]
    to_flat = to_rows.reshape(-1, width)
    queries = (
        project(from_rows.reshape(-1, width), w_query)
        .astype(jnp.bfloat16)
        .reshape(qlen, tables, width)
    )
    keys = project(to_flat, w_key).astype(jnp.bfloat16).reshape(klen, tables, width)
    values = project(to_flat, w_value).astype(jnp.bfloat16).reshape(klen, tables, width)
    return (queries, keys, values)


def finish_grads(from_rows, to_rows, w_query, w_key, w_value, d_queries, d_keys, d_values):
    width = from_rows.shape[-1]
    from_flat = from_rows.reshape(-1, width)
    to_flat = to_rows.reshape(-1, width)
    query_low = d_queries.astype(jnp.bfloat16).reshape(-1, width)
    key_low = d_keys.astype(jnp.bfloat16).reshape(-1, width)
    value_low = d_values.astype(jnp.bfloat16).reshape(-1, width)
    grad_query = outer_sum(from_flat, query_low)
    grad_key = outer_sum(to_flat, key_low)
    grad_value = outer_sum(to_flat, value_low)
    d_from = project_back(query_low, w_query)
    d_to = project_back(key_low, w_key) + project_back(value_low, w_value)
    return (d_from, d_to, grad_query, grad_key, grad_value)


def attend_forward(from_rows, to_rows, w_query, w_key, w_value, lengths, causal):
    qlen, tables, width = from_rows.shape
    queries, keys, values = projections(from_rows, to_rows, w_query, w_key, w_value)
    gathered = gather_pair(keys, values)
    all_keys, all_values = gathered
    query_rows = lax.axis_index("seq") * qlen + jnp.arange(qlen)
    key_rows = jnp.arange(all_keys.shape[0])

    def one_table(table):
        scores = score_block(table_of(queries, table), table_of(all_keys, table))
        allowed = allowed_keys(query_rows, key_rows, lengths[table], causal)
        scores = jnp.where(allowed[None], scores, masked_fill)
        top = jnp.max(scores, -1)
        weights = jnp.exp(scores - top[..., None])
        total = jnp.sum(weights, -1)
        probs = (weights / total[..., None]).astype(jnp.bfloat16)
        context = jnp.einsum(
            "hqk,khd->qhd",
            probs,
            by_heads(table_of(all_values, table)),
            preferred_element_type=jnp.float32,
        )
        return (context.reshape(qlen, width), top + jnp.log(total))

    context, logsum = lax.map(one_table, jnp.arange(tables))
    return (queries, keys, values, gathered, jnp.swapaxes(context, 0, 1), logsum)


def key_value_terms(
    query_part,
    grads_part,
    logsum_part,
    delta_part,
    key_part,
    value_part,
    query_rows,
    part_rows,
    length,
    causal,
    scale,
):
    scores = score_block(query_part, key_part)
    allowed = allowed_keys(query_rows, part_rows, length, causal)
    probs = jnp.where(allowed[None], jnp.exp(scores - logsum_part[..., None]), 0.0)
    grads_here = by_heads(grads_part)
    d_values = jnp.einsum(
        "hqk,qhd->khd", probs.astype(jnp.bfloat16), grads_here, preferred_element_type=jnp.float32
    )
    d_probs = jnp.einsum(
        "qhd,khd->hqk", grads_here, by_heads(value_part), preferred_element_type=jnp.float32
    )
    d_scores = (probs * (d_probs - delta_part.T[..., None])).astype(jnp.bfloat16)
    d_keys = (
        jnp.einsum(
            "hqk,qhd->khd", d_scores, by_heads(query_part), preferred_element_type=jnp.float32
        )
        * scale
    )
    count = key_part.shape[0]
    width = key_part.shape[-1]
    return jnp.concatenate([d_keys.reshape(count, width), d_values.reshape(count, width)], -1)


def attend_backward(state, from_rows, to_rows, w_query, w_key, w_value, lengths, causal, d_context):
    queries, keys, values, gathered, context, logsum = state
    qlen, tables, width = queries.shape
    klen = keys.shape[0]
    all_keys, all_values = gather_pair(keys, values)
    scale = head_scale(width)
    d_low = d_context.reshape(qlen, tables, width).astype(jnp.bfloat16)
    delta = jnp.sum((d_low.astype(jnp.float32) * context).reshape(qlen, tables, HEADS, -1), -1)
    query_rows = lax.axis_index("seq") * qlen + jnp.arange(qlen)
    key_rows = jnp.arange(all_keys.shape[0])

    def query_table(table):
        scores = score_block(table_of(queries, table), table_of(all_keys, table))
        allowed = allowed_keys(query_rows, key_rows, lengths[table], causal)
        probs = jnp.where(allowed[None], jnp.exp(scores - logsum[table][..., None]), 0.0)
        d_probs = jnp.einsum(
            "qhd,khd->hqk",
            by_heads(table_of(d_low, table)),
            by_heads(table_of(all_values, table)),
            preferred_element_type=jnp.float32,
        )
        d_scores = (probs * (d_probs - delta[:, table].T[..., None])).astype(jnp.bfloat16)
        d_query = jnp.einsum(
            "hqk,khd->qhd",
            d_scores,
            by_heads(table_of(all_keys, table)),
            preferred_element_type=jnp.float32,
        )
        return (d_query * scale).reshape(qlen, width)

    d_queries = jnp.swapaxes(lax.map(query_table, jnp.arange(tables)), 0, 1)
    part_rows = jnp.arange(klen * lax.axis_size("seq"))

    def key_table(table, terms):
        piece = key_value_terms(
            table_of(queries, table),
            table_of(d_low, table),
            logsum[table],
            delta[:, table],
            table_of(all_keys, table),
            table_of(all_values, table),
            query_rows,
            part_rows,
            lengths[table],
            causal,
            scale,
        )
        return lax.dynamic_update_index_in_dim(terms, piece, table, 1)

    summed = lax.psum_scatter(
        lax.fori_loop(
            0,
            tables,
            key_table,
            jnp.zeros((klen * lax.axis_size("seq"), tables, 2 * width), jnp.float32),
        ).astype(jnp.bfloat16),
        "seq",
        scatter_dimension=0,
        tiled=True,
    ).astype(jnp.float32)
    return finish_grads(
        from_rows,
        to_rows,
        w_query,
        w_key,
        w_value,
        d_queries,
        summed[..., :width],
        summed[..., width:],
    )


def token_forward(rows, w_expand, w_contract):
    all_rows = gather_rows(rows)
    acts = gelu_exact(project(all_rows, w_expand)).astype(jnp.bfloat16)

    def contract_terms(start, count):
        return project(acts, w_contract)

    return (sum_rows(contract_terms, rows.shape[0]), all_rows)


def token_backward(all_rows, d_out, w_expand, w_contract):
    all_grads = gather_rows(d_out.astype(jnp.bfloat16))
    acts, gelu_back = jax.vjp(gelu_exact, project(all_rows, w_expand))
    d_hidden = gelu_back(project_back(all_grads, w_contract))[0].astype(jnp.bfloat16)
    grad_expand = outer_sum(all_rows, d_hidden)
    grad_contract = outer_sum(acts.astype(jnp.bfloat16), all_grads)

    def expand_terms(start, count):
        return project_back(d_hidden, w_expand)

    return (sum_rows(expand_terms, d_out.shape[0]), grad_expand, grad_contract)


def general_body(
    source_tokens,
    target_tokens,
    source_lengths,
    target_lengths,
    encoder_query,
    encoder_key,
    encoder_value,
    encoder_mix,
    attend_gain,
    attend_shift,
    encoder_expand,
    encoder_contract,
    encoder_gain,
    encoder_shift,
    decoder_query,
    decoder_key,
    decoder_value,
    decoder_mix,
    self_gain,
    self_shift,
    cross_query,
    cross_key,
    cross_value,
    cross_mix,
    cross_gain,
    cross_shift,
    decoder_expand,
    decoder_contract,
    decoder_gain,
    decoder_shift,
    source_cotangent,
    target_cotangent,
):
    slots, tables, width = source_tokens.shape
    places = target_tokens.shape[0]
    source_flat = source_tokens.reshape(-1, width)
    target_flat = target_tokens.reshape(-1, width)
    encoder_state = attend_forward(
        source_tokens,
        source_tokens,
        encoder_query,
        encoder_key,
        encoder_value,
        source_lengths,
        False,
    )
    encoder_context = encoder_state[4].reshape(-1, width).astype(jnp.bfloat16)
    first, first_back = jax.vjp(
        layer_norm,
        source_flat.astype(jnp.float32) + project(encoder_context, encoder_mix),
        attend_gain,
        attend_shift,
    )
    first_low = first.astype(jnp.bfloat16)
    widened, encoder_kept = token_forward(first_low, encoder_expand, encoder_contract)
    second, second_back = jax.vjp(layer_norm, first + widened, encoder_gain, encoder_shift)
    encoded = second.astype(jnp.bfloat16).reshape(slots, tables, width)
    decoder_state = attend_forward(
        target_tokens,
        target_tokens,
        decoder_query,
        decoder_key,
        decoder_value,
        target_lengths,
        True,
    )
    decoder_context = decoder_state[4].reshape(-1, width).astype(jnp.bfloat16)
    third, third_back = jax.vjp(
        layer_norm,
        target_flat.astype(jnp.float32) + project(decoder_context, decoder_mix),
        self_gain,
        self_shift,
    )
    third_blocks = third.astype(jnp.bfloat16).reshape(places, tables, width)
    cross_state = attend_forward(
        third_blocks, encoded, cross_query, cross_key, cross_value, source_lengths, False
    )
    cross_context = cross_state[4].reshape(-1, width).astype(jnp.bfloat16)
    fourth, fourth_back = jax.vjp(
        layer_norm, third + project(cross_context, cross_mix), cross_gain, cross_shift
    )
    fourth_low = fourth.astype(jnp.bfloat16)
    narrowed, decoder_kept = token_forward(fourth_low, decoder_expand, decoder_contract)
    fifth, fifth_back = jax.vjp(layer_norm, fourth + narrowed, decoder_gain, decoder_shift)
    decoded = fifth.astype(jnp.bfloat16).reshape(places, tables, width)
    d_fifth, grad_decoder_gain, grad_decoder_shift = fifth_back(
        target_cotangent.reshape(-1, width).astype(jnp.float32)
    )
    d_rows, grad_decoder_expand, grad_decoder_contract = token_backward(
        decoder_kept, d_fifth, decoder_expand, decoder_contract
    )
    d_fourth, grad_cross_gain, grad_cross_shift = fourth_back(d_fifth + d_rows)
    cross_low = d_fourth.astype(jnp.bfloat16)
    grad_cross_mix = outer_sum(cross_context, cross_low)
    d_cross_context = project_back(cross_low, cross_mix)
    d_third_cross, d_encoded, grad_cross_query, grad_cross_key, grad_cross_value = attend_backward(
        cross_state,
        third_blocks,
        encoded,
        cross_query,
        cross_key,
        cross_value,
        source_lengths,
        False,
        d_cross_context,
    )
    d_third, grad_self_gain, grad_self_shift = third_back(d_fourth + d_third_cross)
    self_low = d_third.astype(jnp.bfloat16)
    grad_decoder_mix = outer_sum(decoder_context, self_low)
    d_from, d_to, grad_decoder_query, grad_decoder_key, grad_decoder_value = attend_backward(
        decoder_state,
        target_tokens,
        target_tokens,
        decoder_query,
        decoder_key,
        decoder_value,
        target_lengths,
        True,
        project_back(self_low, decoder_mix),
    )
    grad_target = (d_third + d_from + d_to).reshape(places, tables, width)
    d_second, grad_encoder_gain, grad_encoder_shift = second_back(
        source_cotangent.reshape(-1, width).astype(jnp.float32) + d_encoded
    )
    d_rows, grad_encoder_expand, grad_encoder_contract = token_backward(
        encoder_kept, d_second, encoder_expand, encoder_contract
    )
    d_first, grad_attend_gain, grad_attend_shift = first_back(d_second + d_rows)
    encoder_low = d_first.astype(jnp.bfloat16)
    grad_encoder_mix = outer_sum(encoder_context, encoder_low)
    d_from, d_to, grad_encoder_query, grad_encoder_key, grad_encoder_value = attend_backward(
        encoder_state,
        source_tokens,
        source_tokens,
        encoder_query,
        encoder_key,
        encoder_value,
        source_lengths,
        False,
        project_back(encoder_low, encoder_mix),
    )
    grad_source = (d_first + d_from + d_to).reshape(slots, tables, width)
    shards = (
        lax.psum_scatter(
            grad_encoder_query.astype(jnp.bfloat16), "seq", scatter_dimension=0, tiled=True
        ).astype(jnp.float32),
        lax.psum_scatter(
            grad_encoder_key.astype(jnp.bfloat16), "seq", scatter_dimension=0, tiled=True
        ).astype(jnp.float32),
        lax.psum_scatter(
            grad_encoder_value.astype(jnp.bfloat16), "seq", scatter_dimension=0, tiled=True
        ).astype(jnp.float32),
        lax.psum_scatter(
            grad_encoder_mix.astype(jnp.bfloat16), "seq", scatter_dimension=0, tiled=True
        ).astype(jnp.float32),
        lax.psum_scatter(
            grad_decoder_query.astype(jnp.bfloat16), "seq", scatter_dimension=0, tiled=True
        ).astype(jnp.float32),
        lax.psum_scatter(
            grad_decoder_key.astype(jnp.bfloat16), "seq", scatter_dimension=0, tiled=True
        ).astype(jnp.float32),
        lax.psum_scatter(
            grad_decoder_value.astype(jnp.bfloat16), "seq", scatter_dimension=0, tiled=True
        ).astype(jnp.float32),
        lax.psum_scatter(
            grad_decoder_mix.astype(jnp.bfloat16), "seq", scatter_dimension=0, tiled=True
        ).astype(jnp.float32),
        lax.psum_scatter(
            grad_cross_query.astype(jnp.bfloat16), "seq", scatter_dimension=0, tiled=True
        ).astype(jnp.float32),
        lax.psum_scatter(
            grad_cross_key.astype(jnp.bfloat16), "seq", scatter_dimension=0, tiled=True
        ).astype(jnp.float32),
        lax.psum_scatter(
            grad_cross_value.astype(jnp.bfloat16), "seq", scatter_dimension=0, tiled=True
        ).astype(jnp.float32),
        lax.psum_scatter(
            grad_cross_mix.astype(jnp.bfloat16), "seq", scatter_dimension=0, tiled=True
        ).astype(jnp.float32),
        lax.psum_scatter(
            grad_attend_gain.astype(jnp.bfloat16), "seq", scatter_dimension=0, tiled=True
        ).astype(jnp.float32),
        lax.psum_scatter(
            grad_attend_shift.astype(jnp.bfloat16), "seq", scatter_dimension=0, tiled=True
        ).astype(jnp.float32),
        lax.psum_scatter(
            grad_encoder_gain.astype(jnp.bfloat16), "seq", scatter_dimension=0, tiled=True
        ).astype(jnp.float32),
        lax.psum_scatter(
            grad_encoder_shift.astype(jnp.bfloat16), "seq", scatter_dimension=0, tiled=True
        ).astype(jnp.float32),
        lax.psum_scatter(
            grad_self_gain.astype(jnp.bfloat16), "seq", scatter_dimension=0, tiled=True
        ).astype(jnp.float32),
        lax.psum_scatter(
            grad_self_shift.astype(jnp.bfloat16), "seq", scatter_dimension=0, tiled=True
        ).astype(jnp.float32),
        lax.psum_scatter(
            grad_cross_gain.astype(jnp.bfloat16), "seq", scatter_dimension=0, tiled=True
        ).astype(jnp.float32),
        lax.psum_scatter(
            grad_cross_shift.astype(jnp.bfloat16), "seq", scatter_dimension=0, tiled=True
        ).astype(jnp.float32),
        lax.psum_scatter(
            grad_decoder_gain.astype(jnp.bfloat16), "seq", scatter_dimension=0, tiled=True
        ).astype(jnp.float32),
        lax.psum_scatter(
            grad_decoder_shift.astype(jnp.bfloat16), "seq", scatter_dimension=0, tiled=True
        ).astype(jnp.float32),
    )
    totals = (
        lax.psum(shards[0].astype(jnp.bfloat16), "dp").astype(jnp.float32),
        lax.psum(shards[1].astype(jnp.bfloat16), "dp").astype(jnp.float32),
        lax.psum(shards[2].astype(jnp.bfloat16), "dp").astype(jnp.float32),
        lax.psum(shards[3].astype(jnp.bfloat16), "dp").astype(jnp.float32),
        lax.psum(shards[4].astype(jnp.bfloat16), "dp").astype(jnp.float32),
        lax.psum(shards[5].astype(jnp.bfloat16), "dp").astype(jnp.float32),
        lax.psum(shards[6].astype(jnp.bfloat16), "dp").astype(jnp.float32),
        lax.psum(shards[7].astype(jnp.bfloat16), "dp").astype(jnp.float32),
        lax.psum(shards[8].astype(jnp.bfloat16), "dp").astype(jnp.float32),
        lax.psum(shards[9].astype(jnp.bfloat16), "dp").astype(jnp.float32),
        lax.psum(shards[10].astype(jnp.bfloat16), "dp").astype(jnp.float32),
        lax.psum(shards[11].astype(jnp.bfloat16), "dp").astype(jnp.float32),
        lax.psum(shards[12].astype(jnp.bfloat16), "dp").astype(jnp.float32),
        lax.psum(shards[13].astype(jnp.bfloat16), "dp").astype(jnp.float32),
        lax.psum(shards[14].astype(jnp.bfloat16), "dp").astype(jnp.float32),
        lax.psum(shards[15].astype(jnp.bfloat16), "dp").astype(jnp.float32),
        lax.psum(shards[16].astype(jnp.bfloat16), "dp").astype(jnp.float32),
        lax.psum(shards[17].astype(jnp.bfloat16), "dp").astype(jnp.float32),
        lax.psum(shards[18].astype(jnp.bfloat16), "dp").astype(jnp.float32),
        lax.psum(shards[19].astype(jnp.bfloat16), "dp").astype(jnp.float32),
        lax.psum(shards[20].astype(jnp.bfloat16), "dp").astype(jnp.float32),
        lax.psum(shards[21].astype(jnp.bfloat16), "dp").astype(jnp.float32),
        lax.psum(grad_encoder_expand.astype(jnp.bfloat16), "dp").astype(jnp.float32),
        lax.psum(grad_encoder_contract.astype(jnp.bfloat16), "dp").astype(jnp.float32),
        lax.psum(grad_decoder_expand.astype(jnp.bfloat16), "dp").astype(jnp.float32),
        lax.psum(grad_decoder_contract.astype(jnp.bfloat16), "dp").astype(jnp.float32),
    )
    return (
        encoded,
        decoded,
        grad_source,
        grad_target,
        totals[0],
        totals[1],
        totals[2],
        totals[3],
        totals[12],
        totals[13],
        totals[22],
        totals[23],
        totals[14],
        totals[15],
        totals[4],
        totals[5],
        totals[6],
        totals[7],
        totals[16],
        totals[17],
        totals[8],
        totals[9],
        totals[10],
        totals[11],
        totals[18],
        totals[19],
        totals[24],
        totals[25],
        totals[20],
        totals[21],
    )


MESH = pl.DeviceIdType.MESH
PEERS = (6, 7, 2, 3, 4, 5, 1)
low = jnp.bfloat16
wide = jnp.float32
VMEM_BYTES = 60 * 2**20


def fits_plane(mesh):
    return mesh.shape["seq"] == 8


def add_low(left, right):
    return (left.astype(wide) + right.astype(wide)).astype(low)


OWNERS = (3, 5, 7, 1, 2, 4, 6, 0)


def nt(left, right):
    return lax.dot_general(left, right, (((1,), (1,)), ((), ())), preferred_element_type=wide)


def nn(left, right):
    return lax.dot_general(left, right, (((1,), (0,)), ((), ())), preferred_element_type=wide)


def tn(left, right):
    return lax.dot_general(left, right, (((0,), (0,)), ((), ())), preferred_element_type=wide)


def lane_head(shape, size):
    return lax.broadcasted_iota(jnp.int32, shape, len(shape) - 1) // size


def vmem_spec():
    return pl.BlockSpec(memory_space=pltpu.VMEM)


def any_spec():
    return pl.BlockSpec(memory_space=pl.ANY)


def greet(masks, size=0):
    me = lax.axis_index("seq")
    barrier = pltpu.get_barrier_semaphore()
    for mask in masks:
        pl.semaphore_signal(barrier, inc=1, device_id={"seq": me ^ mask}, device_id_type=MESH)
    if not size:
        pl.semaphore_wait(barrier, len(masks))
        return
    place = lax.axis_index("dp")
    inner = (place > 0) & (place < size - 1)

    @pl.when(place > 0)
    def _():
        pl.semaphore_signal(barrier, inc=1, device_id={"dp": place - 1}, device_id_type=MESH)

    @pl.when(place < size - 1)
    def _():
        pl.semaphore_signal(barrier, inc=1, device_id={"dp": place + 1}, device_id_type=MESH)

    @pl.when(inner)
    def _():
        pl.semaphore_wait(barrier, len(masks) + 2)

    @pl.when(jnp.logical_not(inner))
    def _():
        pl.semaphore_wait(barrier, len(masks) + 1)


class Line:
    lag = 2

    def __init__(self, size, chunks, mine, came, sent, send, recv):
        place = lax.axis_index("dp")
        self.chunks, self.mine, self.came, self.sent, self.send, self.recv = chunks, mine, came, sent, send, recv
        self.count = mine.shape[0] // chunks
        self.has = (place > 0, place < size - 1)
        self.neighbour = (place - 1, place + 1)
        self.lower = place < size // 2
        self.steps = chunks + self.lag

    def copy(self, side, chunk, first=False):
        part = pl.ds(chunk * self.count, self.count)
        return pltpu.make_async_remote_copy(
            src_ref=self.mine.at[part] if first else self.sent.at[side, part],
            dst_ref=self.came.at[side, part],
            send_sem=self.send.at[side, chunk],
            recv_sem=self.recv.at[side, chunk],
            device_id={"dp": self.neighbour[1 - side]},
            device_id_type=MESH,
        )

    def begin(self):
        for side in range(2):

            @pl.when(jnp.logical_not(self.has[side]))
            def _(side=side):
                for chunk in range(self.chunks):
                    self.copy(side, chunk, True).start()
                self.came[side] = jnp.zeros(self.mine.shape, low)

    def forward(self, side, chunk):
        part = pl.ds(chunk * self.count, self.count)

        @pl.when(self.has[side])
        def _():
            self.copy(side, chunk).wait_recv()

            @pl.when(self.has[1 - side])
            def _():
                self.sent[side, part] = add_low(self.mine[part], self.came[side, part])
                self.copy(side, chunk).start()

    def step(self, number):
        if number >= self.steps:
            return
        for near in range(2):

            @pl.when(self.lower if near == 0 else jnp.logical_not(self.lower))
            def _(near=near):
                if number < self.chunks:
                    self.forward(near, number)
                if number >= self.lag:
                    self.forward(1 - near, number - self.lag)

    def rest(self, first):
        for number in range(first, self.steps):
            self.step(number)

    def total(self, part=slice(None)):
        return self.mine[part].astype(wide) + self.came[0, part].astype(wide) + self.came[1, part].astype(wide)

    def end(self):
        for side in range(2):

            @pl.when(self.has[1 - side])
            def _(side=side):
                for chunk in range(self.chunks):
                    self.copy(side, chunk).wait_send()


def line_scratch(shape, chunks):
    return [
        pltpu.VMEM((2,) + shape, low),
        pltpu.VMEM((2,) + shape, low),
        pltpu.SemaphoreType.DMA((2, chunks)),
        pltpu.SemaphoreType.DMA((2, chunks)),
    ]


def remote(src, dst, send, recv, to):
    return pltpu.make_async_remote_copy(
        src_ref=src, dst_ref=dst, send_sem=send, recv_sem=recv, device_id={"seq": to}, device_id_type=MESH
    )


def params(collective_id):
    return pltpu.CompilerParams(
        collective_id=collective_id, has_side_effects=True, vmem_limit_bytes=VMEM_BYTES
    )


def gather_table_kernel(rows, extra, out, out_extra, send, recv, keep):
    me = lax.axis_index("seq")
    mine = me // 4
    greet((1, 2, 4, 6))
    own = [
        pltpu.make_async_copy(rows.at[mine], out.at[me], keep.at[0]),
        pltpu.make_async_copy(extra, out_extra.at[me], keep.at[1]),
    ]
    for copy in own:
        copy.start()
    started = []
    both = ((0, lambda table: rows.at[table], out), (1, lambda table: extra, out_extra))
    for slot, mask, table in ((0, 6, 1 - mine), (1, 2, mine), (2, 4, 1 - mine), (3, 1, mine)):
        for kind, source, place in both:
            copy = remote(source(table), place.at[me], send.at[kind, slot], recv.at[kind, slot], me ^ mask)
            copy.start()
            started.append(copy)
    for slot, mask in ((1, 2), (2, 4), (0, 6)):
        owner = me ^ mask
        for kind, source, place in both:
            remote(source(0), place.at[owner], send.at[kind, slot], recv.at[kind, slot], me ^ 1).wait_recv()
            copy = remote(
                place.at[owner], place.at[owner], send.at[kind, 4 + slot], recv.at[kind, 4 + slot], me ^ 1
            )
            copy.start()
            started.append(copy)
    for kind, source, place in both:
        remote(source(0), place.at[me ^ 1], send.at[kind, 3], recv.at[kind, 3], me ^ 1).wait_recv()
        for slot, mask in ((1, 2), (2, 4), (0, 6)):
            remote(
                source(0), place.at[me ^ mask ^ 1], send.at[kind, 4 + slot], recv.at[kind, 4 + slot], me ^ 1
            ).wait_recv()
    for copy in started:
        copy.wait_send()
    for copy in own:
        copy.wait()


def gather_table(rows, extra):
    return pl.pallas_call(
        gather_table_kernel,
        out_shape=(
            jax.ShapeDtypeStruct((8,) + rows.shape[1:], rows.dtype),
            jax.ShapeDtypeStruct((8,) + extra.shape, extra.dtype),
        ),
        in_specs=[any_spec()] * 2,
        out_specs=(any_spec(), any_spec()),
        scratch_shapes=[
            pltpu.SemaphoreType.DMA((2, 7)),
            pltpu.SemaphoreType.DMA((2, 7)),
            pltpu.SemaphoreType.DMA((2,)),
        ],
        compiler_params=params(1),
    )(rows, extra)


def scatter_plane_kernel(terms, pairs, expand, contract, out, d_expand, d_contract, sib, pair, came, far, came_far, send, recv, send_pair, recv_pair, send_far, recv_far):
    me = lax.axis_index("seq")
    half = out.shape[0] // 2
    greet((1, 2, 4))
    halves = (pl.ds(0, half), pl.ds(half, half))
    started = []
    chips = (6, 2, 4, 0)
    for slot, mask in enumerate(chips):
        copy = remote(terms.at[me ^ 1 ^ mask], sib.at[slot], send.at[slot], recv.at[slot], me ^ 1)
        copy.start()
        started.append(copy)

    def pair_copy(slot):
        return remote(
            pair.at[slot], came.at[slot], send_pair.at[slot], recv_pair.at[slot], me ^ (2, 4, 2, 4)[slot]
        )

    def far_copy(slot):
        return remote(far.at[slot], came_far.at[slot], send_far.at[slot], recv_far.at[slot], me ^ (4, 2)[slot])

    def both(mask, slot, rows):
        return terms[me ^ mask, rows].astype(wide) + sib[slot, rows].astype(wide)

    for slot, mask in enumerate(chips):
        remote(terms.at[0], sib.at[slot], send.at[slot], recv.at[slot], me ^ 1).wait_recv()
        if mask == 6:
            for side in range(2):
                pair[side] = both(6, 0, halves[side]).astype(low)
                pair_copy(side).start()
        if mask == 2:
            pair[2] = both(2, 1, halves[0]).astype(low)
            pair_copy(2).start()
        if mask == 4:
            pair[3] = both(4, 2, halves[1]).astype(low)
            pair_copy(3).start()
    x = pairs[:, 0].reshape(-1, pairs.shape[3])
    g = pairs[:, 1].reshape(-1, pairs.shape[3])
    act, slope = gelu_parts(nn(x, expand[...]))
    d_hidden = (nt(g, contract[...]) * slope).astype(low)
    d_expand[...] = tn(x, d_hidden)
    d_contract[...] = tn(act.astype(low), g)
    for side in range(2):
        pair_copy(side).wait_recv()
        mask, slot = ((4, 2), (2, 1))[side]
        far[side] = (both(mask, slot, halves[side]) + came[side].astype(wide)).astype(low)
        far_copy(side).start()
    for side in range(2):
        pair_copy(2 + side).wait_recv()
        out[halves[side]] = both(0, 3, halves[side]) + came[2 + side].astype(wide)
    for side in range(2):
        far_copy(side).wait_recv()
        out[halves[side]] += came_far[side].astype(wide)
    for copy in started:
        copy.wait_send()
    for slot in range(4):
        pair_copy(slot).wait_send()
    for side in range(2):
        far_copy(side).wait_send()


def scatter_plane(terms, pairs, expand, contract):
    _, rows, width = terms.shape
    return pl.pallas_call(
        scatter_plane_kernel,
        out_shape=(
            jax.ShapeDtypeStruct((rows, width), wide),
            jax.ShapeDtypeStruct(expand.shape, wide),
            jax.ShapeDtypeStruct(contract.shape, wide),
        ),
        in_specs=[vmem_spec()] * 4,
        out_specs=(vmem_spec(),) * 3,
        scratch_shapes=[
            pltpu.VMEM((4, rows, width), low),
            pltpu.VMEM((4, rows // 2, width), low),
            pltpu.VMEM((4, rows // 2, width), low),
            pltpu.VMEM((2, rows // 2, width), low),
            pltpu.VMEM((2, rows // 2, width), low),
        ]
        + [pltpu.SemaphoreType.DMA((4,))] * 4
        + [pltpu.SemaphoreType.DMA((2,))] * 2,
        compiler_params=params(9),
    )(terms, pairs, expand, contract)


def heads_to_rows_kernel(blocks, out, send, recv, keep):
    me = lax.axis_index("seq")
    width = blocks.shape[2]
    greet(PEERS)

    def place(owner):
        return out.at[owner // 4, :, pl.ds(pl.multiple_of((owner % 4) * width, width), width)]

    local = pltpu.make_async_copy(blocks.at[me], place(me), keep)
    local.start()
    started = []
    for mask in PEERS:
        copy = remote(blocks.at[me ^ mask], place(me), send.at[mask], recv.at[mask], me ^ mask)
        copy.start()
        started.append(copy)
    for mask in PEERS:
        remote(blocks.at[0], place(me ^ mask), send.at[mask], recv.at[mask], me ^ mask).wait_recv()
    for copy in started:
        copy.wait_send()
    local.wait()


def heads_to_rows(blocks):
    _, rows, width = blocks.shape
    return pl.pallas_call(
        heads_to_rows_kernel,
        out_shape=jax.ShapeDtypeStruct((2, rows, 4 * width), blocks.dtype),
        in_specs=[any_spec()],
        out_specs=any_spec(),
        scratch_shapes=[
            pltpu.SemaphoreType.DMA((8,)),
            pltpu.SemaphoreType.DMA((8,)),
            pltpu.SemaphoreType.DMA,
        ],
        compiler_params=params(2),
    )(blocks)


def rows_to_heads_kernel(rows, left, right, out, away, kept, send, recv, keep):
    me = lax.axis_index("seq")
    width = out.shape[2]
    greet(PEERS)

    def part(owner):
        return rows.at[owner // 4, :, pl.ds(pl.multiple_of((owner % 4) * width, width), width)]

    local = pltpu.make_async_copy(part(me), out.at[me], keep)
    local.start()
    started = []
    for mask in PEERS:
        copy = remote(part(me ^ mask), out.at[me], send.at[mask], recv.at[mask], me ^ mask)
        copy.start()
        started.append(copy)
    size = left.shape[1] // 8
    for place, mask in enumerate(OWNERS):
        columns = pl.ds(pl.multiple_of((me ^ mask) * size, size), size)
        (away, kept)[place // 4][place % 4] = tn(left[:, columns], right[...]).astype(low)
    for mask in PEERS:
        remote(part(me), out.at[me ^ mask], send.at[mask], recv.at[mask], me ^ mask).wait_recv()
    for copy in started:
        copy.wait_send()
    local.wait()


def rows_to_heads(rows, left, right):
    _, count, width = rows.shape
    half = jax.ShapeDtypeStruct((4, width // 8, width), low)
    return pl.pallas_call(
        rows_to_heads_kernel,
        out_shape=(jax.ShapeDtypeStruct((8, count, width // 4), rows.dtype), half, half),
        in_specs=[any_spec(), vmem_spec(), vmem_spec()],
        out_specs=(any_spec(), vmem_spec(), vmem_spec()),
        scratch_shapes=[
            pltpu.SemaphoreType.DMA((8,)),
            pltpu.SemaphoreType.DMA((8,)),
            pltpu.SemaphoreType.DMA,
        ],
        compiler_params=params(3),
    )(rows, left, right)


def sum_small_kernel(terms, earlier, out, mine, came, send, recv, send_back, recv_back):
    me = lax.axis_index("seq")
    greet(PEERS)
    mine[...] = terms[...].astype(low)
    started = []
    for mask in PEERS:
        copy = remote(mine.at[me ^ mask], came.at[mask], send.at[mask], recv.at[mask], me ^ mask)
        copy.start()
        started.append(copy)
    total = terms[me].astype(wide)
    for mask in PEERS:
        remote(mine.at[0], came.at[mask], send.at[mask], recv.at[mask], me ^ mask).wait_recv()
        total = total + came[mask].astype(wide)
    out[me] = total.astype(low)
    for mask in PEERS:
        copy = remote(out.at[me], out.at[me], send_back.at[mask], recv_back.at[mask], me ^ mask)
        copy.start()
        started.append(copy)
    for mask in PEERS:
        remote(mine.at[0], out.at[me ^ mask], send_back.at[mask], recv_back.at[mask], me ^ mask).wait_recv()
    for copy in started:
        copy.wait_send()


def sum_small(terms, collective_id, earlier=None):
    count, width = terms.shape
    earlier = terms if earlier is None else earlier
    blocks = (8, count // 8, width)
    return pl.pallas_call(
        sum_small_kernel,
        out_shape=jax.ShapeDtypeStruct(blocks, low),
        in_specs=[vmem_spec(), any_spec()],
        out_specs=vmem_spec(),
        scratch_shapes=[pltpu.VMEM(blocks, low), pltpu.VMEM(blocks, low)]
        + [pltpu.SemaphoreType.DMA((8,))] * 4,
        compiler_params=params(collective_id),
    )(terms.reshape(blocks), earlier).reshape(count, width)


def merge_parts_kernel(terms, stats, out, logsum, came, came_stats, send, recv, send_st, recv_st, back, recv_back, back_st, recv_back_st):
    me = lax.axis_index("seq")
    width = out.shape[2]
    greet(PEERS)
    started = []
    for mask in PEERS:
        for src, dst, s, r in ((stats, came_stats, send_st, recv_st), (terms, came, send, recv)):
            copy = remote(src.at[me ^ mask], dst.at[mask], s.at[mask], r.at[mask], me ^ mask)
            copy.start()
            started.append(copy)
    for mask in PEERS:
        remote(stats.at[0], came_stats.at[mask], send_st.at[mask], recv_st.at[mask], me ^ mask).wait_recv()
    tops = [stats[me, 0]] + [came_stats[mask, 0] for mask in PEERS]
    sums = [stats[me, 1]] + [came_stats[mask, 1] for mask in PEERS]
    top = functools.reduce(jnp.maximum, tops)
    weights = [s * jnp.exp(t - top) for t, s in zip(tops, sums)]
    total = functools.reduce(jnp.add, weights)
    logsum[me] = top + jnp.log(total)
    size = width // HEADS
    spread = (
        lax.broadcasted_iota(jnp.int32, (128, width), 1) // size
        == lax.broadcasted_iota(jnp.int32, (128, width), 0)
    ).astype(wide)
    scaled = jnp.concatenate([w / total for w in weights], 0)
    scaled = lax.dot_general(
        scaled, spread, (((1,), (0,)), ((), ())), precision=lax.Precision.HIGHEST, preferred_element_type=wide
    )
    rows = tops[0].shape[0]
    result = scaled[:rows] * terms[me].astype(wide)
    for place, mask in enumerate(PEERS):
        remote(terms.at[0], came.at[mask], send.at[mask], recv.at[mask], me ^ mask).wait_recv()
        result = result + scaled[(place + 1) * rows : (place + 2) * rows] * came[mask].astype(wide)
    out[me] = result.astype(low)
    for mask in PEERS:
        for ref, s, r in ((out, back, recv_back), (logsum, back_st, recv_back_st)):
            copy = remote(ref.at[me], ref.at[me], s.at[mask], r.at[mask], me ^ mask)
            copy.start()
            started.append(copy)
    for mask in PEERS:
        for ref, s, r in ((out, back, recv_back), (logsum, back_st, recv_back_st)):
            remote(ref.at[me], ref.at[me ^ mask], s.at[mask], r.at[mask], me ^ mask).wait_recv()
    for copy in started:
        copy.wait_send()


def merge_parts(terms, tops, sums):
    count, width = terms.shape
    rows = count // 8
    stats = jnp.stack([tops.reshape(8, rows, 128), sums.reshape(8, rows, 128)], 1)
    out, logsum = pl.pallas_call(
        merge_parts_kernel,
        out_shape=(
            jax.ShapeDtypeStruct((8, rows, width), low),
            jax.ShapeDtypeStruct((8, rows, 128), wide),
        ),
        in_specs=[vmem_spec()] * 2,
        out_specs=(vmem_spec(), vmem_spec()),
        scratch_shapes=[pltpu.VMEM((8, rows, width), low), pltpu.VMEM((8, 2, rows, 128), wide)]
        + [pltpu.SemaphoreType.DMA((8,))] * 8,
        compiler_params=params(5),
    )(terms.reshape(8, rows, width), stats)
    return out.reshape(count, width), logsum.reshape(count, 128)


def finish_kernel(
    size, rows, grads, weights, vectors, joined, feed, middle, out, out_line, out_joined, out_turned, out_straight, out_middle,
    terms, sib, pair, came, blocks, came_blocks, line,
    send, recv, send_pair, recv_pair, send_block, recv_block,
    line_came, line_sent, send_line, recv_line, join_came, join_sent, send_join, recv_join,
):
    me = lax.axis_index("seq")
    mine = me // 4
    count = out.shape[1]
    width = grads.shape[1]
    cut = blocks.shape[1] - 16
    quarter = width // 3
    greet(PEERS, size)
    other = Line(size, 4, joined, join_came, join_sent, send_join, recv_join)
    other.begin()
    own = Line(size, 7, line, line_came, line_sent, send_line, recv_line)

    d = grads[...]

    def block_copy(mask):
        return remote(
            blocks.at[me ^ mask], came_blocks.at[mask], send_block.at[mask], recv_block.at[mask], me ^ mask
        )

    for mask in (6, 2, 4, 0):
        first = ((me ^ mask) // 2) * 2
        columns = pl.ds(pl.multiple_of(first * cut, 2 * cut), 2 * cut)
        both = tn(rows[:, columns], d).astype(low)
        for place in range(2):
            blocks[first + place, :cut] = both[place * cut : (place + 1) * cut]
            blocks[first + place, cut:] = vectors[first + place]
        if mask:
            block_copy(mask).start()
        block_copy(mask + 1).start()
    chips = (6, 2, 4, 0)

    def term(owner):
        return nt(grads[pl.ds(pl.multiple_of(owner * count, count), count)], weights[...])

    def sib_copy(slot):
        return remote(terms.at[slot], sib.at[slot], send.at[slot], recv.at[slot], me ^ 1)

    def pair_copy(slot):
        return remote(pair.at[slot], came.at[slot], send_pair.at[slot], recv_pair.at[slot], me ^ chips[slot])

    for slot, mask in enumerate(chips):
        terms[slot] = term(me ^ 1 ^ mask).astype(low)
        sib_copy(slot).start()
    for slot, mask in enumerate(chips):
        here = term(me ^ mask)
        sib_copy(slot).wait_recv()
        here = here + sib[slot].astype(wide)
        if mask:
            pair[slot] = here.astype(low)
            pair_copy(slot).start()
        else:
            out[mine] = here

    other.rest(0)

    half = out_straight.shape[0]
    out_turned[...] = feed[:half].astype(wide).T
    out_straight[...] = feed[half:].astype(wide)
    out_middle[...] = middle[...].astype(wide)

    for mask in PEERS:
        block_copy(mask).wait_recv()
    came_blocks[0] = blocks[me]

    def came_from(owner, part):
        return came_blocks[owner ^ me, part].astype(wide)

    total = jnp.zeros((16, width), wide)
    for source in range(4):
        both = came_from(source, pl.ds(0, cut)) + came_from(source + 4, pl.ds(0, cut))
        for kind in range(3):
            line[kind * cut : (kind + 1) * cut, source * quarter : (source + 1) * quarter] = both[
                :, kind * quarter : (kind + 1) * quarter
            ].astype(low)
        total = total + came_from(source, pl.ds(cut, 16)) + came_from(source + 4, pl.ds(cut, 16))
    line[3 * cut :] = jnp.zeros_like(line[3 * cut :])
    line[3 * cut : 3 * cut + 16, :width] = total.astype(low)

    own.begin()
    own.rest(0)
    for slot in (1, 2, 0):
        pair_copy(slot).wait_recv()
    out[mine] += came[1].astype(wide)
    out[1 - mine] = came[2].astype(wide) + came[0].astype(wide)

    out_line[...] = own.total()
    out_joined[...] = other.total()
    for mask in PEERS:
        block_copy(mask).wait_send()
    for slot in range(4):
        sib_copy(slot).wait_send()
    for slot in range(3):
        pair_copy(slot).wait_send()
    own.end()
    other.end()


def finish(rows, grads, weights, vectors, joined, feed, middle):
    width = rows.shape[1]
    count = rows.shape[0] // 8
    cut = width // 8
    line = (3 * cut + 64, width)
    blocks = (8, cut + 16, grads.shape[1])
    four, three = pltpu.SemaphoreType.DMA((4,)), pltpu.SemaphoreType.DMA((3,))
    return pl.pallas_call(
        functools.partial(finish_kernel, lax.axis_size("dp")),
        out_shape=(
            jax.ShapeDtypeStruct((2, count, width), wide),
            jax.ShapeDtypeStruct(line, wide),
            jax.ShapeDtypeStruct(joined.shape, wide),
            jax.ShapeDtypeStruct((width, feed.shape[0] // 2), wide),
            jax.ShapeDtypeStruct((feed.shape[0] // 2, width), wide),
            jax.ShapeDtypeStruct(middle.shape, wide),
        ),
        in_specs=[vmem_spec()] * 7,
        out_specs=(vmem_spec(),) * 6,
        scratch_shapes=[
            pltpu.VMEM((4, count, width), low),
            pltpu.VMEM((4, count, width), low),
            pltpu.VMEM((3, count, width), low),
            pltpu.VMEM((3, count, width), low),
            pltpu.VMEM(blocks, low),
            pltpu.VMEM(blocks, low),
            pltpu.VMEM(line, low),
            four,
            four,
            three,
            three,
        ]
        + [pltpu.SemaphoreType.DMA((8,))] * 2
        + line_scratch(line, 7)
        + line_scratch(joined.shape, 4),
        compiler_params=params(6),
    )(rows, grads, weights, vectors, joined, feed, middle)


def plain(**more):
    return pltpu.CompilerParams(vmem_limit_bytes=VMEM_BYTES, **more)


def flash_forward_kernel(length, queries, keys, values, context, logsum, scores, probs):
    rows, width = queries.shape
    count = keys.shape[0]
    heads = width // 64
    strip = 16
    of_head = lane_head((1, width), 64)
    q = queries[...] * jnp.asarray(0.125, low)
    k = keys[...]
    v = values[...]
    total = jnp.zeros((rows, width), wide)
    logs = jnp.zeros((rows, 128), wide)
    lanes = lax.broadcasted_iota(jnp.int32, (1, 128), 1)
    fill = jnp.where(lax.broadcasted_iota(jnp.int32, (1, count), 1) < length[0], 0.0, masked_fill)
    for head in range(heads):
        slot = head % 2
        scores[slot] = nt(jnp.where(of_head == head, q, jnp.zeros_like(q)), k)
        tops, sums = [], []
        for start in range(0, rows, strip):
            part = scores[slot, start : start + strip] + fill
            top = jnp.max(part, -1, keepdims=True)
            weights = jnp.exp(part - top)
            tops.append(top)
            sums.append(jnp.sum(weights, -1, keepdims=True))
            probs[slot, start : start + strip] = weights.astype(low)
        top, summed = jnp.concatenate(tops, 0), jnp.concatenate(sums, 0)
        total = jnp.where(of_head == head, nn(probs[slot], v) * (1.0 / summed), total)
        logs = jnp.where(lanes == head, top + jnp.log(summed), logs)
    context[...] = total.astype(low)
    logsum[...] = logs


def flash_forward(length, three, block):
    count, width = three.shape[0], three.shape[1] // 3
    return pl.pallas_call(
        flash_forward_kernel,
        out_shape=(
            jax.ShapeDtypeStruct((count, width), low),
            jax.ShapeDtypeStruct((count, 128), wide),
        ),
        grid_spec=pltpu.PrefetchScalarGridSpec(
            num_scalar_prefetch=1,
            grid=(count // block,),
            in_specs=[
                pl.BlockSpec((block, width), lambda i, n: (i, 0)),
                pl.BlockSpec((count, width), lambda i, n: (0, 1)),
                pl.BlockSpec((count, width), lambda i, n: (0, 2)),
            ],
            out_specs=[
                pl.BlockSpec((block, width), lambda i, n: (i, 0)),
                pl.BlockSpec((block, 128), lambda i, n: (i, 0)),
            ],
            scratch_shapes=[pltpu.VMEM((2, block, count), wide), pltpu.VMEM((2, block, count), low)],
        ),
        compiler_params=plain(),
    )(length, three, three, three)


def flash_backward_kernel(chunk, length, queries, grads, logsum, delta, keys, keys_t, values, out, q_stack, g_stack, p_stack, s_stack, k_sum, v_sum):
    step = pl.program_id(0)
    rows, width = queries.shape
    count = keys.shape[0]
    heads = width // 64
    of_head = lane_head((1, width), 64)

    @pl.when(step == 0)
    def _():
        k_sum[...] = jnp.zeros_like(k_sum)
        v_sum[...] = jnp.zeros_like(v_sum)

    q = queries[...] * jnp.asarray(0.125, low)
    g = grads[...]
    for head in range(heads):
        place = pl.ds(head * rows, rows)
        q_stack[place] = jnp.where(of_head == head, q, jnp.zeros_like(q))
        g_stack[place] = jnp.where(of_head == head, g, jnp.zeros_like(g))
    dq_sums = [jnp.zeros((64, rows), wide)] * heads
    for start in range(0, count, chunk):
        part = pl.ds(start, chunk)
        k = keys[part]
        v = values[part]
        allowed = start + lax.broadcasted_iota(jnp.int32, (chunk, 1), 0) < length[0]
        fill = jnp.where(allowed, 0.0, masked_fill)
        for head in range(heads):
            place = pl.ds(head * rows, rows)
            scores = nt(k, q_stack[place])
            probs = jnp.exp(scores - logsum[head : head + 1, :] + fill)
            p_stack[:, place] = probs.astype(low)
            d_probs = nt(v, g_stack[place])
            d_scores = (probs * (d_probs - delta[head : head + 1, :])).astype(low)
            s_stack[:, place] = d_scores
            dq_sums[head] = dq_sums[head] + nn(keys_t[head * 64 : head * 64 + 64, part], d_scores)
        v_sum[part] += nn(p_stack[...], g_stack[...])
        k_sum[part] += nn(s_stack[...], q_stack[...])
    dq = jnp.concatenate(dq_sums, 0) * 0.125
    out[pl.ds(pl.multiple_of(step * rows, rows), rows), 0:width] = dq.T.astype(low)

    @pl.when(step == pl.num_programs(0) - 1)
    def _():
        out[:, width : 2 * width] = k_sum[...].astype(low)
        out[:, 2 * width : 3 * width] = v_sum[...].astype(low)


def flash_backward(length, three, grads, logsum, delta, block, chunk):
    count, width = grads.shape
    heads = width // 64
    return pl.pallas_call(
        functools.partial(flash_backward_kernel, chunk),
        out_shape=jax.ShapeDtypeStruct((count, 3 * width), low),
        grid_spec=pltpu.PrefetchScalarGridSpec(
            num_scalar_prefetch=1,
            grid=(count // block,),
            in_specs=[
                pl.BlockSpec((block, width), lambda i, n: (i, 0)),
                pl.BlockSpec((block, width), lambda i, n: (i, 0)),
                pl.BlockSpec((heads, block), lambda i, n: (0, i)),
                pl.BlockSpec((heads, block), lambda i, n: (0, i)),
                pl.BlockSpec((count, width), lambda i, n: (0, 1)),
                pl.BlockSpec((width, count), lambda i, n: (0, 0)),
                pl.BlockSpec((count, width), lambda i, n: (0, 2)),
            ],
            out_specs=pl.BlockSpec((count, 3 * width), lambda i, n: (0, 0)),
            scratch_shapes=[
                pltpu.VMEM((heads * block, width), low),
                pltpu.VMEM((heads * block, width), low),
                pltpu.VMEM((chunk, heads * block), low),
                pltpu.VMEM((chunk, heads * block), low),
                pltpu.VMEM((count, width), wide),
                pltpu.VMEM((count, width), wide),
            ],
        ),
        compiler_params=plain(),
    )(length, three, grads, logsum, delta, three, three[:, width : 2 * width].T, three)


def small_forward_kernel(causal, length, queries, keys, values, context, tops, sums):
    table = pl.program_id(0)
    rows, width = queries.shape
    count = keys.shape[0]
    half = lane_head((1, 128), 64)
    lanes = lax.broadcasted_iota(jnp.int32, (1, 128), 1)
    allowed = lax.broadcasted_iota(jnp.int32, (rows, count), 1) < length[table]
    if causal:
        allowed = allowed & (
            lax.broadcasted_iota(jnp.int32, (rows, count), 1)
            <= lax.broadcasted_iota(jnp.int32, (rows, count), 0)
        )
    top_all = jnp.zeros((rows, 128), wide)
    sum_all = jnp.ones((rows, 128), wide)
    for two in range(width // 128):
        place = pl.ds(two * 128, 128)
        q = queries[:, place] * jnp.asarray(0.125, low)
        k = keys[:, place]
        v = values[:, place]
        total = jnp.zeros((rows, 128), wide)
        for side in range(2):
            scores = nt(jnp.where(half == side, q, jnp.zeros_like(q)), k)
            scores = jnp.where(allowed, scores, masked_fill)
            top = jnp.max(scores, -1, keepdims=True)
            weights = jnp.exp(scores - top)
            summed = jnp.sum(weights, -1, keepdims=True)
            probs = (weights * (1.0 / summed)).astype(low)
            total = jnp.where(half == side, nn(probs, v), total)
            top_all = jnp.where(lanes == 2 * two + side, top, top_all)
            sum_all = jnp.where(lanes == 2 * two + side, summed, sum_all)
        context[:, place] = total.astype(low)
    tops[...] = top_all
    sums[...] = sum_all


def small_forward(length, queries, keys, values, causal):
    tables = length.shape[0]
    rows, width = queries.shape[0] // tables, queries.shape[1]
    count = keys.shape[0] // tables

    def block(size, last):
        return pl.BlockSpec((size, last), lambda t, n: (t, 0))

    return pl.pallas_call(
        functools.partial(small_forward_kernel, causal),
        out_shape=(
            jax.ShapeDtypeStruct(queries.shape, low),
            jax.ShapeDtypeStruct((queries.shape[0], 128), wide),
            jax.ShapeDtypeStruct((queries.shape[0], 128), wide),
        ),
        grid_spec=pltpu.PrefetchScalarGridSpec(
            num_scalar_prefetch=1,
            grid=(tables,),
            in_specs=[block(rows, width), block(count, width), block(count, width)],
            out_specs=[block(rows, width), block(rows, 128), block(rows, 128)],
        ),
        compiler_params=plain(),
    )(length, queries, keys, values)


def small_backward_kernel(causal, length, queries, keys, values, grads, context, logsum, earlier, dq, dk, dv):
    table = pl.program_id(0)
    rows, width = queries.shape
    count = keys.shape[0]
    half = lane_head((1, 128), 64)
    allowed = lax.broadcasted_iota(jnp.int32, (rows, count), 1) < length[table]
    if causal:
        allowed = allowed & (
            lax.broadcasted_iota(jnp.int32, (rows, count), 1)
            <= lax.broadcasted_iota(jnp.int32, (rows, count), 0)
        )
    logs = logsum[...]
    for two in range(width // 128):
        place = pl.ds(two * 128, 128)
        q = queries[:, place] * jnp.asarray(0.125, low)
        k = keys[:, place]
        v = values[:, place]
        g = grads[:, place]
        both = g.astype(wide) * context[:, place].astype(wide)
        dq_here = jnp.zeros((rows, 128), wide)
        dk_here = jnp.zeros((count, 128), wide)
        dv_here = jnp.zeros((count, 128), wide)
        for side in range(2):
            head = 2 * two + side
            q_one = jnp.where(half == side, q, jnp.zeros_like(q))
            g_one = jnp.where(half == side, g, jnp.zeros_like(g))
            delta = jnp.sum(jnp.where(half == side, both, 0.0), -1, keepdims=True)
            scores = nt(q_one, k)
            probs = jnp.where(allowed, jnp.exp(scores - logs[:, head : head + 1]), 0.0)
            d_probs = nt(g_one, v)
            d_scores = (probs * (d_probs - delta)).astype(low)
            dq_here = jnp.where(half == side, nn(d_scores, k), dq_here)
            dk_here = dk_here + tn(d_scores, q_one)
            dv_here = dv_here + tn(probs.astype(low), g_one)
        dq[:, place] = dq_here * 0.125
        dk[:, place] = dk_here.astype(low)
        dv[:, place] = dv_here.astype(low)


def small_backward(length, queries, keys, values, grads, context, logsum, causal, earlier):
    tables = length.shape[0]
    rows, width = queries.shape[0] // tables, queries.shape[1]
    count = keys.shape[0] // tables

    def block(size, last):
        return pl.BlockSpec((size, last), lambda t, n: (t, 0))

    return pl.pallas_call(
        functools.partial(small_backward_kernel, causal),
        out_shape=(
            jax.ShapeDtypeStruct(queries.shape, wide),
            jax.ShapeDtypeStruct(keys.shape, low),
            jax.ShapeDtypeStruct(keys.shape, low),
        ),
        grid_spec=pltpu.PrefetchScalarGridSpec(
            num_scalar_prefetch=1,
            grid=(tables,),
            in_specs=[
                block(rows, width),
                block(count, width),
                block(count, width),
                block(rows, width),
                block(rows, width),
                block(rows, 128),
                any_spec(),
            ],
            out_specs=[block(rows, width), block(count, width), block(count, width)],
        ),
        compiler_params=plain(),
    )(length, queries, keys, values, grads, context, logsum, earlier)


def gelu_parts(values):
    bell = 0.5 * (1.0 + lax.erf(values * 0.7071067811865476))
    slope = bell + values * (0.3989422804014327 * jnp.exp(-0.5 * values * values))
    return values * bell, slope


def feed_forward_kernel(rows, expand, contract, out):
    hidden = nn(rows[...], expand[0])
    act = (hidden * (0.5 * (1.0 + lax.erf(hidden * 0.7071067811865476)))).astype(low)
    term = nn(act, contract[0])

    @pl.when(pl.program_id(0) == 0)
    def _():
        out[...] = term

    @pl.when(pl.program_id(0) > 0)
    def _():
        out[...] += term


def feed_forward(rows, expand, contract):
    count, width = rows.shape
    parts, _, hidden = expand.shape
    return pl.pallas_call(
        feed_forward_kernel,
        out_shape=jax.ShapeDtypeStruct((count, width), wide),
        grid=(parts,),
        in_specs=[
            pl.BlockSpec((count, width), lambda j: (0, 0)),
            pl.BlockSpec((1, width, hidden), lambda j: (j, 0, 0)),
            pl.BlockSpec((1, hidden, width), lambda j: (j, 0, 0)),
        ],
        out_specs=pl.BlockSpec((count, width), lambda j: (0, 0)),
        compiler_params=plain(),
    )(rows, expand, contract)


def outer_kernel(order, earlier, rows, *refs):
    *grads, away, kept = refs
    step = pl.program_id(0)
    half = pl.num_programs(0) // 2
    size = rows.shape[1]
    for place, grad in enumerate(grads):
        term = tn(rows[...], grad[...]).astype(low)

        @pl.when(step < half)
        def _(place=place, term=term):
            away[0, place * size : (place + 1) * size] = term

        @pl.when(step >= half)
        def _(place=place, term=term):
            kept[0, place * size : (place + 1) * size] = term


def outer_by_owner(order, earlier, rows, *grads):
    count, width = rows.shape
    parts = order.shape[0]
    half, size = parts // 2, width // parts
    shape = jax.ShapeDtypeStruct((half, len(grads) * size, width), low)
    return pl.pallas_call(
        outer_kernel,
        out_shape=(shape, shape),
        grid_spec=pltpu.PrefetchScalarGridSpec(
            num_scalar_prefetch=1,
            grid=(parts,),
            in_specs=[any_spec(), pl.BlockSpec((count, size), lambda j, o: (0, o[j]))]
            + [pl.BlockSpec((count, width), lambda j, o: (0, 0))] * len(grads),
            out_specs=[
                pl.BlockSpec((1,) + shape.shape[1:], lambda j, o: (jnp.minimum(j, half - 1), 0, 0)),
                pl.BlockSpec((1,) + shape.shape[1:], lambda j, o: (jnp.maximum(j - half, 0), 0, 0)),
            ],
        ),
        compiler_params=plain(),
    )(order, earlier, rows, *grads)


def feed_backward_kernel(rows, grads, expand, contract, earlier, out, d_both, expand_sum, contract_sum):
    step = pl.program_id(0)
    x = rows[0]
    g = grads[0]
    act, slope = gelu_parts(nn(x, expand[...]))
    d_hidden = (nt(g, contract[...]) * slope).astype(low)
    out[0] = nt(d_hidden, expand[...]).astype(low)
    one = tn(d_hidden, x)
    two = tn(act.astype(low), g)

    @pl.when(step == 0)
    def _():
        expand_sum[...] = one
        contract_sum[...] = two

    @pl.when(step > 0)
    def _():
        expand_sum[...] += one
        contract_sum[...] += two

    @pl.when(step == pl.num_programs(0) - 1)
    def _():
        d_both[: expand_sum.shape[0]] = expand_sum[...].astype(low)
        d_both[expand_sum.shape[0] :] = contract_sum[...].astype(low)


def feed_backward(rows, grads, expand, contract, earlier):
    parts, count, width = rows.shape
    hidden = contract.shape[0]
    return pl.pallas_call(
        feed_backward_kernel,
        out_shape=(jax.ShapeDtypeStruct(rows.shape, low), jax.ShapeDtypeStruct((2 * hidden, width), low)),
        grid=(parts,),
        in_specs=[
            pl.BlockSpec((1, count, width), lambda j: (j, 0, 0)),
            pl.BlockSpec((1, count, width), lambda j: (j, 0, 0)),
            pl.BlockSpec((width, hidden), lambda j: (0, 0)),
            pl.BlockSpec((hidden, width), lambda j: (0, 0)),
            any_spec(),
        ],
        out_specs=[
            pl.BlockSpec((1, count, width), lambda j: (j, 0, 0)),
            pl.BlockSpec((2 * hidden, width), lambda j: (0, 0)),
        ],
        scratch_shapes=[pltpu.VMEM((hidden, width), wide)] * 2,
        compiler_params=plain(),
    )(rows, grads, expand, contract, earlier)


def swap(array, mask):
    return lax.ppermute(array, "seq", [(i, i ^ mask) for i in range(8)])


def add_kernel(left, right, earlier, out):
    out[...] = add_low(left[...], right[...])


def add_after(left, right, earlier):
    return pl.pallas_call(
        add_kernel,
        out_shape=jax.ShapeDtypeStruct(left.shape, low),
        in_specs=[vmem_spec()] * 2 + [any_spec()],
        out_specs=vmem_spec(),
        compiler_params=plain(),
    )(left, right, earlier)


def scatter_cores(away, kept, earlier):
    return add_after(kept, swap(away, 1), earlier)


def scatter_first(both):
    half = both.shape[1] // 2
    one, two = both[:, :half], both[:, half:]
    one_came = swap(jnp.stack([one[0], one[2]]), 2)
    two_came = swap(jnp.stack([two[1], two[2]]), 4)
    return (
        add_low(one[3], one_came[0]),
        add_low(one[1], one_came[1]),
        add_low(two[3], two_came[0]),
        add_low(two[0], two_came[1]),
    )


def scatter_second(parts):
    one, one_far, two, two_far = parts
    return add_low(one, swap(one_far, 4)), add_low(two, swap(two_far, 2))


def plane_body(
    source_tokens,
    target_tokens,
    source_lengths,
    target_lengths,
    encoder_query,
    encoder_key,
    encoder_value,
    encoder_mix,
    attend_gain,
    attend_shift,
    encoder_expand,
    encoder_contract,
    encoder_gain,
    encoder_shift,
    decoder_query,
    decoder_key,
    decoder_value,
    decoder_mix,
    self_gain,
    self_shift,
    cross_query,
    cross_key,
    cross_value,
    cross_mix,
    cross_gain,
    cross_shift,
    decoder_expand,
    decoder_contract,
    decoder_gain,
    decoder_shift,
    source_cotangent,
    target_cotangent,
):
    slots, tables, width = source_tokens.shape
    places = target_tokens.shape[0]
    me = lax.axis_index("seq")
    quarter = width // 4
    slice_rows = width // 8

    def flat(array):
        return jnp.swapaxes(array, 0, 1).reshape(-1, width)

    def unflat(array):
        return jnp.swapaxes(array.reshape(tables, -1, width), 0, 1)

    def columns(weight):
        return lax.dynamic_slice_in_dim(weight, (me % 4) * quarter, quarter, 1)

    def own(rows):
        return lax.dynamic_slice_in_dim(rows, me * slice_rows, slice_rows, 1)

    def own_places(rows):
        return lax.dynamic_slice_in_dim(rows.reshape(tables, 8 * places, width), me * places, places, 1)

    def own_vector(vector):
        return lax.dynamic_slice_in_dim(vector, me * slice_rows, slice_rows, 0)

    source_flat = flat(source_tokens)
    all_expand = lax.all_gather(encoder_expand, "seq", axis=0)
    all_contract = lax.all_gather(encoder_contract, "seq", axis=0)
    target_pair = jnp.stack([jnp.swapaxes(target_tokens, 0, 1), jnp.swapaxes(target_cotangent, 0, 1)], 0)
    rows, target_all = gather_table(source_flat.reshape(tables, slots, width), target_pair.reshape(-1, width))
    rows = rows.reshape(-1, width)
    target_all = jnp.moveaxis(target_all.reshape(8, 2, tables, places, width), 0, 2).reshape(2, -1, width)
    target_flat, target_grad = target_all[0], target_all[1]
    w_three = jnp.concatenate([columns(encoder_query), columns(encoder_key), columns(encoder_value)], 1)
    length = lax.dynamic_slice_in_dim(source_lengths, me // 4, 1, 0)
    three = project(rows, w_three).astype(low)
    context, logsum = flash_forward(length, three, 512)
    encoder_context = heads_to_rows(context.reshape(8, slots, quarter)).reshape(-1, width)
    first, first_back = jax.vjp(
        layer_norm, source_flat.astype(wide) + project(encoder_context, encoder_mix), attend_gain, attend_shift
    )
    first_low = first.astype(low)
    widened = feed_forward(first_low, all_expand, all_contract)
    first_all = lax.all_gather(first_low, "seq", axis=0)
    second, second_back = jax.vjp(layer_norm, first + widened, encoder_gain, encoder_shift)
    encoded = second.astype(low)

    self_queries = project(target_flat, decoder_query).astype(low)
    self_keys = project(target_flat, decoder_key).astype(low)
    self_values = project(target_flat, decoder_value).astype(low)
    decoder_context, self_tops, self_sums = small_forward(
        target_lengths, self_queries, self_keys, self_values, True
    )
    self_logs = self_tops + jnp.log(self_sums)
    third, third_back = jax.vjp(
        layer_norm, target_flat.astype(wide) + project(decoder_context, decoder_mix), self_gain, self_shift
    )
    third_low = third.astype(low)
    cross_queries = project(third_low, cross_query).astype(low)

    cross_keys = project(encoded, cross_key).astype(low)
    cross_values = project(encoded, cross_value).astype(low)
    here = source_lengths - me * slots
    part, part_tops, part_sums = small_forward(here, cross_queries, cross_keys, cross_values, False)
    cross_context, cross_logs = merge_parts(part, part_tops, part_sums)
    fourth, fourth_back = jax.vjp(
        layer_norm, third + project(cross_context, cross_mix), cross_gain, cross_shift
    )
    fourth_low = fourth.astype(low)
    hidden = project(fourth_low, decoder_expand)
    decoder_acts, gelu_back = jax.vjp(gelu_exact, hidden)
    decoder_acts = decoder_acts.astype(low)
    narrowed = sum_small(project(decoder_acts, decoder_contract), 4, first_all).astype(wide)
    fifth, fifth_back = jax.vjp(layer_norm, fourth + narrowed, decoder_gain, decoder_shift)
    decoded = jnp.swapaxes(own_places(fifth.astype(low)), 0, 1)

    d_fifth, grad_decoder_gain, grad_decoder_shift = fifth_back(target_grad.astype(wide))
    fifth_low = d_fifth.astype(low)
    d_hidden = gelu_back(project_back(fifth_low, decoder_contract))[0].astype(low)
    eighth = fourth_low.shape[0] // 8
    decoder_pair = jnp.stack(
        [lax.dynamic_slice_in_dim(array, me * eighth, eighth, 0) for array in (fourth_low, fifth_low)], 0
    )
    decoder_pair = lax.all_gather(decoder_pair, ("dp", "seq"), axis=0)
    def over_tables(terms):
        part = lax.psum_scatter(terms, "dp", scatter_dimension=0, tiled=True)
        return lax.all_gather(part, "dp", axis=0, tiled=True)

    def join(arrays):
        return jnp.concatenate([a.astype(low) for a in arrays], 0)

    d_rows = sum_small(project_back(d_hidden, decoder_expand), 10).astype(wide)
    d_fourth, grad_cross_gain, grad_cross_shift = fourth_back(d_fifth + d_rows)
    cross_low = d_fourth.astype(low)
    grad_cross_mix = outer_sum(own(cross_context), cross_low)
    d_cross = project_back(cross_low, cross_mix).astype(low)
    dq_part, dk_cross, dv_cross = small_backward(
        here, cross_queries, cross_keys, cross_values, d_cross, cross_context, cross_logs, False, cross_logs
    )
    d_encoded = project_back(dk_cross, cross_key) + project_back(dv_cross, cross_value)
    order = me ^ jnp.array(OWNERS, jnp.int32)


    d_second, grad_encoder_gain, grad_encoder_shift = second_back(flat(source_cotangent).astype(wide) + d_encoded)
    d_second_low = d_second.astype(low)
    d_all = lax.all_gather(d_second_low, "seq", axis=0)
    dq_cross = sum_small(dq_part, 11, d_second_low)
    cross_away, cross_kept = outer_by_owner(order, decoder_pair, encoded, dk_cross, dv_cross)
    grad_cross_query = outer_sum(own(third_low), dq_cross)
    d_third, grad_self_gain, grad_self_shift = third_back(d_fourth + project_back(dq_cross, cross_query))
    self_low = d_third.astype(low)
    grad_decoder_mix = outer_sum(own(decoder_context), self_low)
    dq_self, dk_self, dv_self = small_backward(
        target_lengths,
        self_queries,
        self_keys,
        self_values,
        project_back(self_low, decoder_mix).astype(low),
        decoder_context,
        self_logs,
        True,
        cross_away,
    )
    dq_self = dq_self.astype(low)
    target_own = own(target_flat)
    grad_decoder_query = outer_sum(target_own, dq_self)
    grad_decoder_key = outer_sum(target_own, dk_self)
    grad_decoder_value = outer_sum(target_own, dv_self)
    grad_target = own_places(
        d_third
        + project_back(dq_self, decoder_query)
        + project_back(dk_self, decoder_key)
        + project_back(dv_self, decoder_value)
    )
    grad_target = jnp.swapaxes(grad_target, 0, 1)

    decoder_vectors = jnp.stack(
        [
            own_vector(v)
            for v in (
                grad_self_gain,
                grad_self_shift,
                grad_cross_gain,
                grad_cross_shift,
                grad_decoder_gain,
                grad_decoder_shift,
            )
        ],
        0,
    )
    decoder_vectors = jnp.pad(decoder_vectors.reshape(1, -1), ((0, 15), (0, width - 6 * slice_rows)))
    middle = [
        grad_decoder_query,
        grad_decoder_key,
        grad_decoder_value,
        grad_decoder_mix,
        grad_cross_query,
        grad_cross_mix,
        decoder_vectors,
    ]
    middle_join = join(middle + [jnp.zeros((48, width), low)])
    middle_sum = over_tables(middle_join)
    d_terms, feed_join = feed_backward(first_all, d_all, encoder_expand, encoder_contract, dq_self)
    feed_sum = over_tables(feed_join)
    cross_both = scatter_cores(cross_away, cross_kept, feed_join)
    d_rows, grad_decoder_expand, grad_decoder_contract = scatter_plane(
        d_terms, decoder_pair, decoder_expand, decoder_contract
    )
    d_first, grad_attend_gain, grad_attend_shift = first_back(d_second + d_rows)
    encoder_low = d_first.astype(low)
    d_context, mix_away, mix_kept = rows_to_heads(
        project_back(encoder_low, encoder_mix).astype(low).reshape(tables, slots, width), encoder_context, encoder_low
    )
    mix_both = scatter_cores(mix_away, mix_kept, d_context)
    d_context = d_context.reshape(-1, quarter)
    delta = jnp.sum(
        (d_context.astype(wide) * context.astype(wide)).reshape(-1, quarter // 64, 64), -1
    )
    d_three = flash_backward(length, three, d_context, logsum[:, : quarter // 64].T, delta.T, 512, 1024)
    vectors = jnp.stack(
        [grad_attend_gain, grad_attend_shift, grad_encoder_gain, grad_encoder_shift], 0
    ).astype(low)
    vectors = jnp.swapaxes(vectors.reshape(4, 8, slice_rows), 0, 1)
    vectors = jnp.pad(vectors, ((0, 0), (0, 12), (0, 3 * quarter - slice_rows)))
    parts = scatter_second(scatter_first(mix_both)) + scatter_second(scatter_first(cross_both))
    d_source, line, plane_sum, grad_encoder_expand, grad_encoder_contract, middle_wide = finish(
        rows, d_three, w_three, vectors, join(parts), feed_sum, middle_sum
    )
    grad_source = unflat(d_first + d_source.reshape(-1, width))
    encoder_three = line[: 3 * slice_rows].reshape(3, slice_rows, width)
    encoder_vectors = line[3 * slice_rows : 3 * slice_rows + 4, :slice_rows]
    plane_three = plane_sum.reshape(3, slice_rows, width)
    six = middle_wide[: 6 * slice_rows].reshape(6, slice_rows, width)
    decoder_vectors = middle_wide[6 * slice_rows : 6 * slice_rows + 1]
    decoder_vectors = decoder_vectors[0, : 6 * slice_rows].reshape(6, slice_rows)
    return (
        unflat(encoded),
        decoded,
        grad_source,
        grad_target,
        encoder_three[0],
        encoder_three[1],
        encoder_three[2],
        plane_three[0],
        encoder_vectors[0],
        encoder_vectors[1],
        grad_encoder_expand,
        grad_encoder_contract,
        encoder_vectors[2],
        encoder_vectors[3],
        six[0],
        six[1],
        six[2],
        six[3],
        decoder_vectors[0],
        decoder_vectors[1],
        six[4],
        plane_three[1],
        plane_three[2],
        six[5],
        decoder_vectors[2],
        decoder_vectors[3],
        grad_decoder_expand,
        grad_decoder_contract,
        decoder_vectors[4],
        decoder_vectors[5],
    )


def solution(mesh):
    body = plane_body if fits_plane(mesh) else general_body
    in_specs = (
        P("seq", "dp", None),
        P("seq", "dp", None),
        P("dp"),
        P("dp"),
        P(),
        P(),
        P(),
        P(),
        P(),
        P(),
        P(None, "seq"),
        P("seq", None),
        P(),
        P(),
        P(),
        P(),
        P(),
        P(),
        P(),
        P(),
        P(),
        P(),
        P(),
        P(),
        P(),
        P(),
        P(None, "seq"),
        P("seq", None),
        P(),
        P(),
        P("seq", "dp", None),
        P("seq", "dp", None),
    )
    out_specs = (
        P("seq", "dp", None),
        P("seq", "dp", None),
        P("seq", "dp", None),
        P("seq", "dp", None),
        P("seq", None),
        P("seq", None),
        P("seq", None),
        P("seq", None),
        P("seq"),
        P("seq"),
        P(None, "seq"),
        P("seq", None),
        P("seq"),
        P("seq"),
        P("seq", None),
        P("seq", None),
        P("seq", None),
        P("seq", None),
        P("seq"),
        P("seq"),
        P("seq", None),
        P("seq", None),
        P("seq", None),
        P("seq", None),
        P("seq"),
        P("seq"),
        P(None, "seq"),
        P("seq", None),
        P("seq"),
        P("seq"),
    )
    return jax.shard_map(body, mesh=mesh, in_specs=in_specs, out_specs=out_specs, check_vma=False)
```

```python
import functools

import jax
import jax.numpy as jnp
from jax import lax
from jax.experimental import pallas as pl
from jax.experimental.pallas import tpu as pltpu
from jax.sharding import PartitionSpec as P

HEADS = 16


masked_fill = -1e30
norm_epsilon = 1e-05


def layer_norm(rows, gain, shift):
    centre = jnp.mean(rows, -1, keepdims=True)
    centred = rows - centre
    spread = jnp.mean(centred * centred, -1, keepdims=True)
    return centred * lax.rsqrt(spread + norm_epsilon) * gain + shift


def gelu_exact(values):
    return jax.nn.gelu(values, approximate=False)


def project(rows, weight):
    return jnp.dot(rows, weight, preferred_element_type=jnp.float32)


def project_back(grads, weight):
    return jnp.einsum("re,de->rd", grads, weight, preferred_element_type=jnp.float32)


def outer_sum(rows, grads):
    return jnp.einsum("rd,re->de", rows, grads, preferred_element_type=jnp.float32)


def by_heads(array):
    return array.reshape(array.shape[0], HEADS, -1)


def head_scale(width):
    return (width // HEADS) ** (-0.5)


def score_block(queries, keys):
    scores = jnp.einsum(
        "qhd,khd->hqk", by_heads(queries), by_heads(keys), preferred_element_type=jnp.float32
    )
    return scores * head_scale(queries.shape[-1])


def allowed_keys(query_rows, key_rows, length, causal):
    allowed = key_rows[None, :] < length
    if causal:
        allowed = allowed & (key_rows[None, :] <= query_rows[:, None])
    return allowed


def table_of(array, table):
    return lax.dynamic_index_in_dim(array, table, 1, keepdims=False)


def gather_pair(keys, values):
    return (
        lax.all_gather(keys, "seq", axis=0, tiled=True),
        lax.all_gather(values, "seq", axis=0, tiled=True),
    )


def gather_rows(rows):
    return lax.all_gather(rows, "seq", axis=0, tiled=True)


def sum_rows(terms, count):
    return lax.psum_scatter(
        terms(jnp.int32(0), count * lax.axis_size("seq")).astype(jnp.bfloat16),
        "seq",
        scatter_dimension=0,
        tiled=True,
    ).astype(jnp.float32)


def projections(from_rows, to_rows, w_query, w_key, w_value):
    qlen, tables, width = from_rows.shape
    klen = to_rows.shape[0]
    to_flat = to_rows.reshape(-1, width)
    queries = (
        project(from_rows.reshape(-1, width), w_query)
        .astype(jnp.bfloat16)
        .reshape(qlen, tables, width)
    )
    keys = project(to_flat, w_key).astype(jnp.bfloat16).reshape(klen, tables, width)
    values = project(to_flat, w_value).astype(jnp.bfloat16).reshape(klen, tables, width)
    return (queries, keys, values)


def finish_grads(from_rows, to_rows, w_query, w_key, w_value, d_queries, d_keys, d_values):
    width = from_rows.shape[-1]
    from_flat = from_rows.reshape(-1, width)
    to_flat = to_rows.reshape(-1, width)
    query_low = d_queries.astype(jnp.bfloat16).reshape(-1, width)
    key_low = d_keys.astype(jnp.bfloat16).reshape(-1, width)
    value_low = d_values.astype(jnp.bfloat16).reshape(-1, width)
    grad_query = outer_sum(from_flat, query_low)
    grad_key = outer_sum(to_flat, key_low)
    grad_value = outer_sum(to_flat, value_low)
    d_from = project_back(query_low, w_query)
    d_to = project_back(key_low, w_key) + project_back(value_low, w_value)
    return (d_from, d_to, grad_query, grad_key, grad_value)


def attend_forward(from_rows, to_rows, w_query, w_key, w_value, lengths, causal):
    qlen, tables, width = from_rows.shape
    queries, keys, values = projections(from_rows, to_rows, w_query, w_key, w_value)
    gathered = gather_pair(keys, values)
    all_keys, all_values = gathered
    query_rows = lax.axis_index("seq") * qlen + jnp.arange(qlen)
    key_rows = jnp.arange(all_keys.shape[0])

    def one_table(table):
        scores = score_block(table_of(queries, table), table_of(all_keys, table))
        allowed = allowed_keys(query_rows, key_rows, lengths[table], causal)
        scores = jnp.where(allowed[None], scores, masked_fill)
        top = jnp.max(scores, -1)
        weights = jnp.exp(scores - top[..., None])
        total = jnp.sum(weights, -1)
        probs = (weights / total[..., None]).astype(jnp.bfloat16)
        context = jnp.einsum(
            "hqk,khd->qhd",
            probs,
            by_heads(table_of(all_values, table)),
            preferred_element_type=jnp.float32,
        )
        return (context.reshape(qlen, width), top + jnp.log(total))

    context, logsum = lax.map(one_table, jnp.arange(tables))
    return (queries, keys, values, gathered, jnp.swapaxes(context, 0, 1), logsum)


def key_value_terms(
    query_part,
    grads_part,
    logsum_part,
    delta_part,
    key_part,
    value_part,
    query_rows,
    part_rows,
    length,
    causal,
    scale,
):
    scores = score_block(query_part, key_part)
    allowed = allowed_keys(query_rows, part_rows, length, causal)
    probs = jnp.where(allowed[None], jnp.exp(scores - logsum_part[..., None]), 0.0)
    grads_here = by_heads(grads_part)
    d_values = jnp.einsum(
        "hqk,qhd->khd", probs.astype(jnp.bfloat16), grads_here, preferred_element_type=jnp.float32
    )
    d_probs = jnp.einsum(
        "qhd,khd->hqk", grads_here, by_heads(value_part), preferred_element_type=jnp.float32
    )
    d_scores = (probs * (d_probs - delta_part.T[..., None])).astype(jnp.bfloat16)
    d_keys = (
        jnp.einsum(
            "hqk,qhd->khd", d_scores, by_heads(query_part), preferred_element_type=jnp.float32
        )
        * scale
    )
    count = key_part.shape[0]
    width = key_part.shape[-1]
    return jnp.concatenate([d_keys.reshape(count, width), d_values.reshape(count, width)], -1)


def attend_backward(state, from_rows, to_rows, w_query, w_key, w_value, lengths, causal, d_context):
    queries, keys, values, gathered, context, logsum = state
    qlen, tables, width = queries.shape
    klen = keys.shape[0]
    all_keys, all_values = gather_pair(keys, values)
    scale = head_scale(width)
    d_low = d_context.reshape(qlen, tables, width).astype(jnp.bfloat16)
    delta = jnp.sum((d_low.astype(jnp.float32) * context).reshape(qlen, tables, HEADS, -1), -1)
    query_rows = lax.axis_index("seq") * qlen + jnp.arange(qlen)
    key_rows = jnp.arange(all_keys.shape[0])

    def query_table(table):
        scores = score_block(table_of(queries, table), table_of(all_keys, table))
        allowed = allowed_keys(query_rows, key_rows, lengths[table], causal)
        probs = jnp.where(allowed[None], jnp.exp(scores - logsum[table][..., None]), 0.0)
        d_probs = jnp.einsum(
            "qhd,khd->hqk",
            by_heads(table_of(d_low, table)),
            by_heads(table_of(all_values, table)),
            preferred_element_type=jnp.float32,
        )
        d_scores = (probs * (d_probs - delta[:, table].T[..., None])).astype(jnp.bfloat16)
        d_query = jnp.einsum(
            "hqk,khd->qhd",
            d_scores,
            by_heads(table_of(all_keys, table)),
            preferred_element_type=jnp.float32,
        )
        return (d_query * scale).reshape(qlen, width)

    d_queries = jnp.swapaxes(lax.map(query_table, jnp.arange(tables)), 0, 1)
    part_rows = jnp.arange(klen * lax.axis_size("seq"))

    def key_table(table, terms):
        piece = key_value_terms(
            table_of(queries, table),
            table_of(d_low, table),
            logsum[table],
            delta[:, table],
            table_of(all_keys, table),
            table_of(all_values, table),
            query_rows,
            part_rows,
            lengths[table],
            causal,
            scale,
        )
        return lax.dynamic_update_index_in_dim(terms, piece, table, 1)

    summed = lax.psum_scatter(
        lax.fori_loop(
            0,
            tables,
            key_table,
            jnp.zeros((klen * lax.axis_size("seq"), tables, 2 * width), jnp.float32),
        ).astype(jnp.bfloat16),
        "seq",
        scatter_dimension=0,
        tiled=True,
    ).astype(jnp.float32)
    return finish_grads(
        from_rows,
        to_rows,
        w_query,
        w_key,
        w_value,
        d_queries,
        summed[..., :width],
        summed[..., width:],
    )


def token_forward(rows, w_expand, w_contract):
    all_rows = gather_rows(rows)
    acts = gelu_exact(project(all_rows, w_expand)).astype(jnp.bfloat16)

    def contract_terms(start, count):
        return project(acts, w_contract)

    return (sum_rows(contract_terms, rows.shape[0]), all_rows)


def token_backward(all_rows, d_out, w_expand, w_contract):
    all_grads = gather_rows(d_out.astype(jnp.bfloat16))
    acts, gelu_back = jax.vjp(gelu_exact, project(all_rows, w_expand))
    d_hidden = gelu_back(project_back(all_grads, w_contract))[0].astype(jnp.bfloat16)
    grad_expand = outer_sum(all_rows, d_hidden)
    grad_contract = outer_sum(acts.astype(jnp.bfloat16), all_grads)

    def expand_terms(start, count):
        return project_back(d_hidden, w_expand)

    return (sum_rows(expand_terms, d_out.shape[0]), grad_expand, grad_contract)


def general_body(
    source_tokens,
    target_tokens,
    source_lengths,
    target_lengths,
    encoder_query,
    encoder_key,
    encoder_value,
    encoder_mix,
    attend_gain,
    attend_shift,
    encoder_expand,
    encoder_contract,
    encoder_gain,
    encoder_shift,
    decoder_query,
    decoder_key,
    decoder_value,
    decoder_mix,
    self_gain,
    self_shift,
    cross_query,
    cross_key,
    cross_value,
    cross_mix,
    cross_gain,
    cross_shift,
    decoder_expand,
    decoder_contract,
    decoder_gain,
    decoder_shift,
    source_cotangent,
    target_cotangent,
):
    slots, tables, width = source_tokens.shape
    places = target_tokens.shape[0]
    source_flat = source_tokens.reshape(-1, width)
    target_flat = target_tokens.reshape(-1, width)
    encoder_state = attend_forward(
        source_tokens,
        source_tokens,
        encoder_query,
        encoder_key,
        encoder_value,
        source_lengths,
        False,
    )
    encoder_context = encoder_state[4].reshape(-1, width).astype(jnp.bfloat16)
    first, first_back = jax.vjp(
        layer_norm,
        source_flat.astype(jnp.float32) + project(encoder_context, encoder_mix),
        attend_gain,
        attend_shift,
    )
    first_low = first.astype(jnp.bfloat16)
    widened, encoder_kept = token_forward(first_low, encoder_expand, encoder_contract)
    second, second_back = jax.vjp(layer_norm, first + widened, encoder_gain, encoder_shift)
    encoded = second.astype(jnp.bfloat16).reshape(slots, tables, width)
    decoder_state = attend_forward(
        target_tokens,
        target_tokens,
        decoder_query,
        decoder_key,
        decoder_value,
        target_lengths,
        True,
    )
    decoder_context = decoder_state[4].reshape(-1, width).astype(jnp.bfloat16)
    third, third_back = jax.vjp(
        layer_norm,
        target_flat.astype(jnp.float32) + project(decoder_context, decoder_mix),
        self_gain,
        self_shift,
    )
    third_blocks = third.astype(jnp.bfloat16).reshape(places, tables, width)
    cross_state = attend_forward(
        third_blocks, encoded, cross_query, cross_key, cross_value, source_lengths, False
    )
    cross_context = cross_state[4].reshape(-1, width).astype(jnp.bfloat16)
    fourth, fourth_back = jax.vjp(
        layer_norm, third + project(cross_context, cross_mix), cross_gain, cross_shift
    )
    fourth_low = fourth.astype(jnp.bfloat16)
    narrowed, decoder_kept = token_forward(fourth_low, decoder_expand, decoder_contract)
    fifth, fifth_back = jax.vjp(layer_norm, fourth + narrowed, decoder_gain, decoder_shift)
    decoded = fifth.astype(jnp.bfloat16).reshape(places, tables, width)
    d_fifth, grad_decoder_gain, grad_decoder_shift = fifth_back(
        target_cotangent.reshape(-1, width).astype(jnp.float32)
    )
    d_rows, grad_decoder_expand, grad_decoder_contract = token_backward(
        decoder_kept, d_fifth, decoder_expand, decoder_contract
    )
    d_fourth, grad_cross_gain, grad_cross_shift = fourth_back(d_fifth + d_rows)
    cross_low = d_fourth.astype(jnp.bfloat16)
    grad_cross_mix = outer_sum(cross_context, cross_low)
    d_cross_context = project_back(cross_low, cross_mix)
    d_third_cross, d_encoded, grad_cross_query, grad_cross_key, grad_cross_value = attend_backward(
        cross_state,
        third_blocks,
        encoded,
        cross_query,
        cross_key,
        cross_value,
        source_lengths,
        False,
        d_cross_context,
    )
    d_third, grad_self_gain, grad_self_shift = third_back(d_fourth + d_third_cross)
    self_low = d_third.astype(jnp.bfloat16)
    grad_decoder_mix = outer_sum(decoder_context, self_low)
    d_from, d_to, grad_decoder_query, grad_decoder_key, grad_decoder_value = attend_backward(
        decoder_state,
        target_tokens,
        target_tokens,
        decoder_query,
        decoder_key,
        decoder_value,
        target_lengths,
        True,
        project_back(self_low, decoder_mix),
    )
    grad_target = (d_third + d_from + d_to).reshape(places, tables, width)
    d_second, grad_encoder_gain, grad_encoder_shift = second_back(
        source_cotangent.reshape(-1, width).astype(jnp.float32) + d_encoded
    )
    d_rows, grad_encoder_expand, grad_encoder_contract = token_backward(
        encoder_kept, d_second, encoder_expand, encoder_contract
    )
    d_first, grad_attend_gain, grad_attend_shift = first_back(d_second + d_rows)
    encoder_low = d_first.astype(jnp.bfloat16)
    grad_encoder_mix = outer_sum(encoder_context, encoder_low)
    d_from, d_to, grad_encoder_query, grad_encoder_key, grad_encoder_value = attend_backward(
        encoder_state,
        source_tokens,
        source_tokens,
        encoder_query,
        encoder_key,
        encoder_value,
        source_lengths,
        False,
        project_back(encoder_low, encoder_mix),
    )
    grad_source = (d_first + d_from + d_to).reshape(slots, tables, width)
    shards = (
        lax.psum_scatter(
            grad_encoder_query.astype(jnp.bfloat16), "seq", scatter_dimension=0, tiled=True
        ).astype(jnp.float32),
        lax.psum_scatter(
            grad_encoder_key.astype(jnp.bfloat16), "seq", scatter_dimension=0, tiled=True
        ).astype(jnp.float32),
        lax.psum_scatter(
            grad_encoder_value.astype(jnp.bfloat16), "seq", scatter_dimension=0, tiled=True
        ).astype(jnp.float32),
        lax.psum_scatter(
            grad_encoder_mix.astype(jnp.bfloat16), "seq", scatter_dimension=0, tiled=True
        ).astype(jnp.float32),
        lax.psum_scatter(
            grad_decoder_query.astype(jnp.bfloat16), "seq", scatter_dimension=0, tiled=True
        ).astype(jnp.float32),
        lax.psum_scatter(
            grad_decoder_key.astype(jnp.bfloat16), "seq", scatter_dimension=0, tiled=True
        ).astype(jnp.float32),
        lax.psum_scatter(
            grad_decoder_value.astype(jnp.bfloat16), "seq", scatter_dimension=0, tiled=True
        ).astype(jnp.float32),
        lax.psum_scatter(
            grad_decoder_mix.astype(jnp.bfloat16), "seq", scatter_dimension=0, tiled=True
        ).astype(jnp.float32),
        lax.psum_scatter(
            grad_cross_query.astype(jnp.bfloat16), "seq", scatter_dimension=0, tiled=True
        ).astype(jnp.float32),
        lax.psum_scatter(
            grad_cross_key.astype(jnp.bfloat16), "seq", scatter_dimension=0, tiled=True
        ).astype(jnp.float32),
        lax.psum_scatter(
            grad_cross_value.astype(jnp.bfloat16), "seq", scatter_dimension=0, tiled=True
        ).astype(jnp.float32),
        lax.psum_scatter(
            grad_cross_mix.astype(jnp.bfloat16), "seq", scatter_dimension=0, tiled=True
        ).astype(jnp.float32),
        lax.psum_scatter(
            grad_attend_gain.astype(jnp.bfloat16), "seq", scatter_dimension=0, tiled=True
        ).astype(jnp.float32),
        lax.psum_scatter(
            grad_attend_shift.astype(jnp.bfloat16), "seq", scatter_dimension=0, tiled=True
        ).astype(jnp.float32),
        lax.psum_scatter(
            grad_encoder_gain.astype(jnp.bfloat16), "seq", scatter_dimension=0, tiled=True
        ).astype(jnp.float32),
        lax.psum_scatter(
            grad_encoder_shift.astype(jnp.bfloat16), "seq", scatter_dimension=0, tiled=True
        ).astype(jnp.float32),
        lax.psum_scatter(
            grad_self_gain.astype(jnp.bfloat16), "seq", scatter_dimension=0, tiled=True
        ).astype(jnp.float32),
        lax.psum_scatter(
            grad_self_shift.astype(jnp.bfloat16), "seq", scatter_dimension=0, tiled=True
        ).astype(jnp.float32),
        lax.psum_scatter(
            grad_cross_gain.astype(jnp.bfloat16), "seq", scatter_dimension=0, tiled=True
        ).astype(jnp.float32),
        lax.psum_scatter(
            grad_cross_shift.astype(jnp.bfloat16), "seq", scatter_dimension=0, tiled=True
        ).astype(jnp.float32),
        lax.psum_scatter(
            grad_decoder_gain.astype(jnp.bfloat16), "seq", scatter_dimension=0, tiled=True
        ).astype(jnp.float32),
        lax.psum_scatter(
            grad_decoder_shift.astype(jnp.bfloat16), "seq", scatter_dimension=0, tiled=True
        ).astype(jnp.float32),
    )
    totals = (
        lax.psum(shards[0].astype(jnp.bfloat16), "dp").astype(jnp.float32),
        lax.psum(shards[1].astype(jnp.bfloat16), "dp").astype(jnp.float32),
        lax.psum(shards[2].astype(jnp.bfloat16), "dp").astype(jnp.float32),
        lax.psum(shards[3].astype(jnp.bfloat16), "dp").astype(jnp.float32),
        lax.psum(shards[4].astype(jnp.bfloat16), "dp").astype(jnp.float32),
        lax.psum(shards[5].astype(jnp.bfloat16), "dp").astype(jnp.float32),
        lax.psum(shards[6].astype(jnp.bfloat16), "dp").astype(jnp.float32),
        lax.psum(shards[7].astype(jnp.bfloat16), "dp").astype(jnp.float32),
        lax.psum(shards[8].astype(jnp.bfloat16), "dp").astype(jnp.float32),
        lax.psum(shards[9].astype(jnp.bfloat16), "dp").astype(jnp.float32),
        lax.psum(shards[10].astype(jnp.bfloat16), "dp").astype(jnp.float32),
        lax.psum(shards[11].astype(jnp.bfloat16), "dp").astype(jnp.float32),
        lax.psum(shards[12].astype(jnp.bfloat16), "dp").astype(jnp.float32),
        lax.psum(shards[13].astype(jnp.bfloat16), "dp").astype(jnp.float32),
        lax.psum(shards[14].astype(jnp.bfloat16), "dp").astype(jnp.float32),
        lax.psum(shards[15].astype(jnp.bfloat16), "dp").astype(jnp.float32),
        lax.psum(shards[16].astype(jnp.bfloat16), "dp").astype(jnp.float32),
        lax.psum(shards[17].astype(jnp.bfloat16), "dp").astype(jnp.float32),
        lax.psum(shards[18].astype(jnp.bfloat16), "dp").astype(jnp.float32),
        lax.psum(shards[19].astype(jnp.bfloat16), "dp").astype(jnp.float32),
        lax.psum(shards[20].astype(jnp.bfloat16), "dp").astype(jnp.float32),
        lax.psum(shards[21].astype(jnp.bfloat16), "dp").astype(jnp.float32),
        lax.psum(grad_encoder_expand.astype(jnp.bfloat16), "dp").astype(jnp.float32),
        lax.psum(grad_encoder_contract.astype(jnp.bfloat16), "dp").astype(jnp.float32),
        lax.psum(grad_decoder_expand.astype(jnp.bfloat16), "dp").astype(jnp.float32),
        lax.psum(grad_decoder_contract.astype(jnp.bfloat16), "dp").astype(jnp.float32),
    )
    return (
        encoded,
        decoded,
        grad_source,
        grad_target,
        totals[0],
        totals[1],
        totals[2],
        totals[3],
        totals[12],
        totals[13],
        totals[22],
        totals[23],
        totals[14],
        totals[15],
        totals[4],
        totals[5],
        totals[6],
        totals[7],
        totals[16],
        totals[17],
        totals[8],
        totals[9],
        totals[10],
        totals[11],
        totals[18],
        totals[19],
        totals[24],
        totals[25],
        totals[20],
        totals[21],
    )


MESH = pl.DeviceIdType.MESH
PEERS = (6, 7, 2, 3, 4, 5, 1)
low = jnp.bfloat16
wide = jnp.float32
VMEM_BYTES = 60 * 2**20


def fits_plane(mesh):
    return mesh.shape["seq"] == 8


def add_low(left, right):
    return (left.astype(wide) + right.astype(wide)).astype(low)


OWNERS = (3, 5, 7, 1, 2, 4, 6, 0)


def nt(left, right):
    return lax.dot_general(left, right, (((1,), (1,)), ((), ())), preferred_element_type=wide)


def nn(left, right):
    return lax.dot_general(left, right, (((1,), (0,)), ((), ())), preferred_element_type=wide)


def tn(left, right):
    return lax.dot_general(left, right, (((0,), (0,)), ((), ())), preferred_element_type=wide)


def lane_head(shape, size):
    return lax.broadcasted_iota(jnp.int32, shape, len(shape) - 1) // size


def vmem_spec():
    return pl.BlockSpec(memory_space=pltpu.VMEM)


def any_spec():
    return pl.BlockSpec(memory_space=pl.ANY)


def greet(masks, size=0):
    me = lax.axis_index("seq")
    barrier = pltpu.get_barrier_semaphore()
    for mask in masks:
        pl.semaphore_signal(barrier, inc=1, device_id={"seq": me ^ mask}, device_id_type=MESH)
    if not size:
        pl.semaphore_wait(barrier, len(masks))
        return
    place = lax.axis_index("dp")
    inner = (place > 0) & (place < size - 1)

    @pl.when(place > 0)
    def _():
        pl.semaphore_signal(barrier, inc=1, device_id={"dp": place - 1}, device_id_type=MESH)

    @pl.when(place < size - 1)
    def _():
        pl.semaphore_signal(barrier, inc=1, device_id={"dp": place + 1}, device_id_type=MESH)

    @pl.when(inner)
    def _():
        pl.semaphore_wait(barrier, len(masks) + 2)

    @pl.when(jnp.logical_not(inner))
    def _():
        pl.semaphore_wait(barrier, len(masks) + 1)


class Line:
    lag = 2

    def __init__(self, size, chunks, mine, came, sent, send, recv):
        place = lax.axis_index("dp")
        self.chunks, self.mine, self.came, self.sent, self.send, self.recv = chunks, mine, came, sent, send, recv
        self.count = mine.shape[0] // chunks
        self.has = (place > 0, place < size - 1)
        self.neighbour = (place - 1, place + 1)
        self.lower = place < size // 2
        self.steps = chunks + self.lag

    def copy(self, side, chunk, first=False):
        part = pl.ds(chunk * self.count, self.count)
        return pltpu.make_async_remote_copy(
            src_ref=self.mine.at[part] if first else self.sent.at[side, part],
            dst_ref=self.came.at[side, part],
            send_sem=self.send.at[side, chunk],
            recv_sem=self.recv.at[side, chunk],
            device_id={"dp": self.neighbour[1 - side]},
            device_id_type=MESH,
        )

    def begin(self):
        for side in range(2):

            @pl.when(jnp.logical_not(self.has[side]))
            def _(side=side):
                for chunk in range(self.chunks):
                    self.copy(side, chunk, True).start()
                self.came[side] = jnp.zeros(self.mine.shape, low)

    def forward(self, side, chunk):
        part = pl.ds(chunk * self.count, self.count)

        @pl.when(self.has[side])
        def _():
            self.copy(side, chunk).wait_recv()

            @pl.when(self.has[1 - side])
            def _():
                self.sent[side, part] = add_low(self.mine[part], self.came[side, part])
                self.copy(side, chunk).start()

    def step(self, number):
        if number >= self.steps:
            return
        for near in range(2):

            @pl.when(self.lower if near == 0 else jnp.logical_not(self.lower))
            def _(near=near):
                if number < self.chunks:
                    self.forward(near, number)
                if number >= self.lag:
                    self.forward(1 - near, number - self.lag)

    def rest(self, first):
        for number in range(first, self.steps):
            self.step(number)

    def total(self, part=slice(None)):
        return self.mine[part].astype(wide) + self.came[0, part].astype(wide) + self.came[1, part].astype(wide)

    def end(self):
        for side in range(2):

            @pl.when(self.has[1 - side])
            def _(side=side):
                for chunk in range(self.chunks):
                    self.copy(side, chunk).wait_send()


def line_scratch(shape, chunks):
    return [
        pltpu.VMEM((2,) + shape, low),
        pltpu.VMEM((2,) + shape, low),
        pltpu.SemaphoreType.DMA((2, chunks)),
        pltpu.SemaphoreType.DMA((2, chunks)),
    ]


def remote(src, dst, send, recv, to):
    return pltpu.make_async_remote_copy(
        src_ref=src, dst_ref=dst, send_sem=send, recv_sem=recv, device_id={"seq": to}, device_id_type=MESH
    )


def params(collective_id):
    return pltpu.CompilerParams(
        collective_id=collective_id, has_side_effects=True, vmem_limit_bytes=VMEM_BYTES
    )


def gather_table_kernel(rows, extra, out, out_extra, send, recv, keep):
    me = lax.axis_index("seq")
    mine = me // 4
    greet((1, 2, 4, 6))
    own = [
        pltpu.make_async_copy(rows.at[mine], out.at[me], keep.at[0]),
        pltpu.make_async_copy(extra, out_extra.at[me], keep.at[1]),
    ]
    for copy in own:
        copy.start()
    started = []
    both = ((0, lambda table: rows.at[table], out), (1, lambda table: extra, out_extra))
    for slot, mask, table in ((0, 6, 1 - mine), (1, 2, mine), (2, 4, 1 - mine), (3, 1, mine)):
        for kind, source, place in both:
            copy = remote(source(table), place.at[me], send.at[kind, slot], recv.at[kind, slot], me ^ mask)
            copy.start()
            started.append(copy)
    for slot, mask in ((1, 2), (2, 4), (0, 6)):
        owner = me ^ mask
        for kind, source, place in both:
            remote(source(0), place.at[owner], send.at[kind, slot], recv.at[kind, slot], me ^ 1).wait_recv()
            copy = remote(
                place.at[owner], place.at[owner], send.at[kind, 4 + slot], recv.at[kind, 4 + slot], me ^ 1
            )
            copy.start()
            started.append(copy)
    for kind, source, place in both:
        remote(source(0), place.at[me ^ 1], send.at[kind, 3], recv.at[kind, 3], me ^ 1).wait_recv()
        for slot, mask in ((1, 2), (2, 4), (0, 6)):
            remote(
                source(0), place.at[me ^ mask ^ 1], send.at[kind, 4 + slot], recv.at[kind, 4 + slot], me ^ 1
            ).wait_recv()
    for copy in started:
        copy.wait_send()
    for copy in own:
        copy.wait()


def gather_table(rows, extra):
    return pl.pallas_call(
        gather_table_kernel,
        out_shape=(
            jax.ShapeDtypeStruct((8,) + rows.shape[1:], rows.dtype),
            jax.ShapeDtypeStruct((8,) + extra.shape, extra.dtype),
        ),
        in_specs=[any_spec()] * 2,
        out_specs=(any_spec(), any_spec()),
        scratch_shapes=[
            pltpu.SemaphoreType.DMA((2, 7)),
            pltpu.SemaphoreType.DMA((2, 7)),
            pltpu.SemaphoreType.DMA((2,)),
        ],
        compiler_params=params(1),
    )(rows, extra)


def scatter_plane_kernel(terms, pairs, expand, contract, out, d_expand, d_contract, sib, pair, came, far, came_far, send, recv, send_pair, recv_pair, send_far, recv_far):
    me = lax.axis_index("seq")
    half = out.shape[0] // 2
    greet((1, 2, 4))
    halves = (pl.ds(0, half), pl.ds(half, half))
    started = []
    chips = (6, 2, 4, 0)
    for slot, mask in enumerate(chips):
        copy = remote(terms.at[me ^ 1 ^ mask], sib.at[slot], send.at[slot], recv.at[slot], me ^ 1)
        copy.start()
        started.append(copy)

    def pair_copy(slot):
        return remote(
            pair.at[slot], came.at[slot], send_pair.at[slot], recv_pair.at[slot], me ^ (2, 4, 2, 4)[slot]
        )

    def far_copy(slot):
        return remote(far.at[slot], came_far.at[slot], send_far.at[slot], recv_far.at[slot], me ^ (4, 2)[slot])

    def both(mask, slot, rows):
        return terms[me ^ mask, rows].astype(wide) + sib[slot, rows].astype(wide)

    for slot, mask in enumerate(chips):
        remote(terms.at[0], sib.at[slot], send.at[slot], recv.at[slot], me ^ 1).wait_recv()
        if mask == 6:
            for side in range(2):
                pair[side] = both(6, 0, halves[side]).astype(low)
                pair_copy(side).start()
        if mask == 2:
            pair[2] = both(2, 1, halves[0]).astype(low)
            pair_copy(2).start()
        if mask == 4:
            pair[3] = both(4, 2, halves[1]).astype(low)
            pair_copy(3).start()
    x = pairs[:, 0].reshape(-1, pairs.shape[3])
    g = pairs[:, 1].reshape(-1, pairs.shape[3])
    act, slope = gelu_parts(nn(x, expand[...]))
    d_hidden = (nt(g, contract[...]) * slope).astype(low)
    d_expand[...] = tn(x, d_hidden)
    d_contract[...] = tn(act.astype(low), g)
    for side in range(2):
        pair_copy(side).wait_recv()
        mask, slot = ((4, 2), (2, 1))[side]
        far[side] = (both(mask, slot, halves[side]) + came[side].astype(wide)).astype(low)
        far_copy(side).start()
    for side in range(2):
        pair_copy(2 + side).wait_recv()
        out[halves[side]] = both(0, 3, halves[side]) + came[2 + side].astype(wide)
    for side in range(2):
        far_copy(side).wait_recv()
        out[halves[side]] += came_far[side].astype(wide)
    for copy in started:
        copy.wait_send()
    for slot in range(4):
        pair_copy(slot).wait_send()
    for side in range(2):
        far_copy(side).wait_send()


def scatter_plane(terms, pairs, expand, contract):
    _, rows, width = terms.shape
    return pl.pallas_call(
        scatter_plane_kernel,
        out_shape=(
            jax.ShapeDtypeStruct((rows, width), wide),
            jax.ShapeDtypeStruct(expand.shape, wide),
            jax.ShapeDtypeStruct(contract.shape, wide),
        ),
        in_specs=[vmem_spec()] * 4,
        out_specs=(vmem_spec(),) * 3,
        scratch_shapes=[
            pltpu.VMEM((4, rows, width), low),
            pltpu.VMEM((4, rows // 2, width), low),
            pltpu.VMEM((4, rows // 2, width), low),
            pltpu.VMEM((2, rows // 2, width), low),
            pltpu.VMEM((2, rows // 2, width), low),
        ]
        + [pltpu.SemaphoreType.DMA((4,))] * 4
        + [pltpu.SemaphoreType.DMA((2,))] * 2,
        compiler_params=params(9),
    )(terms, pairs, expand, contract)


def heads_to_rows_kernel(blocks, out, send, recv, keep):
    me = lax.axis_index("seq")
    width = blocks.shape[2]
    greet(PEERS)

    def place(owner):
        return out.at[owner // 4, :, pl.ds(pl.multiple_of((owner % 4) * width, width), width)]

    local = pltpu.make_async_copy(blocks.at[me], place(me), keep)
    local.start()
    started = []
    for mask in PEERS:
        copy = remote(blocks.at[me ^ mask], place(me), send.at[mask], recv.at[mask], me ^ mask)
        copy.start()
        started.append(copy)
    for mask in PEERS:
        remote(blocks.at[0], place(me ^ mask), send.at[mask], recv.at[mask], me ^ mask).wait_recv()
    for copy in started:
        copy.wait_send()
    local.wait()


def heads_to_rows(blocks):
    _, rows, width = blocks.shape
    return pl.pallas_call(
        heads_to_rows_kernel,
        out_shape=jax.ShapeDtypeStruct((2, rows, 4 * width), blocks.dtype),
        in_specs=[any_spec()],
        out_specs=any_spec(),
        scratch_shapes=[
            pltpu.SemaphoreType.DMA((8,)),
            pltpu.SemaphoreType.DMA((8,)),
            pltpu.SemaphoreType.DMA,
        ],
        compiler_params=params(2),
    )(blocks)


def rows_to_heads_kernel(rows, left, right, out, away, kept, send, recv, keep):
    me = lax.axis_index("seq")
    width = out.shape[2]
    greet(PEERS)

    def part(owner):
        return rows.at[owner // 4, :, pl.ds(pl.multiple_of((owner % 4) * width, width), width)]

    local = pltpu.make_async_copy(part(me), out.at[me], keep)
    local.start()
    started = []
    for mask in PEERS:
        copy = remote(part(me ^ mask), out.at[me], send.at[mask], recv.at[mask], me ^ mask)
        copy.start()
        started.append(copy)
    size = left.shape[1] // 8
    for place, mask in enumerate(OWNERS):
        columns = pl.ds(pl.multiple_of((me ^ mask) * size, size), size)
        (away, kept)[place // 4][place % 4] = tn(left[:, columns], right[...]).astype(low)
    for mask in PEERS:
        remote(part(me), out.at[me ^ mask], send.at[mask], recv.at[mask], me ^ mask).wait_recv()
    for copy in started:
        copy.wait_send()
    local.wait()


def rows_to_heads(rows, left, right):
    _, count, width = rows.shape
    half = jax.ShapeDtypeStruct((4, width // 8, width), low)
    return pl.pallas_call(
        rows_to_heads_kernel,
        out_shape=(jax.ShapeDtypeStruct((8, count, width // 4), rows.dtype), half, half),
        in_specs=[any_spec(), vmem_spec(), vmem_spec()],
        out_specs=(any_spec(), vmem_spec(), vmem_spec()),
        scratch_shapes=[
            pltpu.SemaphoreType.DMA((8,)),
            pltpu.SemaphoreType.DMA((8,)),
            pltpu.SemaphoreType.DMA,
        ],
        compiler_params=params(3),
    )(rows, left, right)


def sum_small_kernel(terms, earlier, out, mine, came, send, recv, send_back, recv_back):
    me = lax.axis_index("seq")
    greet(PEERS)
    mine[...] = terms[...].astype(low)
    started = []
    for mask in PEERS:
        copy = remote(mine.at[me ^ mask], came.at[mask], send.at[mask], recv.at[mask], me ^ mask)
        copy.start()
        started.append(copy)
    total = terms[me].astype(wide)
    for mask in PEERS:
        remote(mine.at[0], came.at[mask], send.at[mask], recv.at[mask], me ^ mask).wait_recv()
        total = total + came[mask].astype(wide)
    out[me] = total.astype(low)
    for mask in PEERS:
        copy = remote(out.at[me], out.at[me], send_back.at[mask], recv_back.at[mask], me ^ mask)
        copy.start()
        started.append(copy)
    for mask in PEERS:
        remote(mine.at[0], out.at[me ^ mask], send_back.at[mask], recv_back.at[mask], me ^ mask).wait_recv()
    for copy in started:
        copy.wait_send()


def sum_small(terms, collective_id, earlier=None):
    count, width = terms.shape
    earlier = terms if earlier is None else earlier
    blocks = (8, count // 8, width)
    return pl.pallas_call(
        sum_small_kernel,
        out_shape=jax.ShapeDtypeStruct(blocks, low),
        in_specs=[vmem_spec(), any_spec()],
        out_specs=vmem_spec(),
        scratch_shapes=[pltpu.VMEM(blocks, low), pltpu.VMEM(blocks, low)]
        + [pltpu.SemaphoreType.DMA((8,))] * 4,
        compiler_params=params(collective_id),
    )(terms.reshape(blocks), earlier).reshape(count, width)


def sum_small_outer_kernel(
    terms, earlier, left, one, two, out, away, kept, mine, came, send, recv, send_back, recv_back
):
    me = lax.axis_index("seq")
    greet(PEERS)
    mine[...] = terms[...].astype(low)
    started = []
    for mask in PEERS:
        copy = remote(mine.at[me ^ mask], came.at[mask], send.at[mask], recv.at[mask], me ^ mask)
        copy.start()
        started.append(copy)
    size = left.shape[1] // 8

    def outer(place):
        columns = pl.ds(pl.multiple_of((me ^ OWNERS[place]) * size, size), size)
        target = (away, kept)[place // 4]
        for row, grads in enumerate((one, two)):
            target[place % 4, row * size : (row + 1) * size] = tn(left[:, columns], grads[...]).astype(low)

    for place in range(4):
        outer(place)
    total = terms[me].astype(wide)
    for mask in PEERS:
        remote(mine.at[0], came.at[mask], send.at[mask], recv.at[mask], me ^ mask).wait_recv()
        total = total + came[mask].astype(wide)
    out[me] = total.astype(low)
    for mask in PEERS:
        copy = remote(out.at[me], out.at[me], send_back.at[mask], recv_back.at[mask], me ^ mask)
        copy.start()
        started.append(copy)
    for place in range(4, 8):
        outer(place)
    for mask in PEERS:
        remote(mine.at[0], out.at[me ^ mask], send_back.at[mask], recv_back.at[mask], me ^ mask).wait_recv()
    for copy in started:
        copy.wait_send()


def sum_small_outer(terms, earlier, left, one, two):
    count, width = terms.shape
    blocks = (8, count // 8, width)
    half = jax.ShapeDtypeStruct((4, left.shape[1] // 4, width), low)
    total, away, kept = pl.pallas_call(
        sum_small_outer_kernel,
        out_shape=(jax.ShapeDtypeStruct(blocks, low), half, half),
        in_specs=[vmem_spec(), any_spec()] + [vmem_spec()] * 3,
        out_specs=(vmem_spec(),) * 3,
        scratch_shapes=[pltpu.VMEM(blocks, low), pltpu.VMEM(blocks, low)]
        + [pltpu.SemaphoreType.DMA((8,))] * 4,
        compiler_params=params(11),
    )(terms.reshape(blocks), earlier, left, one, two)
    return total.reshape(count, width), away, kept


def merge_parts_kernel(terms, stats, out, logsum, came, came_stats, send, recv, send_st, recv_st, back, recv_back, back_st, recv_back_st):
    me = lax.axis_index("seq")
    width = out.shape[2]
    greet(PEERS)
    started = []
    for mask in PEERS:
        for src, dst, s, r in ((stats, came_stats, send_st, recv_st), (terms, came, send, recv)):
            copy = remote(src.at[me ^ mask], dst.at[mask], s.at[mask], r.at[mask], me ^ mask)
            copy.start()
            started.append(copy)
    for mask in PEERS:
        remote(stats.at[0], came_stats.at[mask], send_st.at[mask], recv_st.at[mask], me ^ mask).wait_recv()
    tops = [stats[me, 0]] + [came_stats[mask, 0] for mask in PEERS]
    sums = [stats[me, 1]] + [came_stats[mask, 1] for mask in PEERS]
    top = functools.reduce(jnp.maximum, tops)
    weights = [s * jnp.exp(t - top) for t, s in zip(tops, sums)]
    total = functools.reduce(jnp.add, weights)
    logsum[me] = top + jnp.log(total)
    size = width // HEADS
    spread = (
        lax.broadcasted_iota(jnp.int32, (128, width), 1) // size
        == lax.broadcasted_iota(jnp.int32, (128, width), 0)
    ).astype(wide)
    scaled = jnp.concatenate([w / total for w in weights], 0)
    scaled = lax.dot_general(
        scaled, spread, (((1,), (0,)), ((), ())), precision=lax.Precision.HIGHEST, preferred_element_type=wide
    )
    rows = tops[0].shape[0]
    result = scaled[:rows] * terms[me].astype(wide)
    for place, mask in enumerate(PEERS):
        remote(terms.at[0], came.at[mask], send.at[mask], recv.at[mask], me ^ mask).wait_recv()
        result = result + scaled[(place + 1) * rows : (place + 2) * rows] * came[mask].astype(wide)
    out[me] = result.astype(low)
    for mask in PEERS:
        for ref, s, r in ((out, back, recv_back), (logsum, back_st, recv_back_st)):
            copy = remote(ref.at[me], ref.at[me], s.at[mask], r.at[mask], me ^ mask)
            copy.start()
            started.append(copy)
    for mask in PEERS:
        for ref, s, r in ((out, back, recv_back), (logsum, back_st, recv_back_st)):
            remote(ref.at[me], ref.at[me ^ mask], s.at[mask], r.at[mask], me ^ mask).wait_recv()
    for copy in started:
        copy.wait_send()


def merge_parts(terms, tops, sums):
    count, width = terms.shape
    rows = count // 8
    stats = jnp.stack([tops.reshape(8, rows, 128), sums.reshape(8, rows, 128)], 1)
    out, logsum = pl.pallas_call(
        merge_parts_kernel,
        out_shape=(
            jax.ShapeDtypeStruct((8, rows, width), low),
            jax.ShapeDtypeStruct((8, rows, 128), wide),
        ),
        in_specs=[vmem_spec()] * 2,
        out_specs=(vmem_spec(), vmem_spec()),
        scratch_shapes=[pltpu.VMEM((8, rows, width), low), pltpu.VMEM((8, 2, rows, 128), wide)]
        + [pltpu.SemaphoreType.DMA((8,))] * 8,
        compiler_params=params(5),
    )(terms.reshape(8, rows, width), stats)
    return out.reshape(count, width), logsum.reshape(count, 128)


def finish_kernel(
    size, rows, grads, weights, vectors, joined, feed, middle, out, out_line, out_joined, out_turned, out_straight, out_middle,
    terms, sib, pair, came, blocks, came_blocks, line,
    send, recv, send_pair, recv_pair, send_block, recv_block,
    line_came, line_sent, send_line, recv_line, join_came, join_sent, send_join, recv_join,
):
    me = lax.axis_index("seq")
    mine = me // 4
    count = out.shape[1]
    width = grads.shape[1]
    cut = blocks.shape[1] - 16
    quarter = width // 3
    greet(PEERS, size)
    other = Line(size, 4, joined, join_came, join_sent, send_join, recv_join)
    other.begin()
    own = Line(size, 7, line, line_came, line_sent, send_line, recv_line)

    d = grads[...]

    def block_copy(mask):
        return remote(
            blocks.at[me ^ mask], came_blocks.at[mask], send_block.at[mask], recv_block.at[mask], me ^ mask
        )

    for mask in (6, 2, 4, 0):
        first = ((me ^ mask) // 2) * 2
        columns = pl.ds(pl.multiple_of(first * cut, 2 * cut), 2 * cut)
        both = tn(rows[:, columns], d).astype(low)
        for place in range(2):
            blocks[first + place, :cut] = both[place * cut : (place + 1) * cut]
            blocks[first + place, cut:] = vectors[first + place]
        if mask:
            block_copy(mask).start()
        block_copy(mask + 1).start()
    chips = (6, 2, 4, 0)

    def term(owner):
        return nt(grads[pl.ds(pl.multiple_of(owner * count, count), count)], weights[...])

    def sib_copy(slot):
        return remote(terms.at[slot], sib.at[slot], send.at[slot], recv.at[slot], me ^ 1)

    def pair_copy(slot):
        return remote(pair.at[slot], came.at[slot], send_pair.at[slot], recv_pair.at[slot], me ^ chips[slot])

    for slot, mask in enumerate(chips):
        terms[slot] = term(me ^ 1 ^ mask).astype(low)
        sib_copy(slot).start()
    for slot, mask in enumerate(chips):
        here = term(me ^ mask)
        sib_copy(slot).wait_recv()
        here = here + sib[slot].astype(wide)
        if mask:
            pair[slot] = here.astype(low)
            pair_copy(slot).start()
        else:
            out[mine] = here

    other.rest(0)

    half = out_straight.shape[0]
    out_turned[...] = feed[:half].astype(wide).T
    out_straight[...] = feed[half:].astype(wide)
    out_middle[...] = middle[...].astype(wide)

    for mask in PEERS:
        block_copy(mask).wait_recv()
    came_blocks[0] = blocks[me]

    def came_from(owner, part):
        return came_blocks[owner ^ me, part].astype(wide)

    total = jnp.zeros((16, width), wide)
    for source in range(4):
        both = came_from(source, pl.ds(0, cut)) + came_from(source + 4, pl.ds(0, cut))
        for kind in range(3):
            line[kind * cut : (kind + 1) * cut, source * quarter : (source + 1) * quarter] = both[
                :, kind * quarter : (kind + 1) * quarter
            ].astype(low)
        total = total + came_from(source, pl.ds(cut, 16)) + came_from(source + 4, pl.ds(cut, 16))
    line[3 * cut :] = jnp.zeros_like(line[3 * cut :])
    line[3 * cut : 3 * cut + 16, :width] = total.astype(low)

    own.begin()
    own.rest(0)
    for slot in (1, 2, 0):
        pair_copy(slot).wait_recv()
    out[mine] += came[1].astype(wide)
    out[1 - mine] = came[2].astype(wide) + came[0].astype(wide)

    out_line[...] = own.total()
    out_joined[...] = other.total()
    for mask in PEERS:
        block_copy(mask).wait_send()
    for slot in range(4):
        sib_copy(slot).wait_send()
    for slot in range(3):
        pair_copy(slot).wait_send()
    own.end()
    other.end()


def finish(rows, grads, weights, vectors, joined, feed, middle):
    width = rows.shape[1]
    count = rows.shape[0] // 8
    cut = width // 8
    line = (3 * cut + 64, width)
    blocks = (8, cut + 16, grads.shape[1])
    four, three = pltpu.SemaphoreType.DMA((4,)), pltpu.SemaphoreType.DMA((3,))
    return pl.pallas_call(
        functools.partial(finish_kernel, lax.axis_size("dp")),
        out_shape=(
            jax.ShapeDtypeStruct((2, count, width), wide),
            jax.ShapeDtypeStruct(line, wide),
            jax.ShapeDtypeStruct(joined.shape, wide),
            jax.ShapeDtypeStruct((width, feed.shape[0] // 2), wide),
            jax.ShapeDtypeStruct((feed.shape[0] // 2, width), wide),
            jax.ShapeDtypeStruct(middle.shape, wide),
        ),
        in_specs=[vmem_spec()] * 7,
        out_specs=(vmem_spec(),) * 6,
        scratch_shapes=[
            pltpu.VMEM((4, count, width), low),
            pltpu.VMEM((4, count, width), low),
            pltpu.VMEM((3, count, width), low),
            pltpu.VMEM((3, count, width), low),
            pltpu.VMEM(blocks, low),
            pltpu.VMEM(blocks, low),
            pltpu.VMEM(line, low),
            four,
            four,
            three,
            three,
        ]
        + [pltpu.SemaphoreType.DMA((8,))] * 2
        + line_scratch(line, 7)
        + line_scratch(joined.shape, 4),
        compiler_params=params(6),
    )(rows, grads, weights, vectors, joined, feed, middle)


def plain(**more):
    return pltpu.CompilerParams(vmem_limit_bytes=VMEM_BYTES, **more)


def flash_forward_kernel(length, queries, keys, values, context, logsum, scores, probs):
    rows, width = queries.shape
    count = keys.shape[0]
    heads = width // 64
    strip = 16
    of_head = lane_head((1, width), 64)
    q = queries[...] * jnp.asarray(0.125, low)
    k = keys[...]
    v = values[...]
    total = jnp.zeros((rows, width), wide)
    logs = jnp.zeros((rows, 128), wide)
    lanes = lax.broadcasted_iota(jnp.int32, (1, 128), 1)
    fill = jnp.where(lax.broadcasted_iota(jnp.int32, (1, count), 1) < length[0], 0.0, masked_fill)
    for head in range(heads):
        slot = head % 2
        scores[slot] = nt(jnp.where(of_head == head, q, jnp.zeros_like(q)), k)
        tops, sums = [], []
        for start in range(0, rows, strip):
            part = scores[slot, start : start + strip] + fill
            top = jnp.max(part, -1, keepdims=True)
            weights = jnp.exp(part - top)
            tops.append(top)
            sums.append(jnp.sum(weights, -1, keepdims=True))
            probs[slot, start : start + strip] = weights.astype(low)
        top, summed = jnp.concatenate(tops, 0), jnp.concatenate(sums, 0)
        total = jnp.where(of_head == head, nn(probs[slot], v) * (1.0 / summed), total)
        logs = jnp.where(lanes == head, top + jnp.log(summed), logs)
    context[...] = total.astype(low)
    logsum[...] = logs


def flash_forward(length, three, block):
    count, width = three.shape[0], three.shape[1] // 3
    return pl.pallas_call(
        flash_forward_kernel,
        out_shape=(
            jax.ShapeDtypeStruct((count, width), low),
            jax.ShapeDtypeStruct((count, 128), wide),
        ),
        grid_spec=pltpu.PrefetchScalarGridSpec(
            num_scalar_prefetch=1,
            grid=(count // block,),
            in_specs=[
                pl.BlockSpec((block, width), lambda i, n: (i, 0)),
                pl.BlockSpec((count, width), lambda i, n: (0, 1)),
                pl.BlockSpec((count, width), lambda i, n: (0, 2)),
            ],
            out_specs=[
                pl.BlockSpec((block, width), lambda i, n: (i, 0)),
                pl.BlockSpec((block, 128), lambda i, n: (i, 0)),
            ],
            scratch_shapes=[pltpu.VMEM((2, block, count), wide), pltpu.VMEM((2, block, count), low)],
        ),
        compiler_params=plain(),
    )(length, three, three, three)


def flash_backward_kernel(chunk, length, queries, grads, logsum, delta, keys, keys_t, values, out, q_stack, g_stack, p_stack, s_stack, k_sum, v_sum):
    step = pl.program_id(0)
    rows, width = queries.shape
    count = keys.shape[0]
    heads = width // 64
    of_head = lane_head((1, width), 64)

    @pl.when(step == 0)
    def _():
        k_sum[...] = jnp.zeros_like(k_sum)
        v_sum[...] = jnp.zeros_like(v_sum)

    q = queries[...] * jnp.asarray(0.125, low)
    g = grads[...]
    for head in range(heads):
        place = pl.ds(head * rows, rows)
        q_stack[place] = jnp.where(of_head == head, q, jnp.zeros_like(q))
        g_stack[place] = jnp.where(of_head == head, g, jnp.zeros_like(g))
    dq_sums = [jnp.zeros((64, rows), wide)] * heads
    for start in range(0, count, chunk):
        part = pl.ds(start, chunk)
        k = keys[part]
        v = values[part]
        allowed = start + lax.broadcasted_iota(jnp.int32, (chunk, 1), 0) < length[0]
        fill = jnp.where(allowed, 0.0, masked_fill)
        for head in range(heads):
            place = pl.ds(head * rows, rows)
            scores = nt(k, q_stack[place])
            probs = jnp.exp(scores - logsum[head : head + 1, :] + fill)
            p_stack[:, place] = probs.astype(low)
            d_probs = nt(v, g_stack[place])
            d_scores = (probs * (d_probs - delta[head : head + 1, :])).astype(low)
            s_stack[:, place] = d_scores
            dq_sums[head] = dq_sums[head] + nn(keys_t[head * 64 : head * 64 + 64, part], d_scores)
        v_sum[part] += nn(p_stack[...], g_stack[...])
        k_sum[part] += nn(s_stack[...], q_stack[...])
    dq = jnp.concatenate(dq_sums, 0) * 0.125
    out[pl.ds(pl.multiple_of(step * rows, rows), rows), 0:width] = dq.T.astype(low)

    @pl.when(step == pl.num_programs(0) - 1)
    def _():
        out[:, width : 2 * width] = k_sum[...].astype(low)
        out[:, 2 * width : 3 * width] = v_sum[...].astype(low)


def flash_backward(length, three, grads, logsum, delta, block, chunk):
    count, width = grads.shape
    heads = width // 64
    return pl.pallas_call(
        functools.partial(flash_backward_kernel, chunk),
        out_shape=jax.ShapeDtypeStruct((count, 3 * width), low),
        grid_spec=pltpu.PrefetchScalarGridSpec(
            num_scalar_prefetch=1,
            grid=(count // block,),
            in_specs=[
                pl.BlockSpec((block, width), lambda i, n: (i, 0)),
                pl.BlockSpec((block, width), lambda i, n: (i, 0)),
                pl.BlockSpec((heads, block), lambda i, n: (0, i)),
                pl.BlockSpec((heads, block), lambda i, n: (0, i)),
                pl.BlockSpec((count, width), lambda i, n: (0, 1)),
                pl.BlockSpec((width, count), lambda i, n: (0, 0)),
                pl.BlockSpec((count, width), lambda i, n: (0, 2)),
            ],
            out_specs=pl.BlockSpec((count, 3 * width), lambda i, n: (0, 0)),
            scratch_shapes=[
                pltpu.VMEM((heads * block, width), low),
                pltpu.VMEM((heads * block, width), low),
                pltpu.VMEM((chunk, heads * block), low),
                pltpu.VMEM((chunk, heads * block), low),
                pltpu.VMEM((count, width), wide),
                pltpu.VMEM((count, width), wide),
            ],
        ),
        compiler_params=plain(),
    )(length, three, grads, logsum, delta, three, three[:, width : 2 * width].T, three)


def small_forward_kernel(causal, length, queries, keys, values, context, tops, sums):
    table = pl.program_id(0)
    rows, width = queries.shape
    count = keys.shape[0]
    half = lane_head((1, 128), 64)
    lanes = lax.broadcasted_iota(jnp.int32, (1, 128), 1)
    allowed = lax.broadcasted_iota(jnp.int32, (rows, count), 1) < length[table]
    if causal:
        allowed = allowed & (
            lax.broadcasted_iota(jnp.int32, (rows, count), 1)
            <= lax.broadcasted_iota(jnp.int32, (rows, count), 0)
        )
    top_all = jnp.zeros((rows, 128), wide)
    sum_all = jnp.ones((rows, 128), wide)
    for two in range(width // 128):
        place = pl.ds(two * 128, 128)
        q = queries[:, place] * jnp.asarray(0.125, low)
        k = keys[:, place]
        v = values[:, place]
        total = jnp.zeros((rows, 128), wide)
        for side in range(2):
            scores = nt(jnp.where(half == side, q, jnp.zeros_like(q)), k)
            scores = jnp.where(allowed, scores, masked_fill)
            top = jnp.max(scores, -1, keepdims=True)
            weights = jnp.exp(scores - top)
            summed = jnp.sum(weights, -1, keepdims=True)
            probs = (weights * (1.0 / summed)).astype(low)
            total = jnp.where(half == side, nn(probs, v), total)
            top_all = jnp.where(lanes == 2 * two + side, top, top_all)
            sum_all = jnp.where(lanes == 2 * two + side, summed, sum_all)
        context[:, place] = total.astype(low)
    tops[...] = top_all
    sums[...] = sum_all


def small_forward(length, queries, keys, values, causal):
    tables = length.shape[0]
    rows, width = queries.shape[0] // tables, queries.shape[1]
    count = keys.shape[0] // tables

    def block(size, last):
        return pl.BlockSpec((size, last), lambda t, n: (t, 0))

    return pl.pallas_call(
        functools.partial(small_forward_kernel, causal),
        out_shape=(
            jax.ShapeDtypeStruct(queries.shape, low),
            jax.ShapeDtypeStruct((queries.shape[0], 128), wide),
            jax.ShapeDtypeStruct((queries.shape[0], 128), wide),
        ),
        grid_spec=pltpu.PrefetchScalarGridSpec(
            num_scalar_prefetch=1,
            grid=(tables,),
            in_specs=[block(rows, width), block(count, width), block(count, width)],
            out_specs=[block(rows, width), block(rows, 128), block(rows, 128)],
        ),
        compiler_params=plain(),
    )(length, queries, keys, values)


def small_backward_kernel(causal, length, queries, keys, values, grads, context, logsum, earlier, dq, dk, dv):
    table = pl.program_id(0)
    rows, width = queries.shape
    count = keys.shape[0]
    half = lane_head((1, 128), 64)
    allowed = lax.broadcasted_iota(jnp.int32, (rows, count), 1) < length[table]
    if causal:
        allowed = allowed & (
            lax.broadcasted_iota(jnp.int32, (rows, count), 1)
            <= lax.broadcasted_iota(jnp.int32, (rows, count), 0)
        )
    logs = logsum[...]
    for two in range(width // 128):
        place = pl.ds(two * 128, 128)
        q = queries[:, place] * jnp.asarray(0.125, low)
        k = keys[:, place]
        v = values[:, place]
        g = grads[:, place]
        both = g.astype(wide) * context[:, place].astype(wide)
        dq_here = jnp.zeros((rows, 128), wide)
        dk_here = jnp.zeros((count, 128), wide)
        dv_here = jnp.zeros((count, 128), wide)
        for side in range(2):
            head = 2 * two + side
            q_one = jnp.where(half == side, q, jnp.zeros_like(q))
            g_one = jnp.where(half == side, g, jnp.zeros_like(g))
            delta = jnp.sum(jnp.where(half == side, both, 0.0), -1, keepdims=True)
            scores = nt(q_one, k)
            probs = jnp.where(allowed, jnp.exp(scores - logs[:, head : head + 1]), 0.0)
            d_probs = nt(g_one, v)
            d_scores = (probs * (d_probs - delta)).astype(low)
            dq_here = jnp.where(half == side, nn(d_scores, k), dq_here)
            dk_here = dk_here + tn(d_scores, q_one)
            dv_here = dv_here + tn(probs.astype(low), g_one)
        dq[:, place] = dq_here * 0.125
        dk[:, place] = dk_here.astype(low)
        dv[:, place] = dv_here.astype(low)


def small_backward(length, queries, keys, values, grads, context, logsum, causal, earlier):
    tables = length.shape[0]
    rows, width = queries.shape[0] // tables, queries.shape[1]
    count = keys.shape[0] // tables

    def block(size, last):
        return pl.BlockSpec((size, last), lambda t, n: (t, 0))

    return pl.pallas_call(
        functools.partial(small_backward_kernel, causal),
        out_shape=(
            jax.ShapeDtypeStruct(queries.shape, wide),
            jax.ShapeDtypeStruct(keys.shape, low),
            jax.ShapeDtypeStruct(keys.shape, low),
        ),
        grid_spec=pltpu.PrefetchScalarGridSpec(
            num_scalar_prefetch=1,
            grid=(tables,),
            in_specs=[
                block(rows, width),
                block(count, width),
                block(count, width),
                block(rows, width),
                block(rows, width),
                block(rows, 128),
                any_spec(),
            ],
            out_specs=[block(rows, width), block(count, width), block(count, width)],
        ),
        compiler_params=plain(),
    )(length, queries, keys, values, grads, context, logsum, earlier)


def gelu_parts(values):
    bell = 0.5 * (1.0 + lax.erf(values * 0.7071067811865476))
    slope = bell + values * (0.3989422804014327 * jnp.exp(-0.5 * values * values))
    return values * bell, slope


def feed_forward_kernel(rows, expand, contract, out):
    hidden = nn(rows[...], expand[0])
    act = (hidden * (0.5 * (1.0 + lax.erf(hidden * 0.7071067811865476)))).astype(low)
    term = nn(act, contract[0])

    @pl.when(pl.program_id(0) == 0)
    def _():
        out[...] = term

    @pl.when(pl.program_id(0) > 0)
    def _():
        out[...] += term


def feed_forward(rows, expand, contract):
    count, width = rows.shape
    parts, _, hidden = expand.shape
    return pl.pallas_call(
        feed_forward_kernel,
        out_shape=jax.ShapeDtypeStruct((count, width), wide),
        grid=(parts,),
        in_specs=[
            pl.BlockSpec((count, width), lambda j: (0, 0)),
            pl.BlockSpec((1, width, hidden), lambda j: (j, 0, 0)),
            pl.BlockSpec((1, hidden, width), lambda j: (j, 0, 0)),
        ],
        out_specs=pl.BlockSpec((count, width), lambda j: (0, 0)),
        compiler_params=plain(),
    )(rows, expand, contract)


def outer_kernel(order, earlier, rows, *refs):
    *grads, away, kept = refs
    step = pl.program_id(0)
    half = pl.num_programs(0) // 2
    size = rows.shape[1]
    for place, grad in enumerate(grads):
        term = tn(rows[...], grad[...]).astype(low)

        @pl.when(step < half)
        def _(place=place, term=term):
            away[0, place * size : (place + 1) * size] = term

        @pl.when(step >= half)
        def _(place=place, term=term):
            kept[0, place * size : (place + 1) * size] = term


def outer_by_owner(order, earlier, rows, *grads):
    count, width = rows.shape
    parts = order.shape[0]
    half, size = parts // 2, width // parts
    shape = jax.ShapeDtypeStruct((half, len(grads) * size, width), low)
    return pl.pallas_call(
        outer_kernel,
        out_shape=(shape, shape),
        grid_spec=pltpu.PrefetchScalarGridSpec(
            num_scalar_prefetch=1,
            grid=(parts,),
            in_specs=[any_spec(), pl.BlockSpec((count, size), lambda j, o: (0, o[j]))]
            + [pl.BlockSpec((count, width), lambda j, o: (0, 0))] * len(grads),
            out_specs=[
                pl.BlockSpec((1,) + shape.shape[1:], lambda j, o: (jnp.minimum(j, half - 1), 0, 0)),
                pl.BlockSpec((1,) + shape.shape[1:], lambda j, o: (jnp.maximum(j - half, 0), 0, 0)),
            ],
        ),
        compiler_params=plain(),
    )(order, earlier, rows, *grads)


def feed_backward_kernel(rows, grads, expand, contract, earlier, out, d_both, expand_sum, contract_sum):
    step = pl.program_id(0)
    x = rows[0]
    g = grads[0]
    act, slope = gelu_parts(nn(x, expand[...]))
    d_hidden = (nt(g, contract[...]) * slope).astype(low)
    out[0] = nt(d_hidden, expand[...]).astype(low)
    one = tn(d_hidden, x)
    two = tn(act.astype(low), g)

    @pl.when(step == 0)
    def _():
        expand_sum[...] = one
        contract_sum[...] = two

    @pl.when(step > 0)
    def _():
        expand_sum[...] += one
        contract_sum[...] += two

    @pl.when(step == pl.num_programs(0) - 1)
    def _():
        d_both[: expand_sum.shape[0]] = expand_sum[...].astype(low)
        d_both[expand_sum.shape[0] :] = contract_sum[...].astype(low)


def feed_backward(rows, grads, expand, contract, earlier):
    parts, count, width = rows.shape
    hidden = contract.shape[0]
    return pl.pallas_call(
        feed_backward_kernel,
        out_shape=(jax.ShapeDtypeStruct(rows.shape, low), jax.ShapeDtypeStruct((2 * hidden, width), low)),
        grid=(parts,),
        in_specs=[
            pl.BlockSpec((1, count, width), lambda j: (j, 0, 0)),
            pl.BlockSpec((1, count, width), lambda j: (j, 0, 0)),
            pl.BlockSpec((width, hidden), lambda j: (0, 0)),
            pl.BlockSpec((hidden, width), lambda j: (0, 0)),
            any_spec(),
        ],
        out_specs=[
            pl.BlockSpec((1, count, width), lambda j: (j, 0, 0)),
            pl.BlockSpec((2 * hidden, width), lambda j: (0, 0)),
        ],
        scratch_shapes=[pltpu.VMEM((hidden, width), wide)] * 2,
        compiler_params=plain(),
    )(rows, grads, expand, contract, earlier)


def swap(array, mask):
    return lax.ppermute(array, "seq", [(i, i ^ mask) for i in range(8)])


def add_kernel(left, right, earlier, out):
    out[...] = add_low(left[...], right[...])


def add_after(left, right, earlier):
    return pl.pallas_call(
        add_kernel,
        out_shape=jax.ShapeDtypeStruct(left.shape, low),
        in_specs=[vmem_spec()] * 2 + [any_spec()],
        out_specs=vmem_spec(),
        compiler_params=plain(),
    )(left, right, earlier)


def scatter_cores(away, kept, earlier):
    return add_after(kept, swap(away, 1), earlier)


def scatter_first(both):
    half = both.shape[1] // 2
    one, two = both[:, :half], both[:, half:]
    one_came = swap(jnp.stack([one[0], one[2]]), 2)
    two_came = swap(jnp.stack([two[1], two[2]]), 4)
    return (
        add_low(one[3], one_came[0]),
        add_low(one[1], one_came[1]),
        add_low(two[3], two_came[0]),
        add_low(two[0], two_came[1]),
    )


def scatter_second(parts):
    one, one_far, two, two_far = parts
    return add_low(one, swap(one_far, 4)), add_low(two, swap(two_far, 2))


def plane_body(
    source_tokens,
    target_tokens,
    source_lengths,
    target_lengths,
    encoder_query,
    encoder_key,
    encoder_value,
    encoder_mix,
    attend_gain,
    attend_shift,
    encoder_expand,
    encoder_contract,
    encoder_gain,
    encoder_shift,
    decoder_query,
    decoder_key,
    decoder_value,
    decoder_mix,
    self_gain,
    self_shift,
    cross_query,
    cross_key,
    cross_value,
    cross_mix,
    cross_gain,
    cross_shift,
    decoder_expand,
    decoder_contract,
    decoder_gain,
    decoder_shift,
    source_cotangent,
    target_cotangent,
):
    slots, tables, width = source_tokens.shape
    places = target_tokens.shape[0]
    me = lax.axis_index("seq")
    quarter = width // 4
    slice_rows = width // 8

    def flat(array):
        return jnp.swapaxes(array, 0, 1).reshape(-1, width)

    def unflat(array):
        return jnp.swapaxes(array.reshape(tables, -1, width), 0, 1)

    def columns(weight):
        return lax.dynamic_slice_in_dim(weight, (me % 4) * quarter, quarter, 1)

    def own(rows):
        return lax.dynamic_slice_in_dim(rows, me * slice_rows, slice_rows, 1)

    def own_places(rows):
        return lax.dynamic_slice_in_dim(rows.reshape(tables, 8 * places, width), me * places, places, 1)

    def own_vector(vector):
        return lax.dynamic_slice_in_dim(vector, me * slice_rows, slice_rows, 0)

    source_flat = flat(source_tokens)
    all_expand = lax.all_gather(encoder_expand, "seq", axis=0)
    all_contract = lax.all_gather(encoder_contract, "seq", axis=0)
    target_pair = jnp.stack([jnp.swapaxes(target_tokens, 0, 1), jnp.swapaxes(target_cotangent, 0, 1)], 0)
    rows, target_all = gather_table(source_flat.reshape(tables, slots, width), target_pair.reshape(-1, width))
    rows = rows.reshape(-1, width)
    target_all = jnp.moveaxis(target_all.reshape(8, 2, tables, places, width), 0, 2).reshape(2, -1, width)
    target_flat, target_grad = target_all[0], target_all[1]
    w_three = jnp.concatenate([columns(encoder_query), columns(encoder_key), columns(encoder_value)], 1)
    length = lax.dynamic_slice_in_dim(source_lengths, me // 4, 1, 0)
    three = project(rows, w_three).astype(low)
    context, logsum = flash_forward(length, three, 512)
    encoder_context = heads_to_rows(context.reshape(8, slots, quarter)).reshape(-1, width)
    first, first_back = jax.vjp(
        layer_norm, source_flat.astype(wide) + project(encoder_context, encoder_mix), attend_gain, attend_shift
    )
    first_low = first.astype(low)
    widened = feed_forward(first_low, all_expand, all_contract)
    first_all = lax.all_gather(first_low, "seq", axis=0)
    second, second_back = jax.vjp(layer_norm, first + widened, encoder_gain, encoder_shift)
    encoded = second.astype(low)

    self_queries = project(target_flat, decoder_query).astype(low)
    self_keys = project(target_flat, decoder_key).astype(low)
    self_values = project(target_flat, decoder_value).astype(low)
    decoder_context, self_tops, self_sums = small_forward(
        target_lengths, self_queries, self_keys, self_values, True
    )
    self_logs = self_tops + jnp.log(self_sums)
    third, third_back = jax.vjp(
        layer_norm, target_flat.astype(wide) + project(decoder_context, decoder_mix), self_gain, self_shift
    )
    third_low = third.astype(low)
    cross_queries = project(third_low, cross_query).astype(low)

    cross_keys = project(encoded, cross_key).astype(low)
    cross_values = project(encoded, cross_value).astype(low)
    here = source_lengths - me * slots
    part, part_tops, part_sums = small_forward(here, cross_queries, cross_keys, cross_values, False)
    cross_context, cross_logs = merge_parts(part, part_tops, part_sums)
    fourth, fourth_back = jax.vjp(
        layer_norm, third + project(cross_context, cross_mix), cross_gain, cross_shift
    )
    fourth_low = fourth.astype(low)
    hidden = project(fourth_low, decoder_expand)
    decoder_acts, gelu_back = jax.vjp(gelu_exact, hidden)
    decoder_acts = decoder_acts.astype(low)
    narrowed = sum_small(project(decoder_acts, decoder_contract), 4, first_all).astype(wide)
    fifth, fifth_back = jax.vjp(layer_norm, fourth + narrowed, decoder_gain, decoder_shift)
    decoded = jnp.swapaxes(own_places(fifth.astype(low)), 0, 1)

    d_fifth, grad_decoder_gain, grad_decoder_shift = fifth_back(target_grad.astype(wide))
    fifth_low = d_fifth.astype(low)
    d_hidden = gelu_back(project_back(fifth_low, decoder_contract))[0].astype(low)
    eighth = fourth_low.shape[0] // 8
    decoder_pair = jnp.stack(
        [lax.dynamic_slice_in_dim(array, me * eighth, eighth, 0) for array in (fourth_low, fifth_low)], 0
    )
    decoder_pair = lax.all_gather(decoder_pair, ("dp", "seq"), axis=0)
    def over_tables(terms):
        part = lax.psum_scatter(terms, "dp", scatter_dimension=0, tiled=True)
        return lax.all_gather(part, "dp", axis=0, tiled=True)

    def join(arrays):
        return jnp.concatenate([a.astype(low) for a in arrays], 0)

    d_rows = sum_small(project_back(d_hidden, decoder_expand), 10).astype(wide)
    d_fourth, grad_cross_gain, grad_cross_shift = fourth_back(d_fifth + d_rows)
    cross_low = d_fourth.astype(low)
    grad_cross_mix = outer_sum(own(cross_context), cross_low)
    d_cross = project_back(cross_low, cross_mix).astype(low)
    dq_part, dk_cross, dv_cross = small_backward(
        here, cross_queries, cross_keys, cross_values, d_cross, cross_context, cross_logs, False, cross_logs
    )
    d_encoded = project_back(dk_cross, cross_key) + project_back(dv_cross, cross_value)
    order = me ^ jnp.array(OWNERS, jnp.int32)


    d_second, grad_encoder_gain, grad_encoder_shift = second_back(flat(source_cotangent).astype(wide) + d_encoded)
    d_second_low = d_second.astype(low)
    d_all = lax.all_gather(d_second_low, "seq", axis=0)
    dq_cross, cross_away, cross_kept = sum_small_outer(dq_part, d_second_low, encoded, dk_cross, dv_cross)
    grad_cross_query = outer_sum(own(third_low), dq_cross)
    d_third, grad_self_gain, grad_self_shift = third_back(d_fourth + project_back(dq_cross, cross_query))
    self_low = d_third.astype(low)
    grad_decoder_mix = outer_sum(own(decoder_context), self_low)
    dq_self, dk_self, dv_self = small_backward(
        target_lengths,
        self_queries,
        self_keys,
        self_values,
        project_back(self_low, decoder_mix).astype(low),
        decoder_context,
        self_logs,
        True,
        decoder_pair,
    )
    dq_self = dq_self.astype(low)
    target_own = own(target_flat)
    grad_decoder_query = outer_sum(target_own, dq_self)
    grad_decoder_key = outer_sum(target_own, dk_self)
    grad_decoder_value = outer_sum(target_own, dv_self)
    grad_target = own_places(
        d_third
        + project_back(dq_self, decoder_query)
        + project_back(dk_self, decoder_key)
        + project_back(dv_self, decoder_value)
    )
    grad_target = jnp.swapaxes(grad_target, 0, 1)

    decoder_vectors = jnp.stack(
        [
            own_vector(v)
            for v in (
                grad_self_gain,
                grad_self_shift,
                grad_cross_gain,
                grad_cross_shift,
                grad_decoder_gain,
                grad_decoder_shift,
            )
        ],
        0,
    )
    decoder_vectors = jnp.pad(decoder_vectors.reshape(1, -1), ((0, 15), (0, width - 6 * slice_rows)))
    middle = [
        grad_decoder_query,
        grad_decoder_key,
        grad_decoder_value,
        grad_decoder_mix,
        grad_cross_query,
        grad_cross_mix,
        decoder_vectors,
    ]
    middle_join = join(middle + [jnp.zeros((48, width), low)])
    middle_sum = over_tables(middle_join)
    d_terms, feed_join = feed_backward(first_all, d_all, encoder_expand, encoder_contract, dq_self)
    feed_sum = over_tables(feed_join)
    cross_both = scatter_cores(cross_away, cross_kept, feed_join)
    d_rows, grad_decoder_expand, grad_decoder_contract = scatter_plane(
        d_terms, decoder_pair, decoder_expand, decoder_contract
    )
    d_first, grad_attend_gain, grad_attend_shift = first_back(d_second + d_rows)
    encoder_low = d_first.astype(low)
    d_context, mix_away, mix_kept = rows_to_heads(
        project_back(encoder_low, encoder_mix).astype(low).reshape(tables, slots, width), encoder_context, encoder_low
    )
    mix_both = scatter_cores(mix_away, mix_kept, d_context)
    d_context = d_context.reshape(-1, quarter)
    delta = jnp.sum(
        (d_context.astype(wide) * context.astype(wide)).reshape(-1, quarter // 64, 64), -1
    )
    d_three = flash_backward(length, three, d_context, logsum[:, : quarter // 64].T, delta.T, 512, 1024)
    vectors = jnp.stack(
        [grad_attend_gain, grad_attend_shift, grad_encoder_gain, grad_encoder_shift], 0
    ).astype(low)
    vectors = jnp.swapaxes(vectors.reshape(4, 8, slice_rows), 0, 1)
    vectors = jnp.pad(vectors, ((0, 0), (0, 12), (0, 3 * quarter - slice_rows)))
    parts = scatter_second(scatter_first(mix_both)) + scatter_second(scatter_first(cross_both))
    d_source, line, plane_sum, grad_encoder_expand, grad_encoder_contract, middle_wide = finish(
        rows, d_three, w_three, vectors, join(parts), feed_sum, middle_sum
    )
    grad_source = unflat(d_first + d_source.reshape(-1, width))
    encoder_three = line[: 3 * slice_rows].reshape(3, slice_rows, width)
    encoder_vectors = line[3 * slice_rows : 3 * slice_rows + 4, :slice_rows]
    plane_three = plane_sum.reshape(3, slice_rows, width)
    six = middle_wide[: 6 * slice_rows].reshape(6, slice_rows, width)
    decoder_vectors = middle_wide[6 * slice_rows : 6 * slice_rows + 1]
    decoder_vectors = decoder_vectors[0, : 6 * slice_rows].reshape(6, slice_rows)
    return (
        unflat(encoded),
        decoded,
        grad_source,
        grad_target,
        encoder_three[0],
        encoder_three[1],
        encoder_three[2],
        plane_three[0],
        encoder_vectors[0],
        encoder_vectors[1],
        grad_encoder_expand,
        grad_encoder_contract,
        encoder_vectors[2],
        encoder_vectors[3],
        six[0],
        six[1],
        six[2],
        six[3],
        decoder_vectors[0],
        decoder_vectors[1],
        six[4],
        plane_three[1],
        plane_three[2],
        six[5],
        decoder_vectors[2],
        decoder_vectors[3],
        grad_decoder_expand,
        grad_decoder_contract,
        decoder_vectors[4],
        decoder_vectors[5],
    )


def solution(mesh):
    body = plane_body if fits_plane(mesh) else general_body
    in_specs = (
        P("seq", "dp", None),
        P("seq", "dp", None),
        P("dp"),
        P("dp"),
        P(),
        P(),
        P(),
        P(),
        P(),
        P(),
        P(None, "seq"),
        P("seq", None),
        P(),
        P(),
        P(),
        P(),
        P(),
        P(),
        P(),
        P(),
        P(),
        P(),
        P(),
        P(),
        P(),
        P(),
        P(None, "seq"),
        P("seq", None),
        P(),
        P(),
        P("seq", "dp", None),
        P("seq", "dp", None),
    )
    out_specs = (
        P("seq", "dp", None),
        P("seq", "dp", None),
        P("seq", "dp", None),
        P("seq", "dp", None),
        P("seq", None),
        P("seq", None),
        P("seq", None),
        P("seq", None),
        P("seq"),
        P("seq"),
        P(None, "seq"),
        P("seq", None),
        P("seq"),
        P("seq"),
        P("seq", None),
        P("seq", None),
        P("seq", None),
        P("seq", None),
        P("seq"),
        P("seq"),
        P("seq", None),
        P("seq", None),
        P("seq", None),
        P("seq", None),
        P("seq"),
        P("seq"),
        P(None, "seq"),
        P("seq", None),
        P("seq"),
        P("seq"),
    )
    return jax.shard_map(body, mesh=mesh, in_specs=in_specs, out_specs=out_specs, check_vma=False)
```
